128 devices in a mesh: row: 8 (over z, core), col: 16 (over y, x).
Axes of the slice: x: 4, y: 4, z: 4, core: 2. Of those that a mesh axis runs over, the one named last changes fastest.
Arguments:
- features: bfloat16 [131072, 256], P(('row', 'col')), may hold values from -6 to 6
- zorder_to: int32 [131072], P(('row', 'col')), may hold values from 0 to 131071, as said below
- hilbert_from: int32 [131072], P(('row', 'col')), may hold values from 0 to 131071, as said below
- qkv_weight: bfloat16 [256, 768], replicated, may hold values from -3 to 3, as said below
- proj_weight: bfloat16 [256, 256], replicated, may hold values from -0.375 to 0.375
- out_grad: bfloat16 [131072, 256], P(('row', 'col')), may hold values from -6 to 6
Outputs:
- block_out: bfloat16 [131072, 256], P(('row', 'col'))
- feature_grad: bfloat16 [131072, 256], P(('row', 'col'))
- qkv_grad: float32 [256, 768], replicated
- proj_grad: float32 [256, 256], replicated
The draws below stay inside these ranges and needn't reach their ends.
Inputs may be any that keep to these rules, and one draw needn't show every extreme that they name: zorder_to is a permutation and hilbert_from is its inverse. The points at the z-order positions of one block of 1024 go to every block of 1024 Hilbert positions, exactly 8 points to each. `hilbert_from`: the inverse of zorder_to. `qkv_weight`: value columns have entries of order 256 ** -0.5 times a few; query and key columns may be up to 4 times larger.
All inputs are finite; a program needn't handle non-finite values.
Results may differ from the reference program's by a relative error of at most 0.007.
The reference program's roundings to bfloat16 on the way count: a program that leaves them out, or rounds other values in their place, can miss the bound.
Values may be sent and summed in bfloat16 or wider, within the bound.
A program may use at most 128 MiB of HBM per device.

```python
import jax
import jax.numpy as jnp
from jax import lax

C = 256
HEADS = 16
PATCH = 1024
ROWS_DEV = 1024
POINTS = 131072
CAP = 8
N_ROW = 8
N_COL = 16


def serial_maps(key):
    devices = N_ROW * N_COL
    groups = ROWS_DEV // CAP
    first, second, third = jax.random.split(key, 3)
    offsets = jax.random.permutation(first, devices)[:groups]
    send_perm = jax.vmap(lambda sub: jax.random.permutation(sub, ROWS_DEV))(jax.random.split(second, devices))
    recv_perm = jax.vmap(lambda sub: jax.random.permutation(sub, ROWS_DEV))(jax.random.split(third, devices))
    source = jnp.arange(devices, dtype=jnp.int32)[:, None]
    target_dev = (source + offsets[send_perm // CAP]) % devices
    target = target_dev * ROWS_DEV + recv_perm[target_dev, send_perm]
    forward = target.reshape(-1).astype(jnp.int32)
    inverse = jnp.zeros((POINTS,), jnp.int32).at[forward].set(jnp.arange(POINTS, dtype=jnp.int32))
    return (forward, inverse)


def draw_zorder_to(key, part):
    maps = serial_maps(key)
    return maps[0]


def draw_hilbert_from(key, part):
    maps = serial_maps(key)
    return maps[1]


def draw_qkv_weight(key, part):
    key = jax.random.fold_in(key, 7)
    values = jax.random.normal(key, (C, 3 * C), jnp.float32) * C ** (-0.5)
    values = jnp.clip(values, -6.0 * C ** (-0.5), 6.0 * C ** (-0.5))
    return values.astype(jnp.bfloat16)


def block_levels(rng, extent, cuts, least, high):
    loudness, own = 1.0, jax.random.fold_in(rng, 6)
    for position, parts in cuts:
        heights = jnp.exp(jax.random.uniform(jax.random.fold_in(own, position), (parts,), jnp.float32, least / len(cuts), high / len(cuts)))
        loudness = loudness * jnp.repeat(heights, extent[position] // parts).reshape([-1 if axis == position else 1 for axis in range(len(extent))])
    return loudness


def noise(rng, extent, deviation, reach, cuts=(), kind=jnp.bfloat16):
    entries = deviation * jax.random.normal(rng, extent, jnp.float32)
    if cuts:
        entries = entries * block_levels(rng, extent, cuts, -0.22, 0.18)
    return jnp.clip(entries, -reach, reach).astype(kind)


def setup_inputs(seed: int = 0) -> dict:
    streams_of = jax.random.split(jax.random.key(seed), 7)
    features = noise(streams_of[0], (POINTS, C), 1.0, 6.0, ((0, 128),))
    zorder_to = draw_zorder_to(jax.random.fold_in(streams_of[6], 71), 0)
    hilbert_from = draw_hilbert_from(jax.random.fold_in(streams_of[6], 71), 0)
    qkv_weight = draw_qkv_weight(jax.random.fold_in(streams_of[6], 71), 0)
    proj_weight = noise(streams_of[4], (C, C), C ** -0.5, 0.375)
    out_grad = noise(streams_of[5], (POINTS, C), 1.0, 6.0, ((0, 128),))
    return dict(features=features, zorder_to=zorder_to, hilbert_from=hilbert_from, qkv_weight=qkv_weight, proj_weight=proj_weight, out_grad=out_grad)


def patch_step(carry, pieces, qkv_weight, proj_weight):
    qkv_total, proj_total = carry
    inputs, upstream_gradient = pieces
    width = inputs.shape[1]
    head_dim = width // HEADS
    scale = 1.0 / head_dim ** 0.5
    values_in = inputs.astype(jnp.float32)
    mean_removed = values_in - lax.optimization_barrier(jnp.mean(values_in, axis=1, keepdims=True))
    inverse_deviation = lax.rsqrt(lax.optimization_barrier(jnp.mean(mean_removed * mean_removed, axis=1, keepdims=True)) + 1e-05)
    standardized_input = mean_removed * inverse_deviation
    normalized_rows = standardized_input.astype(jnp.bfloat16)
    qkv = jnp.dot(normalized_rows, qkv_weight, preferred_element_type=jnp.float32).astype(jnp.bfloat16)
    attended_grad = jnp.einsum('nd,cd->nc', upstream_gradient.astype(jnp.float32), proj_weight.astype(jnp.float32)).astype(jnp.bfloat16)
    per_block = 4
    attended_parts = []
    query_parts = []
    key_parts = []
    value_parts = []
    span = per_block * head_dim
    for block in range(HEADS // per_block):
        low = block * span
        queries = qkv[:, low:low + span].reshape(-1, per_block, head_dim).astype(jnp.float32)
        key_rows = qkv[:, width + low:width + low + span].reshape(-1, per_block, head_dim).astype(jnp.float32)
        value_rows = qkv[:, 2 * width + low:2 * width + low + span].reshape(-1, per_block, head_dim).astype(jnp.float32)
        scores = jnp.einsum('qhd,khd->hqk', queries, key_rows) * scale
        maxima = lax.optimization_barrier(jnp.max(scores, axis=2, keepdims=True))
        expon = jnp.exp(scores - maxima)
        probs = (expon / lax.optimization_barrier(jnp.sum(expon, axis=2, keepdims=True))).astype(jnp.bfloat16)
        prob_f = probs.astype(jnp.float32)
        attended_parts.append(jnp.einsum('hqk,khd->qhd', prob_f, value_rows).reshape(-1, span))
        grad_rows = attended_grad[:, low:low + span].reshape(-1, per_block, head_dim).astype(jnp.float32)
        value_parts.append(jnp.einsum('hqk,qhd->khd', prob_f, grad_rows).reshape(-1, span))
        prob_grad = jnp.einsum('qhd,khd->hqk', grad_rows, value_rows)
        score_grad = (prob_f * (prob_grad - lax.optimization_barrier(jnp.sum(prob_grad * prob_f, axis=2, keepdims=True))) * scale).astype(jnp.bfloat16).astype(jnp.float32)
        query_parts.append(jnp.einsum('hqk,khd->qhd', score_grad, key_rows).reshape(-1, span))
        key_parts.append(jnp.einsum('hqk,qhd->khd', score_grad, queries).reshape(-1, span))
    attended = jnp.concatenate(attended_parts, axis=1).astype(jnp.bfloat16)
    qkv_cot = jnp.concatenate(query_parts + key_parts + value_parts, axis=1).astype(jnp.bfloat16)
    block_out = (values_in + jnp.dot(attended, proj_weight, preferred_element_type=jnp.float32)).astype(jnp.bfloat16)
    proj_total = proj_total + jnp.einsum('nc,nd->cd', attended.astype(jnp.float32), upstream_gradient.astype(jnp.float32))
    qkv_total = qkv_total + jnp.einsum('nc,nd->cd', normalized_rows.astype(jnp.float32), qkv_cot.astype(jnp.float32))
    normalized_gradient = jnp.einsum('ne,ce->nc', qkv_cot.astype(jnp.float32), qkv_weight.astype(jnp.float32))
    gradient_dot_mean = lax.optimization_barrier(jnp.mean(normalized_gradient, axis=1, keepdims=True))
    mixed_product_mean = lax.optimization_barrier(jnp.mean(normalized_gradient * standardized_input, axis=1, keepdims=True))
    sorted_gradient = (upstream_gradient.astype(jnp.float32) + inverse_deviation * (normalized_gradient - gradient_dot_mean - standardized_input * mixed_product_mean)).astype(jnp.bfloat16)
    return ((qkv_total, proj_total), (block_out, sorted_gradient))

def reference(features, zorder_to, hilbert_from, qkv_weight, proj_weight, out_grad):
    ordered = features[hilbert_from]
    patches = POINTS // PATCH
    start = (jnp.zeros((C, 3 * C), jnp.float32), jnp.zeros((C, C), jnp.float32))

    def stepper(carry, pieces):
        return patch_step(carry, pieces, qkv_weight, proj_weight)
    totals, results = lax.scan(stepper, start, (ordered.reshape(patches, PATCH, C), out_grad.reshape(patches, PATCH, C)))
    block_out = results[0].reshape(POINTS, C)
    sorted_gradient = results[1].reshape(POINTS, C)
    feature_grad = sorted_gradient[zorder_to]
    return (block_out, feature_grad, totals[0], totals[1])
```

```python
import functools

import jax
import jax.numpy as jnp
from jax import lax
from jax.experimental import pallas as pl
from jax.experimental.pallas import tpu as pltpu
from jax.sharding import PartitionSpec as P

HEADS = 16
HEAD_DIM = 16
PATCH = 1024
C = 256
QB = 512
CHUNK = 32
CHUNKS = PATCH // CHUNK
STRIP = 256
EXP_SCALE = 0.25 * 1.4426950408889634

F32 = jnp.float32
BF16 = jnp.bfloat16


def dot(a, b):
    return jnp.dot(a, b, preferred_element_type=F32)


def dot_nt(a, b):
    return lax.dot_general(a, b, (((1,), (1,)), ((), ())), preferred_element_type=F32)


def normalize(x):
    centered = x - jnp.mean(x, axis=1, keepdims=True)
    rstd = lax.rsqrt(jnp.mean(centered * centered, axis=1, keepdims=True) + 1e-05)
    return centered * rstd, rstd


def transposed(a):
    return a.astype(F32).T.astype(BF16)


MESH = pl.DeviceIdType.MESH
N_ROW = 8
N_COL = 16
DEVICES = N_ROW * N_COL
CHIPS = DEVICES // 2
CAP = PATCH // DEVICES
LANES = 128


def slots(key_row):
    key_col = jnp.broadcast_to(key_row, (LANES, PATCH)).T
    ranks = []
    for block in range(PATCH // LANES):
        keys = key_row[:, block * LANES : (block + 1) * LANES]
        below = jnp.where(key_col < keys, 1.0, 0.0)
        ranks.append(jnp.sum(below, axis=0, keepdims=True))
    return jnp.concatenate(ranks, axis=1)


def scatter_matrix(slot_row):
    position = lax.broadcasted_iota(jnp.int32, (PATCH, PATCH), 0).astype(F32)
    return jnp.where(slot_row == position, 1.0, 0.0).astype(BF16)


def gather_matrix(slot_row):
    slot_col = jnp.broadcast_to(slot_row, (LANES, PATCH)).T
    lane = lax.broadcasted_iota(jnp.int32, (PATCH, LANES), 1)
    blocks = [
        jnp.where(slot_col == (lane + block * LANES).astype(F32), 1.0, 0.0).astype(BF16)
        for block in range(PATCH // LANES)
    ]
    return jnp.concatenate(blocks, axis=1)


def chip_major(point):
    device = point // PATCH
    row, col = device // N_COL, device % N_COL
    return ((row // 2) * N_COL + col) * 2 + row % 2


def send_slots(zorder_ref):
    point = zorder_ref[...]
    return slots((chip_major(point) * PATCH + point % PATCH).astype(F32))


def recv_slots(hilbert_ref):
    local = lax.broadcasted_iota(jnp.int32, (1, PATCH), 1)
    return slots((chip_major(hilbert_ref[...]) * PATCH + local).astype(F32))


def packed(rows):
    rows = rows.reshape(DEVICES, CAP, C)
    pieces = jnp.concatenate([rows[:, :, :LANES], rows[:, :, LANES:]], axis=1).astype(BF16)
    return pieces.reshape(CHIPS, 2, 2 * CAP, LANES)


def unpacked(pieces):
    pieces = pieces.reshape(DEVICES, 2 * CAP, LANES).astype(F32)
    left = pieces[:, :CAP].reshape(PATCH, LANES)
    right = pieces[:, CAP:].reshape(PATCH, LANES)
    return jnp.concatenate([left, right], axis=1).astype(BF16)


def position():
    row, col = lax.axis_index("row"), lax.axis_index("col")
    core = lax.rem(row, 2)
    return core, (row // 2) * N_COL + col, (row + 1 - 2 * core, col)


def chip_after(step):
    core, chip, _ = position()
    other = lax.rem(chip + step, CHIPS)
    return other, ((other // N_COL) * 2 + core, lax.rem(other, N_COL))


def for_chips(act):
    def body(step, _):
        act(*chip_after(step))
        return 0

    lax.fori_loop(1, CHIPS, body, 0)


def greet(barrier):
    _, _, sibling = position()
    pl.semaphore_signal(barrier, inc=1, device_id=sibling, device_id_type=MESH)
    for_chips(
        lambda _, device: pl.semaphore_signal(
            barrier, inc=1, device_id=device, device_id_type=MESH
        )
    )


def pair_copy(out_ref, both_ref, send_sem, recv_sem):
    core, _, sibling = position()
    return pltpu.make_async_remote_copy(
        src_ref=out_ref.at[:, 1 - core],
        dst_ref=both_ref.at[:, core],
        send_sem=send_sem,
        recv_sem=recv_sem,
        device_id=sibling,
        device_id_type=MESH,
    )


def chip_copies(both_ref, in_ref, send_sem, recv_sem):
    _, chip, _ = position()
    for_chips(
        lambda other, device: pltpu.make_async_remote_copy(
            src_ref=both_ref.at[other],
            dst_ref=in_ref.at[chip],
            send_sem=send_sem,
            recv_sem=recv_sem,
            device_id=device,
            device_id_type=MESH,
        ).start()
    )
    in_ref[chip] = both_ref[chip]


def wait_bytes(ref, count, sem):
    view = ref.at[pl.ds(0, count)]
    pltpu.make_async_copy(view, view, sem).wait()


GROUPS = 2
GROUP_HEADS = HEADS // GROUPS
GROUP_ROWS = C // GROUPS


def tiles(section):
    section = section.reshape(GROUP_ROWS // 8, 8, C)
    halves = [section[:, None, :, :LANES], section[:, None, :, LANES:]]
    return jnp.concatenate(halves, axis=1).reshape(CHIPS // 2, 8, LANES)


def untiled(pieces):
    pieces = pieces.reshape(GROUP_ROWS // 8, 2, 8, LANES)
    return jnp.concatenate([pieces[:, 0], pieces[:, 1]], axis=2).reshape(GROUP_ROWS, C)


def block_kernel(
    feat_hbm, zorder_hbm, hilbert_hbm, wqkv_hbm, wp_hbm, og_hbm,
    out_ref, feat_grad_ref, qkvg_ref, projg_ref,
    feat_ref, zorder_ref, hilbert_ref, wqkv_ref, wp_ref, og_ref, oga_ref, x_ref, normed_ref,
    xhat_ref, rstd_ref, k_ref, v_ref, qt_ref, kt_ref, vt_ref, dot_ref,
    p_ref, ds_ref, e_ref, at_ref, dqt_ref, dkt_ref, dvt_ref,
    there_out, there_both, there_in, back_out, back_both, back_in,
    part_ref, half_ref, sum_ref, chunk_in_ref, result_ref, total_ref,
    load_sems, there_sems, back_sems, group_sems,
):
    half_width = C // 2
    core, chip, sibling = position()
    barrier = pltpu.get_barrier_semaphore()
    sources = (zorder_hbm, feat_hbm, hilbert_hbm, og_hbm, wp_hbm, wqkv_hbm)
    targets = (zorder_ref, feat_ref, hilbert_ref, og_ref, wp_ref, wqkv_ref)
    loads = [
        pltpu.make_async_copy(source, target, load_sems.at[i])
        for i, (source, target) in enumerate(zip(sources, targets))
    ]
    for load in loads:
        load.start()
    greet(barrier)
    loads[0].wait()
    scatter = scatter_matrix(send_slots(zorder_ref))
    loads[1].wait()
    there_out[...] = packed(dot(scatter, feat_ref[...]))
    pl.semaphore_wait(barrier, CHIPS)
    pair = pair_copy(there_out, there_both, there_sems.at[0], there_sems.at[1])
    pair.start()
    there_both[:, core] = there_out[:, core]
    pair.wait()
    chip_copies(there_both, there_in, there_sems.at[2], there_sems.at[3])

    for load in loads[2:]:
        load.wait()
    oga_ref[...] = dot(scatter_matrix(recv_slots(hilbert_ref)), og_ref[...]).astype(BF16)
    do_t = dot_nt(wp_ref[...], oga_ref[...]).astype(BF16).astype(F32)
    dot_ref[...] = (do_t * 0.25).astype(BF16).reshape(HEADS, HEAD_DIM, PATCH)
    wqkv_t = transposed(wqkv_ref[...])
    p_ref[1] = jnp.zeros((PATCH, QB), BF16)
    ds_ref[1] = jnp.zeros((PATCH, QB), BF16)
    dkt_ref[0] = jnp.zeros((HEAD_DIM, PATCH), F32)
    dvt_ref[0] = jnp.zeros((HEAD_DIM, PATCH), F32)
    wait_bytes(there_in, CHIPS - 1, there_sems.at[3])

    x = unpacked(there_in[...])
    x_ref[...] = x
    xhat, rstd = normalize(x.astype(F32))
    xhat_ref[...] = xhat
    rstd_ref[...] = rstd
    normed = xhat.astype(BF16)
    normed_ref[...] = normed
    kv = dot(normed, wqkv_ref[:, C:]).astype(BF16)
    for ref, low in ((k_ref, 0), (v_ref, C)):
        ref[0] = kv[:, low : low + half_width]
        ref[1] = kv[:, low + half_width : low + C]
    qkv_t = dot(wqkv_t, transposed(normed)).astype(BF16)
    for ref, part in ((qt_ref, 0), (kt_ref, 1), (vt_ref, 2)):
        ref[...] = qkv_t[part * C : (part + 1) * C].reshape(HEADS, HEAD_DIM, PATCH)

    def group_part(g):
        heads = slice(g * GROUP_HEADS, (g + 1) * GROUP_HEADS)
        for section, ref in enumerate((dqt_ref, dkt_ref, dvt_ref, at_ref)):
            rows = ref[heads].reshape(GROUP_ROWS, PATCH).astype(BF16)
            other = oga_ref if section == 3 else normed_ref
            low = section % 2 * (CHIPS // 2)
            part_ref[g, section // 2, low : low + CHIPS // 2] = tiles(dot(rows, other[...]))

    def group_half(g):
        return pltpu.make_async_remote_copy(
            src_ref=part_ref.at[g, 1 - core],
            dst_ref=half_ref.at[g],
            send_sem=group_sems.at[g, 0],
            recv_sem=group_sems.at[g, 1],
            device_id=sibling,
            device_id_type=MESH,
        )

    def group_scatter(g):
        group_half(g).wait()
        sum_ref[g] = part_ref[g, core] + half_ref[g]
        for_chips(
            lambda other, device: pltpu.make_async_remote_copy(
                src_ref=sum_ref.at[g, other],
                dst_ref=chunk_in_ref.at[g, chip],
                send_sem=group_sems.at[g, 2],
                recv_sem=group_sems.at[g, 3],
                device_id=device,
                device_id_type=MESH,
            ).start()
        )
        chunk_in_ref[g, chip] = sum_ref[g, chip]

    def group_gather(g):
        wait_bytes(chunk_in_ref.at[g], CHIPS - 1, group_sems.at[g, 3])
        result_ref[g] = jnp.sum(chunk_in_ref[g], axis=0)
        for_chips(
            lambda other, device: pltpu.make_async_remote_copy(
                src_ref=result_ref.at[g],
                dst_ref=total_ref.at[g, core, chip],
                send_sem=group_sems.at[g, 4],
                recv_sem=group_sems.at[g, 5],
                device_id=device,
                device_id_type=MESH,
            ).start()
        )
        total_ref[g, core, chip] = result_ref[g]

    def group_final(g):
        return pltpu.make_async_remote_copy(
            src_ref=total_ref.at[g, core],
            dst_ref=total_ref.at[g, core],
            send_sem=group_sems.at[g, 6],
            recv_sem=group_sems.at[g, 7],
            device_id=sibling,
            device_id_type=MESH,
        )

    def group_finish(g):
        wait_bytes(total_ref.at[g, core], CHIPS - 1, group_sems.at[g, 5])
        group_final(g).start()

    def group_close(g):
        group_final(g).wait()
        wait_bytes(sum_ref.at[g], CHIPS - 1, group_sems.at[g, 2])
        wait_bytes(sum_ref.at[g], CHIPS - 1, group_sems.at[g, 4])
        rows = slice(g * GROUP_ROWS, (g + 1) * GROUP_ROWS)
        for section in range(4):
            low = section % 2 * (CHIPS // 2)
            sums = untiled(total_ref[g, section // 2, low : low + CHIPS // 2])
            if section == 3:
                projg_ref[rows, :] = sums
            else:
                low = section * C + g * GROUP_ROWS
                qkvg_ref[:, low : low + GROUP_ROWS] = sums.T

    def query_side(h, block):
        ql = slice(block * QB, (block + 1) * QB)
        dqt_ref[h, :, ql] = dot(kt_ref[h], ds_ref[block]).astype(BF16)

    def value_side(h, block):
        ql = slice(block * QB, (block + 1) * QB)
        dv = dot_nt(dot_ref[h, :, ql], p_ref[block]) * 4.0
        dvt_ref[h] = dvt_ref[h] + dv if block else dv

    def key_side(h, block):
        ql = slice(block * QB, (block + 1) * QB)
        dk = dot_nt(qt_ref[h, :, ql], ds_ref[block])
        dkt_ref[h] = dkt_ref[h] + dk if block else dk

    behind = (query_side, value_side, key_side)

    def block_step(h, block, km, vm, before):
        half = h // 8
        ql = slice(block * QB, (block + 1) * QB)
        qt = qt_ref[pl.ds(half * 8, 8), :, ql].reshape(half_width, QB)
        dot_t = dot_ref[pl.ds(half * 8, 8), :, ql].reshape(half_width, QB)
        tops, sums = [], []
        for j in range(PATCH // STRIP):
            s = dot(km[j * STRIP : (j + 1) * STRIP], qt)
            if j < len(behind):
                behind[j](before, 1 - block)
            for c in range(STRIP // CHUNK):
                part = s[c * CHUNK : (c + 1) * CHUNK].reshape(CHUNK // 8, 8, QB)
                top = jnp.max(part, axis=0)
                e = jnp.exp2((part - top) * EXP_SCALE)
                e_ref[block, j * (STRIP // CHUNK) + c] = e
                tops.append(top)
                sums.append(jnp.sum(e, axis=0))
        peak = functools.reduce(jnp.maximum, tops)
        peak = jnp.max(peak, axis=0, keepdims=True)
        weights = [jnp.exp2((top - peak) * EXP_SCALE) for top in tops]
        total = functools.reduce(jnp.add, [a * w for a, w in zip(sums, weights)])
        inverse = 1.0 / jnp.sum(total, axis=0, keepdims=True)
        for c in range(CHUNKS):
            p = e_ref[block, c] * (weights[c] * inverse)
            p_ref[block, c * CHUNK : (c + 1) * CHUNK] = p.reshape(CHUNK, QB).astype(BF16)
        ot = dot(vt_ref[h], p_ref[block])
        at_ref[h, :, ql] = ot.astype(BF16)
        delta = jnp.sum(ot * dot_ref[h, :, ql].astype(F32), axis=0, keepdims=True)
        for j in range(PATCH // STRIP):
            dp = dot(vm[j * STRIP : (j + 1) * STRIP], dot_t)
            for c in range(STRIP // CHUNK):
                rows = slice(j * STRIP + c * CHUNK, j * STRIP + (c + 1) * CHUNK)
                p = p_ref[block, rows].astype(F32)
                ds = p * (dp[c * CHUNK : (c + 1) * CHUNK] - delta)
                ds_ref[block, rows] = ds.astype(BF16)

    def head_step(h, _):
        half = h // 8
        lane = lax.broadcasted_iota(jnp.int32, (1, half_width), 1) // HEAD_DIM
        mask = (lane == h % 8).astype(F32).astype(BF16)
        km = k_ref[half] * mask
        vm = v_ref[half] * mask
        block_step(h, 0, km, vm, jnp.maximum(h - 1, 0))
        block_step(h, 1, km, vm, h)

        @pl.when(h == GROUP_HEADS)
        def _():
            group_part(0)
            group_half(0).start()

        @pl.when(h == GROUP_HEADS + 2)
        def _():
            group_scatter(0)

        @pl.when(h == GROUP_HEADS + 4)
        def _():
            group_gather(0)

        @pl.when(h == GROUP_HEADS + 6)
        def _():
            group_finish(0)

        return 0

    lax.fori_loop(0, HEADS, head_step, 0)
    for side in behind:
        side(HEADS - 1, 1)

    group_part(1)
    group_half(1).start()
    cot_t = [ref[...].reshape(C, PATCH).astype(BF16) for ref in (dqt_ref, dkt_ref, dvt_ref)]
    ng = dot(wqkv_ref[...], jnp.concatenate(cot_t, axis=0)).T
    xhat = xhat_ref[...]
    ng_mean = jnp.mean(ng, axis=1, keepdims=True)
    mixed = jnp.mean(ng * xhat, axis=1, keepdims=True)
    back_out[...] = packed(
        oga_ref[...].astype(F32) + rstd_ref[...] * (ng - ng_mean - xhat * mixed)
    )
    back = pair_copy(back_out, back_both, back_sems.at[0], back_sems.at[1])
    back.start()
    back_both[:, core] = back_out[:, core]
    group_scatter(1)
    back.wait()
    chip_copies(back_both, back_in, back_sems.at[2], back_sems.at[3])

    at = at_ref[...].reshape(C, PATCH)
    block_out = x_ref[...].astype(F32) + dot(transposed(at), wp_ref[...])
    gather = gather_matrix(recv_slots(hilbert_ref))
    out_ref[...] = dot(gather, block_out.astype(BF16)).astype(BF16)
    group_close(0)
    group_gather(1)
    gather = gather_matrix(send_slots(zorder_ref))
    wait_bytes(back_in, CHIPS - 1, back_sems.at[3])
    feat_grad_ref[...] = dot(gather, unpacked(back_in[...])).astype(BF16)
    group_finish(1)
    wait_bytes(there_in, CHIPS - 1, there_sems.at[2])
    wait_bytes(back_in, CHIPS - 1, back_sems.at[2])
    group_close(1)


def on_device(features, zorder_to, hilbert_from, qkv_weight, proj_weight, out_grad):
    vmem = pl.BlockSpec(memory_space=pltpu.VMEM)
    points = pltpu.VMEM((PATCH, C), BF16)
    index = pltpu.VMEM((1, PATCH), jnp.int32)
    halves = pltpu.VMEM((2, PATCH, C // 2), BF16)
    heads_t = pltpu.VMEM((HEADS, HEAD_DIM, PATCH), BF16)
    heads_f = pltpu.VMEM((HEADS, HEAD_DIM, PATCH), F32)
    queries = pltpu.VMEM((2, PATCH, QB), BF16)
    pieces = pltpu.VMEM((CHIPS, 2, 2 * CAP, LANES), BF16)
    both_cores = pltpu.VMEM((GROUPS, 2, CHIPS, 8, LANES), F32)
    one_core = pltpu.VMEM((GROUPS, CHIPS, 8, LANES), F32)
    return pl.pallas_call(
        block_kernel,
        out_shape=(
            jax.ShapeDtypeStruct((PATCH, C), BF16),
            jax.ShapeDtypeStruct((PATCH, C), BF16),
            jax.ShapeDtypeStruct((C, 3 * C), F32),
            jax.ShapeDtypeStruct((C, C), F32),
        ),
        in_specs=[pl.BlockSpec(memory_space=pl.ANY)] * 6,
        out_specs=(vmem,) * 4,
        scratch_shapes=[
            points, index, index,
            pltpu.VMEM((C, 3 * C), BF16),
            pltpu.VMEM((C, C), BF16),
            points, points, points, points,
            pltpu.VMEM((PATCH, C), F32),
            pltpu.VMEM((PATCH, 1), F32),
            halves, halves, heads_t, heads_t, heads_t, heads_t,
            queries, queries,
            pltpu.VMEM((2, CHUNKS, CHUNK // 8, 8, QB), F32),
            heads_t, heads_t, heads_f, heads_f,
            pieces, pieces, pieces, pieces, pieces, pieces,
            both_cores, one_core, one_core, one_core,
            pltpu.VMEM((GROUPS, 8, LANES), F32),
            both_cores,
            pltpu.SemaphoreType.DMA((6,)),
            pltpu.SemaphoreType.DMA((4,)),
            pltpu.SemaphoreType.DMA((4,)),
            pltpu.SemaphoreType.DMA((GROUPS, 8)),
        ],
        compiler_params=pltpu.CompilerParams(
            collective_id=0, has_side_effects=True, vmem_limit_bytes=60 * 1024 * 1024
        ),
        cost_estimate=pl.CostEstimate(
            flops=28_000_000_000, bytes_accessed=5_000_000, transcendentals=16_777_216
        ),
    )(
        features,
        zorder_to.reshape(1, PATCH),
        hilbert_from.reshape(1, PATCH),
        qkv_weight,
        proj_weight,
        out_grad,
    )


def solution(mesh):
    in_specs = (
        P(("row", "col"), None),
        P(("row", "col")),
        P(("row", "col")),
        P(),
        P(),
        P(("row", "col"), None),
    )
    out_specs = (P(("row", "col"), None), P(("row", "col"), None), P(), P())
    return jax.shard_map(
        on_device, mesh=mesh, in_specs=in_specs, out_specs=out_specs, check_vma=False
    )
```

```python
import functools

import jax
import jax.numpy as jnp
from jax import lax
from jax.experimental import pallas as pl
from jax.experimental.pallas import tpu as pltpu
from jax.sharding import PartitionSpec as P

HEADS = 16
HEAD_DIM = 16
PATCH = 1024
C = 256
QB = 512
CHUNK = 32
CHUNKS = PATCH // CHUNK
STRIP = 256
EXP_SCALE = 0.25 * 1.4426950408889634

F32 = jnp.float32
BF16 = jnp.bfloat16


def dot(a, b):
    return jnp.dot(a, b, preferred_element_type=F32)


def dot_nt(a, b):
    return lax.dot_general(a, b, (((1,), (1,)), ((), ())), preferred_element_type=F32)


def normalize(x):
    centered = x - jnp.mean(x, axis=1, keepdims=True)
    rstd = lax.rsqrt(jnp.mean(centered * centered, axis=1, keepdims=True) + 1e-05)
    return centered * rstd, rstd


def transposed(a):
    return a.astype(F32).T.astype(BF16)


MESH = pl.DeviceIdType.MESH
N_ROW = 8
N_COL = 16
DEVICES = N_ROW * N_COL
CHIPS = DEVICES // 2
CAP = PATCH // DEVICES
LANES = 128


STRIDE = 27
INVERSE_STRIDE = 19
PARTS = 4
PART_DEVICES = DEVICES // PARTS
PART_ROWS = PATCH // PARTS


def as_column(row):
    return jnp.broadcast_to(row, (LANES, PATCH)).T


def slots(key_row):
    key_col = as_column(key_row)
    ranks = []
    for block in range(PATCH // LANES):
        keys = key_row[:, block * LANES : (block + 1) * LANES]
        below = jnp.where(key_col < keys, 1.0, 0.0)
        ranks.append(jnp.sum(below, axis=0, keepdims=True))
    return jnp.concatenate(ranks, axis=1)


def scatter_rows(slot_row, part):
    row = lax.broadcasted_iota(jnp.int32, (PART_ROWS, PATCH), 0) + part * PART_ROWS
    return jnp.where(slot_row == row.astype(F32), 1.0, 0.0).astype(BF16)


def gather_columns(slot_col, part):
    lane = lax.broadcasted_iota(jnp.int32, (PATCH, LANES), 1) + part * PART_ROWS
    blocks = [
        jnp.where(slot_col == (lane + low).astype(F32), 1.0, 0.0).astype(BF16)
        for low in range(0, PART_ROWS, LANES)
    ]
    return jnp.concatenate(blocks, axis=1)


def linear(row, col):
    return ((row // 2) * N_COL + col) * 2 + row % 2


def my_linear():
    row, col = lax.axis_index("row"), lax.axis_index("col")
    return ((row // 2) * N_COL + col) * 2 + lax.rem(row, 2)


def coordinates(index):
    chip = index // 2
    return (chip // N_COL) * 2 + lax.rem(index, 2), lax.rem(chip, N_COL)


def relative_slot(offset):
    return (offset + DEVICES) * INVERSE_STRIDE % DEVICES


def send_slots(zorder_ref):
    point = zorder_ref[...]
    device = point // PATCH
    there = linear(device // N_COL, device % N_COL)
    return slots((relative_slot(there - my_linear()) * PATCH + point % PATCH).astype(F32))


def recv_slots(hilbert_ref):
    device = hilbert_ref[...] // PATCH
    there = linear(device // N_COL, device % N_COL)
    local = lax.broadcasted_iota(jnp.int32, (1, PATCH), 1)
    return slots((relative_slot(my_linear() - there) * PATCH + local).astype(F32))


def packed(rows):
    rows = rows.reshape(PART_DEVICES, CAP, C)
    return jnp.concatenate([rows[:, :, :LANES], rows[:, :, LANES:]], axis=1).astype(BF16)


def unpacked(pieces):
    pieces = pieces.astype(F32)
    left = pieces[:, :CAP].reshape(PART_ROWS, LANES)
    right = pieces[:, CAP:].reshape(PART_ROWS, LANES)
    return jnp.concatenate([left, right], axis=1).astype(BF16)


def part_pieces(part):
    return slice(part * PART_DEVICES, (part + 1) * PART_DEVICES)


def position():
    row, col = lax.axis_index("row"), lax.axis_index("col")
    core = lax.rem(row, 2)
    return core, (row // 2) * N_COL + col, (row + 1 - 2 * core, col)


def for_chips(act):
    core, chip, _ = position()

    def body(step, _):
        other = lax.rem(chip + step * 13, CHIPS)
        act(other, ((other // N_COL) * 2 + core, lax.rem(other, N_COL)))
        return 0

    lax.fori_loop(1, CHIPS, body, 0)


def greet(barrier):
    me = my_linear()

    def body(step, _):
        device = coordinates(lax.rem(me + step, DEVICES))
        pl.semaphore_signal(barrier, inc=1, device_id=device, device_id_type=MESH)
        return 0

    lax.fori_loop(1, DEVICES, body, 0)


def send_part(out_ref, in_ref, part, stride, send_sem, recv_sem):
    me = my_linear()

    def body(step, _):
        pltpu.make_async_remote_copy(
            src_ref=out_ref.at[step],
            dst_ref=in_ref.at[step],
            send_sem=send_sem,
            recv_sem=recv_sem,
            device_id=coordinates(lax.rem(me + step * stride, DEVICES)),
            device_id_type=MESH,
        ).start()
        return 0

    lax.fori_loop(max(part * PART_DEVICES, 1), (part + 1) * PART_DEVICES, body, 0)
    if part == 0:
        in_ref[0] = out_ref[0]


def wait_part(in_ref, part, recv_sem):
    wait_bytes(in_ref, PART_DEVICES - (part == 0), recv_sem)


def wait_bytes(ref, count, sem):
    view = ref.at[pl.ds(0, count)]
    pltpu.make_async_copy(view, view, sem).wait()


GROUPS = 2
GROUP_HEADS = HEADS // GROUPS
GROUP_ROWS = C // GROUPS


def tiles(section):
    section = section.reshape(GROUP_ROWS // 8, 8, C)
    halves = [section[:, None, :, :LANES], section[:, None, :, LANES:]]
    return jnp.concatenate(halves, axis=1).reshape(CHIPS // 2, 8, LANES)


def untiled(pieces):
    pieces = pieces.reshape(GROUP_ROWS // 8, 2, 8, LANES)
    return jnp.concatenate([pieces[:, 0], pieces[:, 1]], axis=2).reshape(GROUP_ROWS, C)


def block_kernel(
    feat_hbm, zorder_hbm, hilbert_hbm, wqkv_hbm, wp_hbm, og_hbm,
    out_hbm, feat_grad_hbm, qkvg_hbm, projg_hbm,
    out_ref, feat_grad_ref, qkvg_ref, projg_ref,
    feat_ref, zorder_ref, hilbert_ref, wqkv_ref, wp_ref, og_ref, oga_ref, x_ref, normed_ref,
    wqkv_t_ref, xhat_ref, rstd_ref, k_ref, v_ref, qt_ref, kt_ref, vt_ref, dot_ref,
    p_ref, ds_ref, e_ref, at_ref, dqt_ref, dkt_ref, dvt_ref,
    there_out, there_in, back_out, back_in,
    part_ref, half_ref, sum_ref, chunk_in_ref, result_ref, total_ref,
    load_sems, there_sems, back_sems, group_sems, store_sems,
):
    half_width = C // 2
    core, chip, sibling = position()
    barrier = pltpu.get_barrier_semaphore()
    sources = (zorder_hbm, feat_hbm, hilbert_hbm, og_hbm, wp_hbm, wqkv_hbm)
    targets = (zorder_ref, feat_ref, hilbert_ref, og_ref, wp_ref, wqkv_ref)
    loads = [
        pltpu.make_async_copy(source, target, load_sems.at[i])
        for i, (source, target) in enumerate(zip(sources, targets))
    ]
    stores = [
        pltpu.make_async_copy(source, target, store_sems.at[i])
        for i, (source, target) in enumerate((
            (out_ref, out_hbm),
            (feat_grad_ref, feat_grad_hbm),
            (qkvg_ref, qkvg_hbm),
            (projg_ref, projg_hbm),
        ))
    ]
    for load in loads:
        load.start()
    greet(barrier)
    loads[0].wait()
    there_slots = send_slots(zorder_ref)
    loads[1].wait()
    for part in range(PARTS):
        rows = dot(scatter_rows(there_slots, part), feat_ref[...])
        there_out[part_pieces(part)] = packed(rows)
        if part == 0:
            pl.semaphore_wait(barrier, DEVICES - 1)
        send_part(
            there_out, there_in, part, STRIDE, there_sems.at[PARTS], there_sems.at[part]
        )

    for load in loads[2:]:
        load.wait()
    back_slots = recv_slots(hilbert_ref)
    for part in range(PARTS):
        rows = slice(part * PART_ROWS, (part + 1) * PART_ROWS)
        oga_ref[rows] = dot(scatter_rows(back_slots, part), og_ref[...]).astype(BF16)
    do_t = dot_nt(wp_ref[...], oga_ref[...]).astype(BF16).astype(F32)
    dot_ref[...] = (do_t * 0.25).astype(BF16).reshape(HEADS, HEAD_DIM, PATCH)
    wqkv_t_ref[...] = transposed(wqkv_ref[...])
    p_ref[1] = jnp.zeros((PATCH, QB), BF16)
    ds_ref[1] = jnp.zeros((PATCH, QB), BF16)
    dkt_ref[0] = jnp.zeros((HEAD_DIM, PATCH), F32)
    dvt_ref[0] = jnp.zeros((HEAD_DIM, PATCH), F32)

    for part in range(PARTS):
        wait_part(there_in, part, there_sems.at[part])
        rows = slice(part * PART_ROWS, (part + 1) * PART_ROWS)
        x = unpacked(there_in[part_pieces(part)])
        x_ref[rows] = x
        xhat, rstd = normalize(x.astype(F32))
        xhat_ref[rows] = xhat
        rstd_ref[rows] = rstd
        normed = xhat.astype(BF16)
        normed_ref[rows] = normed
        kv = dot(normed, wqkv_ref[:, C:]).astype(BF16)
        for ref, low in ((k_ref, 0), (v_ref, C)):
            ref[0, rows] = kv[:, low : low + half_width]
            ref[1, rows] = kv[:, low + half_width : low + C]
        qkv_t = dot(wqkv_t_ref[...], transposed(normed)).astype(BF16)
        for ref, low in ((qt_ref, 0), (kt_ref, C), (vt_ref, 2 * C)):
            ref[:, :, rows] = qkv_t[low : low + C].reshape(HEADS, HEAD_DIM, PART_ROWS)

    def group_part(g):
        heads = slice(g * GROUP_HEADS, (g + 1) * GROUP_HEADS)
        for section, ref in enumerate((dqt_ref, dkt_ref, dvt_ref, at_ref)):
            rows = ref[heads].reshape(GROUP_ROWS, PATCH).astype(BF16)
            other = oga_ref if section == 3 else normed_ref
            low = section % 2 * (CHIPS // 2)
            part_ref[g, section // 2, low : low + CHIPS // 2] = tiles(dot(rows, other[...]))

    def group_half(g):
        return pltpu.make_async_remote_copy(
            src_ref=part_ref.at[g, 1 - core],
            dst_ref=half_ref.at[g],
            send_sem=group_sems.at[g, 0],
            recv_sem=group_sems.at[g, 1],
            device_id=sibling,
            device_id_type=MESH,
        )

    def group_scatter(g):
        group_half(g).wait()
        sum_ref[g] = part_ref[g, core] + half_ref[g]
        for_chips(
            lambda other, device: pltpu.make_async_remote_copy(
                src_ref=sum_ref.at[g, other],
                dst_ref=chunk_in_ref.at[g, chip],
                send_sem=group_sems.at[g, 2],
                recv_sem=group_sems.at[g, 3],
                device_id=device,
                device_id_type=MESH,
            ).start()
        )
        chunk_in_ref[g, chip] = sum_ref[g, chip]

    def group_gather(g):
        wait_bytes(chunk_in_ref.at[g], CHIPS - 1, group_sems.at[g, 3])
        result_ref[g] = jnp.sum(chunk_in_ref[g], axis=0)
        for_chips(
            lambda other, device: pltpu.make_async_remote_copy(
                src_ref=result_ref.at[g],
                dst_ref=total_ref.at[g, core, chip],
                send_sem=group_sems.at[g, 4],
                recv_sem=group_sems.at[g, 5],
                device_id=device,
                device_id_type=MESH,
            ).start()
        )
        total_ref[g, core, chip] = result_ref[g]

    def group_final(g):
        return pltpu.make_async_remote_copy(
            src_ref=total_ref.at[g, core],
            dst_ref=total_ref.at[g, core],
            send_sem=group_sems.at[g, 6],
            recv_sem=group_sems.at[g, 7],
            device_id=sibling,
            device_id_type=MESH,
        )

    def group_finish(g):
        wait_bytes(total_ref.at[g, core], CHIPS - 1, group_sems.at[g, 5])
        group_final(g).start()

    def group_close(g):
        group_final(g).wait()
        wait_bytes(sum_ref.at[g], CHIPS - 1, group_sems.at[g, 2])
        wait_bytes(sum_ref.at[g], CHIPS - 1, group_sems.at[g, 4])
        rows = slice(g * GROUP_ROWS, (g + 1) * GROUP_ROWS)
        for section in range(4):
            low = section % 2 * (CHIPS // 2)
            sums = untiled(total_ref[g, section // 2, low : low + CHIPS // 2])
            if section == 3:
                projg_ref[rows, :] = sums
            else:
                low = section * C + g * GROUP_ROWS
                qkvg_ref[:, low : low + GROUP_ROWS] = sums.T

    def query_side(h, block):
        ql = slice(block * QB, (block + 1) * QB)
        dqt_ref[h, :, ql] = dot(kt_ref[h], ds_ref[block]).astype(BF16)

    def value_side(h, block):
        ql = slice(block * QB, (block + 1) * QB)
        dv = dot_nt(dot_ref[h, :, ql], p_ref[block]) * 4.0
        dvt_ref[h] = dvt_ref[h] + dv if block else dv

    def key_side(h, block):
        ql = slice(block * QB, (block + 1) * QB)
        dk = dot_nt(qt_ref[h, :, ql], ds_ref[block])
        dkt_ref[h] = dkt_ref[h] + dk if block else dk

    def block_step(h, block, km, vm, before):
        half = h // 8
        ql = slice(block * QB, (block + 1) * QB)
        qt = qt_ref[pl.ds(half * 8, 8), :, ql].reshape(half_width, QB)
        dot_t = dot_ref[pl.ds(half * 8, 8), :, ql].reshape(half_width, QB)
        tops, sums = [], []
        for j in range(PATCH // STRIP):
            s = dot(km[j * STRIP : (j + 1) * STRIP], qt)
            if j == 0:
                query_side(before, 1 - block)
            for c in range(STRIP // CHUNK):
                part = s[c * CHUNK : (c + 1) * CHUNK].reshape(CHUNK // 8, 8, QB)
                top = jnp.max(part, axis=0)
                e = jnp.exp2((part - top) * EXP_SCALE)
                e_ref[block, j * (STRIP // CHUNK) + c] = e
                tops.append(top)
                sums.append(jnp.sum(e, axis=0))
        value_side(before, 1 - block)
        peak = functools.reduce(jnp.maximum, tops)
        peak = jnp.max(peak, axis=0, keepdims=True)
        weights = [jnp.exp2((top - peak) * EXP_SCALE) for top in tops]
        total = functools.reduce(jnp.add, [a * w for a, w in zip(sums, weights)])
        inverse = 1.0 / jnp.sum(total, axis=0, keepdims=True)
        for c in range(CHUNKS):
            p = e_ref[block, c] * (weights[c] * inverse)
            p_ref[block, c * CHUNK : (c + 1) * CHUNK] = p.reshape(CHUNK, QB).astype(BF16)
        ot = dot(vt_ref[h], p_ref[block])
        key_side(before, 1 - block)
        at_ref[h, :, ql] = ot.astype(BF16)
        delta = jnp.sum(ot * dot_ref[h, :, ql].astype(F32), axis=0, keepdims=True)
        for j in range(PATCH // STRIP):
            dp = dot(vm[j * STRIP : (j + 1) * STRIP], dot_t)
            for c in range(STRIP // CHUNK):
                rows = slice(j * STRIP + c * CHUNK, j * STRIP + (c + 1) * CHUNK)
                p = p_ref[block, rows].astype(F32)
                ds = p * (dp[c * CHUNK : (c + 1) * CHUNK] - delta)
                ds_ref[block, rows] = ds.astype(BF16)

    def head_step(h, _):
        half = h // 8
        lane = lax.broadcasted_iota(jnp.int32, (1, half_width), 1) // HEAD_DIM
        mask = (lane == h % 8).astype(F32).astype(BF16)
        km = k_ref[half] * mask
        vm = v_ref[half] * mask
        block_step(h, 0, km, vm, jnp.maximum(h - 1, 0))
        block_step(h, 1, km, vm, h)

        @pl.when(h == GROUP_HEADS)
        def _():
            group_part(0)
            group_half(0).start()

        @pl.when(h == GROUP_HEADS + 2)
        def _():
            group_scatter(0)

        @pl.when(h == GROUP_HEADS + 4)
        def _():
            group_gather(0)

        @pl.when(h == GROUP_HEADS + 6)
        def _():
            group_finish(0)

        return 0

    lax.fori_loop(0, HEADS, head_step, 0)
    query_side(HEADS - 1, 1)
    value_side(HEADS - 1, 1)
    key_side(HEADS - 1, 1)

    group_part(1)
    group_half(1).start()
    cot_t = [ref[...].reshape(C, PATCH).astype(BF16) for ref in (dqt_ref, dkt_ref, dvt_ref)]
    ng_t = dot(wqkv_ref[...], jnp.concatenate(cot_t, axis=0))
    for part in range(PARTS):
        rows = slice(part * PART_ROWS, (part + 1) * PART_ROWS)
        ng = ng_t[:, rows].T
        xhat = xhat_ref[rows]
        ng_mean = jnp.mean(ng, axis=1, keepdims=True)
        mixed = jnp.mean(ng * xhat, axis=1, keepdims=True)
        back_out[part_pieces(part)] = packed(
            oga_ref[rows].astype(F32) + rstd_ref[rows] * (ng - ng_mean - xhat * mixed)
        )
        send_part(
            back_out, back_in, part, DEVICES - STRIDE, back_sems.at[PARTS], back_sems.at[part]
        )
        if part == 1:
            group_scatter(1)

    at = at_ref[...].reshape(C, PATCH)
    block_out = x_ref[...].astype(F32) + dot(transposed(at), wp_ref[...])
    block_out = block_out.astype(BF16)
    slot_col = as_column(recv_slots(hilbert_ref))
    gather = [gather_columns(slot_col, part) for part in range(PARTS)]
    out_ref[...] = dot(jnp.concatenate(gather, axis=1), block_out).astype(BF16)
    stores[0].start()
    group_close(0)
    group_gather(1)
    slot_col = as_column(send_slots(zorder_ref))
    total = jnp.zeros((PATCH, C), F32)
    for part in range(PARTS):
        gather = gather_columns(slot_col, part)
        wait_part(back_in, part, back_sems.at[part])
        total += dot(gather, unpacked(back_in[part_pieces(part)]))
    feat_grad_ref[...] = total.astype(BF16)
    stores[1].start()
    group_finish(1)
    wait_bytes(there_in, DEVICES - 1, there_sems.at[PARTS])
    wait_bytes(back_in, DEVICES - 1, back_sems.at[PARTS])
    group_close(1)
    stores[2].start()
    stores[3].start()
    for store in stores:
        store.wait()


def finish_kernel(*refs):
    sources, targets, rooms, sems = refs[:4], refs[4:8], refs[8:12], refs[12]
    ins = [
        pltpu.make_async_copy(source, room, sems.at[0, i])
        for i, (source, room) in enumerate(zip(sources, rooms))
    ]
    outs = [
        pltpu.make_async_copy(room, target, sems.at[1, i])
        for i, (room, target) in enumerate(zip(rooms, targets))
    ]
    for copy in ins:
        copy.start()
    for copy_in, copy_out in zip(ins, outs):
        copy_in.wait()
        copy_out.start()
    for copy in outs:
        copy.wait()


def on_device(features, zorder_to, hilbert_from, qkv_weight, proj_weight, out_grad):
    anywhere = pl.BlockSpec(memory_space=pl.ANY)
    out_shape = (
        jax.ShapeDtypeStruct((PATCH, C), BF16),
        jax.ShapeDtypeStruct((PATCH, C), BF16),
        jax.ShapeDtypeStruct((C, 3 * C), F32),
        jax.ShapeDtypeStruct((C, C), F32),
    )
    points = pltpu.VMEM((PATCH, C), BF16)
    index = pltpu.VMEM((1, PATCH), jnp.int32)
    halves = pltpu.VMEM((2, PATCH, C // 2), BF16)
    heads_t = pltpu.VMEM((HEADS, HEAD_DIM, PATCH), BF16)
    heads_f = pltpu.VMEM((HEADS, HEAD_DIM, PATCH), F32)
    queries = pltpu.VMEM((2, PATCH, QB), BF16)
    pieces = pltpu.VMEM((DEVICES, 2 * CAP, LANES), BF16)
    both_cores = pltpu.VMEM((GROUPS, 2, CHIPS, 8, LANES), F32)
    one_core = pltpu.VMEM((GROUPS, CHIPS, 8, LANES), F32)
    results = pl.pallas_call(
        block_kernel,
        out_shape=out_shape,
        in_specs=[anywhere] * 6,
        out_specs=(anywhere,) * 4,
        scratch_shapes=[
            points, points,
            pltpu.VMEM((C, 3 * C), F32),
            pltpu.VMEM((C, C), F32),
            points, index, index,
            pltpu.VMEM((C, 3 * C), BF16),
            pltpu.VMEM((C, C), BF16),
            points, points, points, points,
            pltpu.VMEM((3 * C, C), BF16),
            pltpu.VMEM((PATCH, C), F32),
            pltpu.VMEM((PATCH, 1), F32),
            halves, halves, heads_t, heads_t, heads_t, heads_t,
            queries, queries,
            pltpu.VMEM((2, CHUNKS, CHUNK // 8, 8, QB), F32),
            heads_t, heads_t, heads_f, heads_f,
            pieces, pieces, pieces, pieces,
            both_cores, one_core, one_core, one_core,
            pltpu.VMEM((GROUPS, 8, LANES), F32),
            both_cores,
            pltpu.SemaphoreType.DMA((6,)),
            pltpu.SemaphoreType.DMA((PARTS + 1,)),
            pltpu.SemaphoreType.DMA((PARTS + 1,)),
            pltpu.SemaphoreType.DMA((GROUPS, 8)),
            pltpu.SemaphoreType.DMA((4,)),
        ],
        compiler_params=pltpu.CompilerParams(
            collective_id=0, has_side_effects=True, vmem_limit_bytes=60 * 1024 * 1024
        ),
        cost_estimate=pl.CostEstimate(
            flops=28_000_000_000, bytes_accessed=5_000_000, transcendentals=16_777_216
        ),
    )(
        features,
        zorder_to.reshape(1, PATCH),
        hilbert_from.reshape(1, PATCH),
        qkv_weight,
        proj_weight,
        out_grad,
    )
    return pl.pallas_call(
        finish_kernel,
        out_shape=out_shape,
        in_specs=[anywhere] * 4,
        out_specs=(anywhere,) * 4,
        scratch_shapes=[
            points, points,
            pltpu.VMEM((C, 3 * C), F32),
            pltpu.VMEM((C, C), F32),
            pltpu.SemaphoreType.DMA((2, 4)),
        ],
        compiler_params=pltpu.CompilerParams(vmem_limit_bytes=60 * 1024 * 1024),
        cost_estimate=pl.CostEstimate(flops=0, bytes_accessed=4_000_000, transcendentals=0),
    )(*results)


def solution(mesh):
    in_specs = (
        P(("row", "col"), None),
        P(("row", "col")),
        P(("row", "col")),
        P(),
        P(),
        P(("row", "col"), None),
    )
    out_specs = (P(("row", "col"), None), P(("row", "col"), None), P(), P())
    return jax.shard_map(
        on_device, mesh=mesh, in_specs=in_specs, out_specs=out_specs, check_vma=False
    )
```

```python
import functools

import jax
import jax.numpy as jnp
from jax import lax
from jax.experimental import pallas as pl
from jax.experimental.pallas import tpu as pltpu
from jax.sharding import PartitionSpec as P

HEADS = 16
HEAD_DIM = 16
PATCH = 1024
C = 256
QB = 512
CHUNK = 32
CHUNKS = PATCH // CHUNK
STRIP = 256
EXP_SCALE = 0.25 * 1.4426950408889634

F32 = jnp.float32
BF16 = jnp.bfloat16


def dot(a, b):
    return jnp.dot(a, b, preferred_element_type=F32)


def dot_nt(a, b):
    return lax.dot_general(a, b, (((1,), (1,)), ((), ())), preferred_element_type=F32)


def normalize(x):
    centered = x - jnp.mean(x, axis=1, keepdims=True)
    rstd = lax.rsqrt(jnp.mean(centered * centered, axis=1, keepdims=True) + 1e-05)
    return centered * rstd, rstd


def transposed(a):
    return a.astype(F32).T.astype(BF16)


MESH = pl.DeviceIdType.MESH
N_ROW = 8
N_COL = 16
DEVICES = N_ROW * N_COL
CHIPS = DEVICES // 2
CAP = PATCH // DEVICES
LANES = 128


STRIDE = 13
INVERSE_STRIDE = 5
PARTS = 4
PART_CHIPS = CHIPS // PARTS
PART_ROWS = PATCH // PARTS


def as_column(row):
    return jnp.broadcast_to(row, (LANES, PATCH)).T


def slots(key_row):
    key_col = as_column(key_row)
    ranks = []
    for block in range(PATCH // LANES):
        keys = key_row[:, block * LANES : (block + 1) * LANES]
        below = jnp.where(key_col < keys, 1.0, 0.0)
        ranks.append(jnp.sum(below, axis=0, keepdims=True))
    return jnp.concatenate(ranks, axis=1)


def scatter_rows(slot_row, part):
    row = lax.broadcasted_iota(jnp.int32, (PART_ROWS, PATCH), 0) + part * PART_ROWS
    return jnp.where(slot_row == row.astype(F32), 1.0, 0.0).astype(BF16)


def gather_columns(slot_col, part):
    lane = lax.broadcasted_iota(jnp.int32, (PATCH, LANES), 1) + part * PART_ROWS
    blocks = [
        jnp.where(slot_col == (lane + low).astype(F32), 1.0, 0.0).astype(BF16)
        for low in range(0, PART_ROWS, LANES)
    ]
    return jnp.concatenate(blocks, axis=1)


def chip_and_core(point):
    device = point // PATCH
    row, col = device // N_COL, device % N_COL
    return (row // 2) * N_COL + col, row % 2


def relative_slot(offset, core):
    return ((offset + CHIPS) * INVERSE_STRIDE % CHIPS) * 2 + core


def send_slots(zorder_ref):
    point = zorder_ref[...]
    chip, core = chip_and_core(point)
    slot = relative_slot(chip - position()[1], core)
    return slots((slot * PATCH + point % PATCH).astype(F32))


def recv_slots(hilbert_ref):
    chip, core = chip_and_core(hilbert_ref[...])
    slot = relative_slot(position()[1] - chip, core)
    local = lax.broadcasted_iota(jnp.int32, (1, PATCH), 1)
    return slots((slot * PATCH + local).astype(F32))


def packed(rows):
    rows = rows.reshape(2 * PART_CHIPS, CAP, C)
    pieces = jnp.concatenate([rows[:, :, :LANES], rows[:, :, LANES:]], axis=1).astype(BF16)
    return pieces.reshape(PART_CHIPS, 2, 2 * CAP, LANES)


def unpacked(pieces):
    pieces = pieces.reshape(2 * PART_CHIPS, 2 * CAP, LANES).astype(F32)
    left = pieces[:, :CAP].reshape(PART_ROWS, LANES)
    right = pieces[:, CAP:].reshape(PART_ROWS, LANES)
    return jnp.concatenate([left, right], axis=1).astype(BF16)


def part_chips(part):
    return slice(part * PART_CHIPS, (part + 1) * PART_CHIPS)


def position():
    row, col = lax.axis_index("row"), lax.axis_index("col")
    core = lax.rem(row, 2)
    return core, (row // 2) * N_COL + col, (row + 1 - 2 * core, col)


def chip_device(chip):
    core, _, _ = position()
    return (chip // N_COL) * 2 + core, lax.rem(chip, N_COL)


def for_chips(act):
    _, chip, _ = position()

    def body(step, _):
        other = lax.rem(chip + step * STRIDE, CHIPS)
        act(other, chip_device(other))
        return 0

    lax.fori_loop(1, CHIPS, body, 0)


def greet(barrier):
    _, _, sibling = position()
    pl.semaphore_signal(barrier, inc=1, device_id=sibling, device_id_type=MESH)
    for_chips(
        lambda _, device: pl.semaphore_signal(
            barrier, inc=1, device_id=device, device_id_type=MESH
        )
    )


def pair_copy(out_ref, both_ref, part, sems):
    core, _, sibling = position()
    return pltpu.make_async_remote_copy(
        src_ref=out_ref.at[part_chips(part), 1 - core],
        dst_ref=both_ref.at[part_chips(part), core],
        send_sem=sems.at[0, part],
        recv_sem=sems.at[1, part],
        device_id=sibling,
        device_id_type=MESH,
    )


def start_part(rows, out_ref, both_ref, part, sems):
    core, _, _ = position()
    out_ref[part_chips(part)] = packed(rows)
    pair_copy(out_ref, both_ref, part, sems).start()
    both_ref[part_chips(part), core] = out_ref[part_chips(part), core]


def send_part(out_ref, both_ref, in_ref, part, stride, sems):
    _, chip, _ = position()
    pair_copy(out_ref, both_ref, part, sems).wait()

    def body(step, _):
        pltpu.make_async_remote_copy(
            src_ref=both_ref.at[step],
            dst_ref=in_ref.at[step],
            send_sem=sems.at[2, part],
            recv_sem=sems.at[3, part],
            device_id=chip_device(lax.rem(chip + step * stride, CHIPS)),
            device_id_type=MESH,
        ).start()
        return 0

    lax.fori_loop(max(part * PART_CHIPS, 1), (part + 1) * PART_CHIPS, body, 0)
    if part == 0:
        in_ref[0] = both_ref[0]


def wait_part(in_ref, part, sem):
    wait_bytes(in_ref, PART_CHIPS - (part == 0), sem)


def wait_bytes(ref, count, sem):
    view = ref.at[pl.ds(0, count)]
    pltpu.make_async_copy(view, view, sem).wait()


GROUPS = 2
SIDE = 8
GROUP_HEADS = HEADS // GROUPS
GROUP_ROWS = C // GROUPS


def tiles(section):
    section = section.reshape(GROUP_ROWS // 8, 8, C)
    halves = [section[:, None, :, :LANES], section[:, None, :, LANES:]]
    return jnp.concatenate(halves, axis=1).reshape(CHIPS // 2, 8, LANES)


def untiled(pieces):
    pieces = pieces.reshape(GROUP_ROWS // 8, 2, 8, LANES)
    return jnp.concatenate([pieces[:, 0], pieces[:, 1]], axis=2).reshape(GROUP_ROWS, C)


def block_kernel(
    feat_hbm, zorder_hbm, hilbert_hbm, wqkv_hbm, wp_hbm, og_hbm,
    out_hbm, feat_grad_hbm, qkvg_hbm, projg_hbm,
    out_ref, feat_grad_ref, qkvg_ref, projg_ref,
    feat_ref, zorder_ref, hilbert_ref, wqkv_ref, wp_ref, og_ref, oga_ref, x_ref, normed_ref,
    wqkv_t_ref, xhat_ref, rstd_ref, k_ref, v_ref, qt_ref, kt_ref, vt_ref, dot_ref,
    p_ref, ds_ref, e_ref, at_ref, dqt_ref, dkt_ref, dvt_ref,
    there_out, there_both, there_in, back_out, back_both, back_in,
    part_ref, half_ref, sum_ref, chunk_in_ref, result_ref, total_ref, low_out_ref, low_in_ref,
    load_sems, there_sems, back_sems, group_sems, level_sems, store_sems,
):
    half_width = C // 2
    core, chip, sibling = position()
    barrier = pltpu.get_barrier_semaphore()
    sources = (zorder_hbm, feat_hbm, hilbert_hbm, og_hbm, wp_hbm, wqkv_hbm)
    targets = (zorder_ref, feat_ref, hilbert_ref, og_ref, wp_ref, wqkv_ref)
    loads = [
        pltpu.make_async_copy(source, target, load_sems.at[i])
        for i, (source, target) in enumerate(zip(sources, targets))
    ]
    stores = [
        pltpu.make_async_copy(source, target, store_sems.at[i])
        for i, (source, target) in enumerate((
            (out_ref, out_hbm),
            (feat_grad_ref, feat_grad_hbm),
            (qkvg_ref, qkvg_hbm),
            (projg_ref, projg_hbm),
        ))
    ]
    for load in loads:
        load.start()
    greet(barrier)
    loads[0].wait()
    there_slots = send_slots(zorder_ref)
    loads[1].wait()
    for part in range(PARTS):
        rows = dot(scatter_rows(there_slots, part), feat_ref[...])
        if part == 0:
            pl.semaphore_wait(barrier, CHIPS)
        start_part(rows, there_out, there_both, part, there_sems)
        if part:
            send_part(there_out, there_both, there_in, part - 1, STRIDE, there_sems)
    send_part(there_out, there_both, there_in, PARTS - 1, STRIDE, there_sems)

    for load in loads[2:]:
        load.wait()
    back_slots = recv_slots(hilbert_ref)
    for part in range(PARTS):
        rows = slice(part * PART_ROWS, (part + 1) * PART_ROWS)
        oga_ref[rows] = dot(scatter_rows(back_slots, part), og_ref[...]).astype(BF16)
    do_t = dot_nt(wp_ref[...], oga_ref[...]).astype(BF16).astype(F32)
    dot_ref[...] = (do_t * 0.25).astype(BF16).reshape(HEADS, HEAD_DIM, PATCH)
    wqkv_t_ref[...] = transposed(wqkv_ref[...])
    p_ref[1] = jnp.zeros((PATCH, QB), BF16)
    ds_ref[1] = jnp.zeros((PATCH, QB), BF16)
    dkt_ref[0] = jnp.zeros((HEAD_DIM, PATCH), F32)
    dvt_ref[0] = jnp.zeros((HEAD_DIM, PATCH), F32)

    for part in range(PARTS):
        wait_part(there_in, part, there_sems.at[3, part])
        rows = slice(part * PART_ROWS, (part + 1) * PART_ROWS)
        x = unpacked(there_in[part_chips(part)])
        x_ref[rows] = x
        xhat, rstd = normalize(x.astype(F32))
        xhat_ref[rows] = xhat
        rstd_ref[rows] = rstd
        normed = xhat.astype(BF16)
        normed_ref[rows] = normed
        kv = dot(normed, wqkv_ref[:, C:]).astype(BF16)
        for ref, low in ((k_ref, 0), (v_ref, C)):
            ref[0, rows] = kv[:, low : low + half_width]
            ref[1, rows] = kv[:, low + half_width : low + C]
        qkv_t = dot(wqkv_t_ref[...], transposed(normed)).astype(BF16)
        for ref, low in ((qt_ref, 0), (kt_ref, C), (vt_ref, 2 * C)):
            ref[:, :, rows] = qkv_t[low : low + C].reshape(HEADS, HEAD_DIM, PART_ROWS)

    def group_part(g):
        heads = slice(g * GROUP_HEADS, (g + 1) * GROUP_HEADS)
        for section, ref in enumerate((dqt_ref, dkt_ref, dvt_ref, at_ref)):
            rows = ref[heads].reshape(GROUP_ROWS, PATCH).astype(BF16)
            other = oga_ref if section == 3 else normed_ref
            low = section % 2 * (CHIPS // 2)
            part_ref[g, section // 2, low : low + CHIPS // 2] = tiles(dot(rows, other[...]))

    def group_half(g):
        return pltpu.make_async_remote_copy(
            src_ref=part_ref.at[g, 1 - core],
            dst_ref=half_ref.at[g],
            send_sem=group_sems.at[g, 0],
            recv_sem=group_sems.at[g, 1],
            device_id=sibling,
            device_id_type=MESH,
        )

    def group_scatter(g):
        group_half(g).wait()
        sum_ref[g] = part_ref[g, core] + half_ref[g]
        for_chips(
            lambda other, device: pltpu.make_async_remote_copy(
                src_ref=sum_ref.at[g, other],
                dst_ref=chunk_in_ref.at[g, chip],
                send_sem=group_sems.at[g, 2],
                recv_sem=group_sems.at[g, 3],
                device_id=device,
                device_id_type=MESH,
            ).start()
        )
        chunk_in_ref[g, chip] = sum_ref[g, chip]

    def group_gather(g):
        wait_bytes(chunk_in_ref.at[g], CHIPS - 1, group_sems.at[g, 3])
        result_ref[g] = jnp.sum(chunk_in_ref[g], axis=0)
        for_chips(
            lambda other, device: pltpu.make_async_remote_copy(
                src_ref=result_ref.at[g],
                dst_ref=total_ref.at[g, core, chip],
                send_sem=group_sems.at[g, 4],
                recv_sem=group_sems.at[g, 5],
                device_id=device,
                device_id_type=MESH,
            ).start()
        )
        total_ref[g, core, chip] = result_ref[g]

    def group_final(g):
        return pltpu.make_async_remote_copy(
            src_ref=total_ref.at[g, core],
            dst_ref=total_ref.at[g, core],
            send_sem=group_sems.at[g, 6],
            recv_sem=group_sems.at[g, 7],
            device_id=sibling,
            device_id_type=MESH,
        )

    def group_finish(g):
        wait_bytes(total_ref.at[g, core], CHIPS - 1, group_sems.at[g, 5])
        group_final(g).start()

    high, low = chip // SIDE, lax.rem(chip, SIDE)

    def level_copy(src, dst, to, sem):
        return pltpu.make_async_remote_copy(
            src_ref=src,
            dst_ref=dst,
            send_sem=level_sems.at[0, sem],
            recv_sem=level_sems.at[1, sem],
            device_id=chip_device(to),
            device_id_type=MESH,
        )

    def others(mine, act):
        def body(step, _):
            act(lax.rem(mine + step, SIDE))
            return 0

        lax.fori_loop(1, SIDE, body, 0)

    def level_wait(direction, sem, rows):
        view = sum_ref.at[0, pl.ds(0, (SIDE - 1) * rows)]
        pltpu.make_async_copy(view, view, level_sems.at[direction, sem]).wait()

    def run(index):
        return pl.ds(index * SIDE, SIDE)

    def scatter_high():
        group_half(0).wait()
        sum_ref[0] = part_ref[0, core] + half_ref[0]
        others(high, lambda to: level_copy(
            sum_ref.at[0, run(to)], chunk_in_ref.at[0, run(high)], to * SIDE + low, 0
        ).start())
        chunk_in_ref[0, run(high)] = sum_ref[0, run(high)]

    def scatter_low():
        level_wait(1, 0, SIDE)
        summed = chunk_in_ref[0].reshape(SIDE, SIDE, 8, LANES)
        low_out_ref[...] = jnp.sum(summed, axis=0)
        others(low, lambda to: level_copy(
            low_out_ref.at[to], low_in_ref.at[low], high * SIDE + to, 1
        ).start())
        low_in_ref[low] = low_out_ref[low]

    def gather_low():
        level_wait(1, 1, 1)
        result_ref[0] = jnp.sum(low_in_ref[...], axis=0)
        others(low, lambda to: level_copy(
            result_ref.at[0], total_ref.at[0, core, chip], high * SIDE + to, 2
        ).start())
        total_ref[0, core, chip] = result_ref[0]

    def gather_high():
        level_wait(1, 2, 1)
        others(high, lambda to: level_copy(
            total_ref.at[0, core, run(high)], total_ref.at[0, core, run(high)], to * SIDE + low, 3
        ).start())

    def gather_done():
        level_wait(1, 3, SIDE)
        group_final(0).start()

    def group_close(g):
        group_final(g).wait()
        if g == 0:
            for sem, rows in enumerate((SIDE, 1, 1, SIDE)):
                level_wait(0, sem, rows)
        else:
            wait_bytes(sum_ref.at[g], CHIPS - 1, group_sems.at[g, 2])
            wait_bytes(sum_ref.at[g], CHIPS - 1, group_sems.at[g, 4])
        rows = slice(g * GROUP_ROWS, (g + 1) * GROUP_ROWS)
        for section in range(4):
            low = section % 2 * (CHIPS // 2)
            sums = untiled(total_ref[g, section // 2, low : low + CHIPS // 2])
            if section == 3:
                projg_ref[rows, :] = sums
            else:
                low = section * C + g * GROUP_ROWS
                qkvg_ref[:, low : low + GROUP_ROWS] = sums.T

    def query_side(h, block):
        ql = slice(block * QB, (block + 1) * QB)
        dqt_ref[h, :, ql] = dot(kt_ref[h], ds_ref[block]).astype(BF16)

    def value_side(h, block):
        ql = slice(block * QB, (block + 1) * QB)
        dv = dot_nt(dot_ref[h, :, ql], p_ref[block]) * 4.0
        dvt_ref[h] = dvt_ref[h] + dv if block else dv

    def key_side(h, block):
        ql = slice(block * QB, (block + 1) * QB)
        dk = dot_nt(qt_ref[h, :, ql], ds_ref[block])
        dkt_ref[h] = dkt_ref[h] + dk if block else dk

    def block_step(h, block, km, vm, before):
        half = h // 8
        ql = slice(block * QB, (block + 1) * QB)
        qt = qt_ref[pl.ds(half * 8, 8), :, ql].reshape(half_width, QB)
        dot_t = dot_ref[pl.ds(half * 8, 8), :, ql].reshape(half_width, QB)
        tops, sums = [], []
        for j in range(PATCH // STRIP):
            s = dot(km[j * STRIP : (j + 1) * STRIP], qt)
            if j == 0:
                query_side(before, 1 - block)
            for c in range(STRIP // CHUNK):
                part = s[c * CHUNK : (c + 1) * CHUNK].reshape(CHUNK // 8, 8, QB)
                top = jnp.max(part, axis=0)
                e = jnp.exp2((part - top) * EXP_SCALE)
                e_ref[block, j * (STRIP // CHUNK) + c] = e
                tops.append(top)
                sums.append(jnp.sum(e, axis=0))
        value_side(before, 1 - block)
        peak = functools.reduce(jnp.maximum, tops)
        peak = jnp.max(peak, axis=0, keepdims=True)
        weights = [jnp.exp2((top - peak) * EXP_SCALE) for top in tops]
        total = functools.reduce(jnp.add, [a * w for a, w in zip(sums, weights)])
        inverse = 1.0 / jnp.sum(total, axis=0, keepdims=True)
        for c in range(CHUNKS):
            p = e_ref[block, c] * (weights[c] * inverse)
            p_ref[block, c * CHUNK : (c + 1) * CHUNK] = p.reshape(CHUNK, QB).astype(BF16)
        ot = dot(vt_ref[h], p_ref[block])
        key_side(before, 1 - block)
        at_ref[h, :, ql] = ot.astype(BF16)
        delta = jnp.sum(ot * dot_ref[h, :, ql].astype(F32), axis=0, keepdims=True)
        for j in range(PATCH // STRIP):
            dp = dot(vm[j * STRIP : (j + 1) * STRIP], dot_t)
            for c in range(STRIP // CHUNK):
                rows = slice(j * STRIP + c * CHUNK, j * STRIP + (c + 1) * CHUNK)
                p = p_ref[block, rows].astype(F32)
                ds = p * (dp[c * CHUNK : (c + 1) * CHUNK] - delta)
                ds_ref[block, rows] = ds.astype(BF16)

    def head_step(h, _):
        half = h // 8
        lane = lax.broadcasted_iota(jnp.int32, (1, half_width), 1) // HEAD_DIM
        mask = (lane == h % 8).astype(F32).astype(BF16)
        km = k_ref[half] * mask
        vm = v_ref[half] * mask
        block_step(h, 0, km, vm, jnp.maximum(h - 1, 0))
        block_step(h, 1, km, vm, h)

        @pl.when(h == GROUP_HEADS)
        def _():
            group_part(0)
            group_half(0).start()

        for step, act in enumerate(
            (scatter_high, scatter_low, gather_low, gather_high, gather_done), 1
        ):
            pl.when(h == GROUP_HEADS + step)(act)

        return 0

    lax.fori_loop(0, HEADS, head_step, 0)
    query_side(HEADS - 1, 1)
    value_side(HEADS - 1, 1)
    key_side(HEADS - 1, 1)

    group_part(1)
    group_half(1).start()
    cot_t = [ref[...].reshape(C, PATCH).astype(BF16) for ref in (dqt_ref, dkt_ref, dvt_ref)]
    ng_t = dot(wqkv_ref[...], jnp.concatenate(cot_t, axis=0))
    for part in range(PARTS):
        rows = slice(part * PART_ROWS, (part + 1) * PART_ROWS)
        ng = ng_t[:, rows].T
        xhat = xhat_ref[rows]
        ng_mean = jnp.mean(ng, axis=1, keepdims=True)
        mixed = jnp.mean(ng * xhat, axis=1, keepdims=True)
        grad = oga_ref[rows].astype(F32) + rstd_ref[rows] * (ng - ng_mean - xhat * mixed)
        start_part(grad, back_out, back_both, part, back_sems)
        if part == 1:
            group_scatter(1)
        if part:
            send_part(back_out, back_both, back_in, part - 1, CHIPS - STRIDE, back_sems)
    send_part(back_out, back_both, back_in, PARTS - 1, CHIPS - STRIDE, back_sems)

    at = at_ref[...].reshape(C, PATCH)
    block_out = x_ref[...].astype(F32) + dot(transposed(at), wp_ref[...])
    block_out = block_out.astype(BF16)
    slot_col = as_column(recv_slots(hilbert_ref))
    gather = [gather_columns(slot_col, part) for part in range(PARTS)]
    out_ref[...] = dot(jnp.concatenate(gather, axis=1), block_out).astype(BF16)
    stores[0].start()
    group_close(0)
    group_gather(1)
    slot_col = as_column(send_slots(zorder_ref))
    total = jnp.zeros((PATCH, C), F32)
    for part in range(PARTS):
        gather = gather_columns(slot_col, part)
        wait_part(back_in, part, back_sems.at[3, part])
        total += dot(gather, unpacked(back_in[part_chips(part)]))
    feat_grad_ref[...] = total.astype(BF16)
    stores[1].start()
    group_finish(1)
    for part in range(PARTS):
        wait_part(there_in, part, there_sems.at[2, part])
        wait_part(back_in, part, back_sems.at[2, part])
    group_close(1)
    stores[2].start()
    stores[3].start()
    for store in stores:
        store.wait()


def finish_kernel(*refs):
    sources, targets, rooms, sems = refs[:4], refs[4:8], refs[8:12], refs[12]
    ins = [
        pltpu.make_async_copy(source, room, sems.at[0, i])
        for i, (source, room) in enumerate(zip(sources, rooms))
    ]
    outs = [
        pltpu.make_async_copy(room, target, sems.at[1, i])
        for i, (room, target) in enumerate(zip(rooms, targets))
    ]
    for copy in ins:
        copy.start()
    for copy_in, copy_out in zip(ins, outs):
        copy_in.wait()
        copy_out.start()
    for copy in outs:
        copy.wait()


def on_device(features, zorder_to, hilbert_from, qkv_weight, proj_weight, out_grad):
    anywhere = pl.BlockSpec(memory_space=pl.ANY)
    out_shape = (
        jax.ShapeDtypeStruct((PATCH, C), BF16),
        jax.ShapeDtypeStruct((PATCH, C), BF16),
        jax.ShapeDtypeStruct((C, 3 * C), F32),
        jax.ShapeDtypeStruct((C, C), F32),
    )
    points = pltpu.VMEM((PATCH, C), BF16)
    index = pltpu.VMEM((1, PATCH), jnp.int32)
    halves = pltpu.VMEM((2, PATCH, C // 2), BF16)
    heads_t = pltpu.VMEM((HEADS, HEAD_DIM, PATCH), BF16)
    heads_f = pltpu.VMEM((HEADS, HEAD_DIM, PATCH), F32)
    queries = pltpu.VMEM((2, PATCH, QB), BF16)
    pieces = pltpu.VMEM((CHIPS, 2, 2 * CAP, LANES), BF16)
    both_cores = pltpu.VMEM((GROUPS, 2, CHIPS, 8, LANES), F32)
    one_core = pltpu.VMEM((GROUPS, CHIPS, 8, LANES), F32)
    results = pl.pallas_call(
        block_kernel,
        out_shape=out_shape,
        in_specs=[anywhere] * 6,
        out_specs=(anywhere,) * 4,
        scratch_shapes=[
            points, points,
            pltpu.VMEM((C, 3 * C), F32),
            pltpu.VMEM((C, C), F32),
            points, index, index,
            pltpu.VMEM((C, 3 * C), BF16),
            pltpu.VMEM((C, C), BF16),
            points, points, points, points,
            pltpu.VMEM((3 * C, C), BF16),
            pltpu.VMEM((PATCH, C), F32),
            pltpu.VMEM((PATCH, 1), F32),
            halves, halves, heads_t, heads_t, heads_t, heads_t,
            queries, queries,
            pltpu.VMEM((2, CHUNKS, CHUNK // 8, 8, QB), F32),
            heads_t, heads_t, heads_f, heads_f,
            pieces, pieces, pieces, pieces, pieces, pieces,
            both_cores, one_core, one_core, one_core,
            pltpu.VMEM((GROUPS, 8, LANES), F32),
            both_cores,
            pltpu.VMEM((SIDE, 8, LANES), F32),
            pltpu.VMEM((SIDE, 8, LANES), F32),
            pltpu.SemaphoreType.DMA((6,)),
            pltpu.SemaphoreType.DMA((4, PARTS)),
            pltpu.SemaphoreType.DMA((4, PARTS)),
            pltpu.SemaphoreType.DMA((GROUPS, 8)),
            pltpu.SemaphoreType.DMA((2, 4)),
            pltpu.SemaphoreType.DMA((4,)),
        ],
        compiler_params=pltpu.CompilerParams(
            collective_id=0, has_side_effects=True, vmem_limit_bytes=60 * 1024 * 1024
        ),
        cost_estimate=pl.CostEstimate(
            flops=28_000_000_000, bytes_accessed=5_000_000, transcendentals=16_777_216
        ),
    )(
        features,
        zorder_to.reshape(1, PATCH),
        hilbert_from.reshape(1, PATCH),
        qkv_weight,
        proj_weight,
        out_grad,
    )
    return pl.pallas_call(
        finish_kernel,
        out_shape=out_shape,
        in_specs=[anywhere] * 4,
        out_specs=(anywhere,) * 4,
        scratch_shapes=[
            points, points,
            pltpu.VMEM((C, 3 * C), F32),
            pltpu.VMEM((C, C), F32),
            pltpu.SemaphoreType.DMA((2, 4)),
        ],
        compiler_params=pltpu.CompilerParams(vmem_limit_bytes=60 * 1024 * 1024),
        cost_estimate=pl.CostEstimate(flops=0, bytes_accessed=4_000_000, transcendentals=0),
    )(*results)


def solution(mesh):
    in_specs = (
        P(("row", "col"), None),
        P(("row", "col")),
        P(("row", "col")),
        P(),
        P(),
        P(("row", "col"), None),
    )
    out_specs = (P(("row", "col"), None), P(("row", "col"), None), P(), P())
    return jax.shard_map(
        on_device, mesh=mesh, in_specs=in_specs, out_specs=out_specs, check_vma=False
    )
```

```python
import functools

import jax
import jax.numpy as jnp
from jax import lax
from jax.experimental import pallas as pl
from jax.experimental.pallas import tpu as pltpu
from jax.sharding import PartitionSpec as P

HEADS = 16
HEAD_DIM = 16
PATCH = 1024
C = 256
QB = 512
CHUNK = 64
CHUNKS = PATCH // CHUNK
STRIP = 256
EXP_SCALE = 0.25 * 1.4426950408889634

F32 = jnp.float32
BF16 = jnp.bfloat16


def dot(a, b):
    return jnp.dot(a, b, preferred_element_type=F32)


def dot_nt(a, b):
    return lax.dot_general(a, b, (((1,), (1,)), ((), ())), preferred_element_type=F32)


def normalize(x):
    centered = x - jnp.mean(x, axis=1, keepdims=True)
    rstd = lax.rsqrt(jnp.mean(centered * centered, axis=1, keepdims=True) + 1e-05)
    return centered * rstd, rstd


def transposed(a):
    return a.astype(F32).T.astype(BF16)


MESH = pl.DeviceIdType.MESH
N_ROW = 8
N_COL = 16
DEVICES = N_ROW * N_COL
CHIPS = DEVICES // 2
CAP = PATCH // DEVICES
LANES = 128


STRIDE = 13
INVERSE_STRIDE = 5
PARTS = 4
PART_CHIPS = CHIPS // PARTS
PART_ROWS = PATCH // PARTS


def as_column(row):
    return jnp.broadcast_to(row, (LANES, PATCH)).T


def slots(key_row):
    key_col = as_column(key_row)
    ranks = []
    for block in range(PATCH // LANES):
        keys = key_row[:, block * LANES : (block + 1) * LANES]
        below = jnp.where(key_col < keys, 1.0, 0.0)
        ranks.append(jnp.sum(below, axis=0, keepdims=True))
    return jnp.concatenate(ranks, axis=1)


def scatter_rows(slot_row, part):
    row = lax.broadcasted_iota(jnp.int32, (PART_ROWS, PATCH), 0) + part * PART_ROWS
    return jnp.where(slot_row == row.astype(F32), 1.0, 0.0).astype(BF16)


def gather_columns(slot_col, part):
    lane = lax.broadcasted_iota(jnp.int32, (PATCH, LANES), 1) + part * PART_ROWS
    blocks = [
        jnp.where(slot_col == (lane + low).astype(F32), 1.0, 0.0).astype(BF16)
        for low in range(0, PART_ROWS, LANES)
    ]
    return jnp.concatenate(blocks, axis=1)


def chip_and_core(point):
    device = point // PATCH
    row, col = device // N_COL, device % N_COL
    return (row // 2) * N_COL + col, row % 2


def relative_slot(offset, core):
    return ((offset + CHIPS) * INVERSE_STRIDE % CHIPS) * 2 + core


def send_slots(zorder_ref):
    point = zorder_ref[...]
    chip, core = chip_and_core(point)
    slot = relative_slot(chip - position()[1], core)
    return slots((slot * PATCH + point % PATCH).astype(F32))


def recv_slots(hilbert_ref):
    chip, core = chip_and_core(hilbert_ref[...])
    slot = relative_slot(position()[1] - chip, core)
    local = lax.broadcasted_iota(jnp.int32, (1, PATCH), 1)
    return slots((slot * PATCH + local).astype(F32))


def packed(rows):
    rows = rows.reshape(2 * PART_CHIPS, CAP, C)
    pieces = jnp.concatenate([rows[:, :, :LANES], rows[:, :, LANES:]], axis=1).astype(BF16)
    return pieces.reshape(PART_CHIPS, 2, 2 * CAP, LANES)


def unpacked(pieces):
    pieces = pieces.reshape(2 * PART_CHIPS, 2 * CAP, LANES).astype(F32)
    left = pieces[:, :CAP].reshape(PART_ROWS, LANES)
    right = pieces[:, CAP:].reshape(PART_ROWS, LANES)
    return jnp.concatenate([left, right], axis=1).astype(BF16)


def part_chips(part):
    return slice(part * PART_CHIPS, (part + 1) * PART_CHIPS)


def position():
    row, col = lax.axis_index("row"), lax.axis_index("col")
    core = lax.rem(row, 2)
    return core, (row // 2) * N_COL + col, (row + 1 - 2 * core, col)


def chip_device(chip):
    core, _, _ = position()
    return (chip // N_COL) * 2 + core, lax.rem(chip, N_COL)


def for_chips(act):
    _, chip, _ = position()

    def body(step, _):
        other = lax.rem(chip + step * STRIDE, CHIPS)
        act(other, chip_device(other))
        return 0

    lax.fori_loop(1, CHIPS, body, 0)


def greet(barrier):
    _, _, sibling = position()
    pl.semaphore_signal(barrier, inc=1, device_id=sibling, device_id_type=MESH)
    for_chips(
        lambda _, device: pl.semaphore_signal(
            barrier, inc=1, device_id=device, device_id_type=MESH
        )
    )


def pair_copy(out_ref, both_ref, part, sems):
    core, _, sibling = position()
    return pltpu.make_async_remote_copy(
        src_ref=out_ref.at[part_chips(part), 1 - core],
        dst_ref=both_ref.at[part_chips(part), core],
        send_sem=sems.at[0, part],
        recv_sem=sems.at[1, part],
        device_id=sibling,
        device_id_type=MESH,
    )


def start_part(rows, out_ref, both_ref, part, sems):
    core, _, _ = position()
    out_ref[part_chips(part)] = packed(rows)
    pair_copy(out_ref, both_ref, part, sems).start()
    both_ref[part_chips(part), core] = out_ref[part_chips(part), core]


def send_part(out_ref, both_ref, in_ref, part, stride, sems):
    _, chip, _ = position()
    pair_copy(out_ref, both_ref, part, sems).wait()

    def body(step, _):
        pltpu.make_async_remote_copy(
            src_ref=both_ref.at[step],
            dst_ref=in_ref.at[step],
            send_sem=sems.at[2, part],
            recv_sem=sems.at[3, part],
            device_id=chip_device(lax.rem(chip + step * stride, CHIPS)),
            device_id_type=MESH,
        ).start()
        return 0

    lax.fori_loop(max(part * PART_CHIPS, 1), (part + 1) * PART_CHIPS, body, 0)
    if part == 0:
        in_ref[0] = both_ref[0]


def wait_part(in_ref, part, sem):
    wait_bytes(in_ref, PART_CHIPS - (part == 0), sem)


def wait_bytes(ref, count, sem):
    view = ref.at[pl.ds(0, count)]
    pltpu.make_async_copy(view, view, sem).wait()


GROUPS = 2
SIDE = 8
GROUP_HEADS = HEADS // GROUPS
GROUP_ROWS = C // GROUPS


def tiles(section):
    section = section.reshape(GROUP_ROWS // 8, 8, C)
    halves = [section[:, None, :, :LANES], section[:, None, :, LANES:]]
    return jnp.concatenate(halves, axis=1).reshape(CHIPS // 2, 8, LANES)


def untiled(pieces):
    pieces = pieces.reshape(GROUP_ROWS // 8, 2, 8, LANES)
    return jnp.concatenate([pieces[:, 0], pieces[:, 1]], axis=2).reshape(GROUP_ROWS, C)


def block_kernel(
    feat_hbm, zorder_hbm, hilbert_hbm, wqkv_hbm, wp_hbm, og_hbm,
    out_hbm, feat_grad_hbm, qkvg_hbm, projg_hbm,
    out_ref, feat_grad_ref, qkvg_ref, projg_ref,
    feat_ref, zorder_ref, hilbert_ref, wqkv_ref, wp_ref, og_ref, oga_ref, x_ref, normed_ref,
    wqkv_t_ref, xhat_ref, rstd_ref, k_ref, v_ref, qt_ref, kt_ref, vt_ref, dot_ref,
    p_ref, ds_ref, e_ref, at_ref, dqt_ref, dkt_ref, dvt_ref,
    there_out, there_both, there_in, back_out, back_both, back_in,
    part_ref, half_ref, sum_ref, chunk_in_ref, result_ref, total_ref, low_out_ref, low_in_ref,
    load_sems, there_sems, back_sems, group_sems, level_sems, store_sems,
):
    half_width = C // 2
    core, chip, sibling = position()
    barrier = pltpu.get_barrier_semaphore()
    sources = (zorder_hbm, feat_hbm, hilbert_hbm, og_hbm, wp_hbm, wqkv_hbm)
    targets = (zorder_ref, feat_ref, hilbert_ref, og_ref, wp_ref, wqkv_ref)
    loads = [
        pltpu.make_async_copy(source, target, load_sems.at[i])
        for i, (source, target) in enumerate(zip(sources, targets))
    ]
    stores = [
        pltpu.make_async_copy(source, target, store_sems.at[i])
        for i, (source, target) in enumerate((
            (out_ref, out_hbm),
            (feat_grad_ref, feat_grad_hbm),
            (qkvg_ref, qkvg_hbm),
            (projg_ref, projg_hbm),
        ))
    ]
    for load in loads:
        load.start()
    greet(barrier)
    loads[0].wait()
    there_slots = send_slots(zorder_ref)
    loads[1].wait()
    for part in range(PARTS):
        rows = dot(scatter_rows(there_slots, part), feat_ref[...])
        if part == 0:
            pl.semaphore_wait(barrier, CHIPS)
        start_part(rows, there_out, there_both, part, there_sems)
        if part:
            send_part(there_out, there_both, there_in, part - 1, STRIDE, there_sems)
    send_part(there_out, there_both, there_in, PARTS - 1, STRIDE, there_sems)

    for load in loads[2:]:
        load.wait()
    back_slots = recv_slots(hilbert_ref)
    for part in range(PARTS):
        rows = slice(part * PART_ROWS, (part + 1) * PART_ROWS)
        oga_ref[rows] = dot(scatter_rows(back_slots, part), og_ref[...]).astype(BF16)
    do_t = dot_nt(wp_ref[...], oga_ref[...]).astype(BF16).astype(F32)
    dot_ref[...] = (do_t * 0.25).astype(BF16).reshape(HEADS, HEAD_DIM, PATCH)
    wqkv_t_ref[...] = transposed(wqkv_ref[...])
    p_ref[1] = jnp.zeros((PATCH, QB), BF16)
    ds_ref[1] = jnp.zeros((PATCH, QB), BF16)
    dkt_ref[0] = jnp.zeros((HEAD_DIM, PATCH), F32)
    dvt_ref[0] = jnp.zeros((HEAD_DIM, PATCH), F32)

    for part in range(PARTS):
        wait_part(there_in, part, there_sems.at[3, part])
        rows = slice(part * PART_ROWS, (part + 1) * PART_ROWS)
        x = unpacked(there_in[part_chips(part)])
        x_ref[rows] = x
        xhat, rstd = normalize(x.astype(F32))
        xhat_ref[rows] = xhat
        rstd_ref[rows] = rstd
        normed = xhat.astype(BF16)
        normed_ref[rows] = normed
        kv = dot(normed, wqkv_ref[:, C:]).astype(BF16)
        for ref, low in ((k_ref, 0), (v_ref, C)):
            ref[0, rows] = kv[:, low : low + half_width]
            ref[1, rows] = kv[:, low + half_width : low + C]
        qkv_t = dot(wqkv_t_ref[...], transposed(normed)).astype(BF16)
        for ref, low in ((qt_ref, 0), (kt_ref, C), (vt_ref, 2 * C)):
            ref[:, :, rows] = qkv_t[low : low + C].reshape(HEADS, HEAD_DIM, PART_ROWS)

    def group_part(g):
        heads = slice(g * GROUP_HEADS, (g + 1) * GROUP_HEADS)

        def rows(ref):
            return ref[heads].reshape(GROUP_ROWS, PATCH).astype(BF16)

        cot = jnp.concatenate([rows(ref) for ref in (dqt_ref, dkt_ref, dvt_ref)], axis=0)
        sums = dot(cot, normed_ref[...])
        sums = [sums[i * GROUP_ROWS : (i + 1) * GROUP_ROWS] for i in range(3)]
        for section, value in enumerate(sums + [dot(rows(at_ref), oga_ref[...])]):
            low = section % 2 * (CHIPS // 2)
            part_ref[g, section // 2, low : low + CHIPS // 2] = tiles(value)

    def group_half(g):
        return pltpu.make_async_remote_copy(
            src_ref=part_ref.at[g, 1 - core],
            dst_ref=half_ref.at[g],
            send_sem=group_sems.at[g, 0],
            recv_sem=group_sems.at[g, 1],
            device_id=sibling,
            device_id_type=MESH,
        )

    def group_scatter(g):
        group_half(g).wait()
        sum_ref[g] = part_ref[g, core] + half_ref[g]
        for_chips(
            lambda other, device: pltpu.make_async_remote_copy(
                src_ref=sum_ref.at[g, other],
                dst_ref=chunk_in_ref.at[g, chip],
                send_sem=group_sems.at[g, 2],
                recv_sem=group_sems.at[g, 3],
                device_id=device,
                device_id_type=MESH,
            ).start()
        )
        chunk_in_ref[g, chip] = sum_ref[g, chip]

    def group_gather(g):
        wait_bytes(chunk_in_ref.at[g], CHIPS - 1, group_sems.at[g, 3])
        result_ref[g] = jnp.sum(chunk_in_ref[g], axis=0)
        for_chips(
            lambda other, device: pltpu.make_async_remote_copy(
                src_ref=result_ref.at[g],
                dst_ref=total_ref.at[g, core, chip],
                send_sem=group_sems.at[g, 4],
                recv_sem=group_sems.at[g, 5],
                device_id=device,
                device_id_type=MESH,
            ).start()
        )
        total_ref[g, core, chip] = result_ref[g]

    def group_final(g):
        return pltpu.make_async_remote_copy(
            src_ref=total_ref.at[g, core],
            dst_ref=total_ref.at[g, core],
            send_sem=group_sems.at[g, 6],
            recv_sem=group_sems.at[g, 7],
            device_id=sibling,
            device_id_type=MESH,
        )

    def group_finish(g):
        wait_bytes(total_ref.at[g, core], CHIPS - 1, group_sems.at[g, 5])
        group_final(g).start()

    high, low = chip // SIDE, lax.rem(chip, SIDE)

    def level_copy(src, dst, to, sem):
        return pltpu.make_async_remote_copy(
            src_ref=src,
            dst_ref=dst,
            send_sem=level_sems.at[0, sem],
            recv_sem=level_sems.at[1, sem],
            device_id=chip_device(to),
            device_id_type=MESH,
        )

    def others(mine, act):
        def body(step, _):
            act(lax.rem(mine + step, SIDE))
            return 0

        lax.fori_loop(1, SIDE, body, 0)

    def level_wait(direction, sem, rows):
        view = sum_ref.at[0, pl.ds(0, (SIDE - 1) * rows)]
        pltpu.make_async_copy(view, view, level_sems.at[direction, sem]).wait()

    def run(index):
        return pl.ds(index * SIDE, SIDE)

    def scatter_high():
        group_half(0).wait()
        sum_ref[0] = part_ref[0, core] + half_ref[0]
        others(high, lambda to: level_copy(
            sum_ref.at[0, run(to)], chunk_in_ref.at[0, run(high)], to * SIDE + low, 0
        ).start())
        chunk_in_ref[0, run(high)] = sum_ref[0, run(high)]

    def scatter_low():
        level_wait(1, 0, SIDE)
        summed = chunk_in_ref[0].reshape(SIDE, SIDE, 8, LANES)
        low_out_ref[...] = jnp.sum(summed, axis=0)
        others(low, lambda to: level_copy(
            low_out_ref.at[to], low_in_ref.at[low], high * SIDE + to, 1
        ).start())
        low_in_ref[low] = low_out_ref[low]

    def gather_low():
        level_wait(1, 1, 1)
        result_ref[0] = jnp.sum(low_in_ref[...], axis=0)
        others(low, lambda to: level_copy(
            result_ref.at[0], total_ref.at[0, core, chip], high * SIDE + to, 2
        ).start())
        total_ref[0, core, chip] = result_ref[0]

    def gather_high():
        level_wait(1, 2, 1)
        others(high, lambda to: level_copy(
            total_ref.at[0, core, run(high)], total_ref.at[0, core, run(high)], to * SIDE + low, 3
        ).start())

    def gather_done():
        level_wait(1, 3, SIDE)
        group_final(0).start()

    def group_close(g):
        group_final(g).wait()
        if g == 0:
            for sem, rows in enumerate((SIDE, 1, 1, SIDE)):
                level_wait(0, sem, rows)
        else:
            wait_bytes(sum_ref.at[g], CHIPS - 1, group_sems.at[g, 2])
            wait_bytes(sum_ref.at[g], CHIPS - 1, group_sems.at[g, 4])
        rows = slice(g * GROUP_ROWS, (g + 1) * GROUP_ROWS)
        for section in range(4):
            low = section % 2 * (CHIPS // 2)
            sums = untiled(total_ref[g, section // 2, low : low + CHIPS // 2])
            if section == 3:
                projg_ref[rows, :] = sums
            else:
                low = section * C + g * GROUP_ROWS
                qkvg_ref[:, low : low + GROUP_ROWS] = sums.T

    def query_side(h, block):
        ql = slice(block * QB, (block + 1) * QB)
        dqt_ref[h, :, ql] = dot(kt_ref[h], ds_ref[block]).astype(BF16)

    def value_side(h, block):
        ql = slice(block * QB, (block + 1) * QB)
        dv = dot_nt(dot_ref[h, :, ql], p_ref[block]) * 4.0
        dvt_ref[h] = dvt_ref[h] + dv if block else dv

    def key_side(h, block):
        ql = slice(block * QB, (block + 1) * QB)
        dk = dot_nt(qt_ref[h, :, ql], ds_ref[block])
        dkt_ref[h] = dkt_ref[h] + dk if block else dk

    def block_step(h, block, km, vm, before):
        half = h // 8
        ql = slice(block * QB, (block + 1) * QB)
        qt = qt_ref[pl.ds(half * 8, 8), :, ql].reshape(half_width, QB)
        dot_t = dot_ref[pl.ds(half * 8, 8), :, ql].reshape(half_width, QB)
        tops, sums = [], []
        for j in range(PATCH // STRIP):
            s = dot(km[j * STRIP : (j + 1) * STRIP], qt)
            if j == 0:
                query_side(before, 1 - block)
            for c in range(STRIP // CHUNK):
                part = s[c * CHUNK : (c + 1) * CHUNK].reshape(CHUNK // 8, 8, QB)
                top = jnp.max(part, axis=0)
                e = jnp.exp2((part - top) * EXP_SCALE)
                e_ref[block, j * (STRIP // CHUNK) + c] = e
                tops.append(top)
                sums.append(jnp.sum(e, axis=0))
        value_side(before, 1 - block)
        peak = functools.reduce(jnp.maximum, tops)
        peak = jnp.max(peak, axis=0, keepdims=True)
        weights = [jnp.exp2((top - peak) * EXP_SCALE) for top in tops]
        total = functools.reduce(jnp.add, [a * w for a, w in zip(sums, weights)])
        inverse = 1.0 / jnp.sum(total, axis=0, keepdims=True)
        for c in range(CHUNKS):
            p = e_ref[block, c] * (weights[c] * inverse)
            p_ref[block, c * CHUNK : (c + 1) * CHUNK] = p.reshape(CHUNK, QB).astype(BF16)
        ot = dot(vt_ref[h], p_ref[block])
        key_side(before, 1 - block)
        at_ref[h, :, ql] = ot.astype(BF16)
        delta = jnp.sum(ot * dot_ref[h, :, ql].astype(F32), axis=0, keepdims=True)
        for j in range(PATCH // STRIP):
            dp = dot(vm[j * STRIP : (j + 1) * STRIP], dot_t)
            for c in range(STRIP // CHUNK):
                rows = slice(j * STRIP + c * CHUNK, j * STRIP + (c + 1) * CHUNK)
                p = p_ref[block, rows].astype(F32)
                ds = p * (dp[c * CHUNK : (c + 1) * CHUNK] - delta)
                ds_ref[block, rows] = ds.astype(BF16)

    def head_step(h, _):
        half = h // 8
        lane = lax.broadcasted_iota(jnp.int32, (1, half_width), 1) // HEAD_DIM
        mask = (lane == h % 8).astype(F32).astype(BF16)
        km = k_ref[half] * mask
        vm = v_ref[half] * mask
        block_step(h, 0, km, vm, jnp.maximum(h - 1, 0))
        block_step(h, 1, km, vm, h)

        @pl.when(h == GROUP_HEADS)
        def _():
            group_part(0)
            group_half(0).start()

        for step, act in enumerate(
            (scatter_high, scatter_low, gather_low, gather_high, gather_done), 1
        ):
            pl.when(h == GROUP_HEADS + step)(act)

        return 0

    lax.fori_loop(0, HEADS, head_step, 0)
    query_side(HEADS - 1, 1)
    value_side(HEADS - 1, 1)
    key_side(HEADS - 1, 1)

    cot_t = [ref[...].reshape(C, PATCH).astype(BF16) for ref in (dqt_ref, dkt_ref, dvt_ref)]
    ng_t = dot(wqkv_ref[...], jnp.concatenate(cot_t, axis=0))
    for part in range(PARTS):
        rows = slice(part * PART_ROWS, (part + 1) * PART_ROWS)
        ng = ng_t[:, rows].T
        xhat = xhat_ref[rows]
        ng_mean = jnp.mean(ng, axis=1, keepdims=True)
        mixed = jnp.mean(ng * xhat, axis=1, keepdims=True)
        grad = oga_ref[rows].astype(F32) + rstd_ref[rows] * (ng - ng_mean - xhat * mixed)
        start_part(grad, back_out, back_both, part, back_sems)
        if part:
            send_part(back_out, back_both, back_in, part - 1, CHIPS - STRIDE, back_sems)
    send_part(back_out, back_both, back_in, PARTS - 1, CHIPS - STRIDE, back_sems)
    group_part(1)
    group_half(1).start()

    at = at_ref[...].reshape(C, PATCH)
    block_out = x_ref[...].astype(F32) + dot(transposed(at), wp_ref[...])
    block_out = block_out.astype(BF16)
    group_scatter(1)
    slot_col = as_column(recv_slots(hilbert_ref))
    gather = [gather_columns(slot_col, part) for part in range(PARTS)]
    out_ref[...] = dot(jnp.concatenate(gather, axis=1), block_out).astype(BF16)
    stores[0].start()
    group_close(0)
    group_gather(1)
    slot_col = as_column(send_slots(zorder_ref))
    total = jnp.zeros((PATCH, C), F32)
    for part in range(PARTS):
        gather = gather_columns(slot_col, part)
        wait_part(back_in, part, back_sems.at[3, part])
        total += dot(gather, unpacked(back_in[part_chips(part)]))
    feat_grad_ref[...] = total.astype(BF16)
    stores[1].start()
    group_finish(1)
    for part in range(PARTS):
        wait_part(there_in, part, there_sems.at[2, part])
        wait_part(back_in, part, back_sems.at[2, part])
    group_close(1)
    stores[2].start()
    stores[3].start()
    for store in stores:
        store.wait()


def finish_kernel(*refs):
    sources, targets, rooms, sems = refs[:4], refs[4:8], refs[8:12], refs[12]
    ins = [
        pltpu.make_async_copy(source, room, sems.at[0, i])
        for i, (source, room) in enumerate(zip(sources, rooms))
    ]
    outs = [
        pltpu.make_async_copy(room, target, sems.at[1, i])
        for i, (room, target) in enumerate(zip(rooms, targets))
    ]
    for copy in ins:
        copy.start()
    for copy_in, copy_out in zip(ins, outs):
        copy_in.wait()
        copy_out.start()
    for copy in outs:
        copy.wait()


def on_device(features, zorder_to, hilbert_from, qkv_weight, proj_weight, out_grad):
    anywhere = pl.BlockSpec(memory_space=pl.ANY)
    out_shape = (
        jax.ShapeDtypeStruct((PATCH, C), BF16),
        jax.ShapeDtypeStruct((PATCH, C), BF16),
        jax.ShapeDtypeStruct((C, 3 * C), F32),
        jax.ShapeDtypeStruct((C, C), F32),
    )
    points = pltpu.VMEM((PATCH, C), BF16)
    index = pltpu.VMEM((1, PATCH), jnp.int32)
    halves = pltpu.VMEM((2, PATCH, C // 2), BF16)
    heads_t = pltpu.VMEM((HEADS, HEAD_DIM, PATCH), BF16)
    heads_f = pltpu.VMEM((HEADS, HEAD_DIM, PATCH), F32)
    queries = pltpu.VMEM((2, PATCH, QB), BF16)
    pieces = pltpu.VMEM((CHIPS, 2, 2 * CAP, LANES), BF16)
    both_cores = pltpu.VMEM((GROUPS, 2, CHIPS, 8, LANES), F32)
    one_core = pltpu.VMEM((GROUPS, CHIPS, 8, LANES), F32)
    results = pl.pallas_call(
        block_kernel,
        out_shape=out_shape,
        in_specs=[anywhere] * 6,
        out_specs=(anywhere,) * 4,
        scratch_shapes=[
            points, points,
            pltpu.VMEM((C, 3 * C), F32),
            pltpu.VMEM((C, C), F32),
            points, index, index,
            pltpu.VMEM((C, 3 * C), BF16),
            pltpu.VMEM((C, C), BF16),
            points, points, points, points,
            pltpu.VMEM((3 * C, C), BF16),
            pltpu.VMEM((PATCH, C), F32),
            pltpu.VMEM((PATCH, 1), F32),
            halves, halves, heads_t, heads_t, heads_t, heads_t,
            queries, queries,
            pltpu.VMEM((2, CHUNKS, CHUNK // 8, 8, QB), F32),
            heads_t, heads_t, heads_f, heads_f,
            pieces, pieces, pieces, pieces, pieces, pieces,
            both_cores, one_core, one_core, one_core,
            pltpu.VMEM((GROUPS, 8, LANES), F32),
            both_cores,
            pltpu.VMEM((SIDE, 8, LANES), F32),
            pltpu.VMEM((SIDE, 8, LANES), F32),
            pltpu.SemaphoreType.DMA((6,)),
            pltpu.SemaphoreType.DMA((4, PARTS)),
            pltpu.SemaphoreType.DMA((4, PARTS)),
            pltpu.SemaphoreType.DMA((GROUPS, 8)),
            pltpu.SemaphoreType.DMA((2, 4)),
            pltpu.SemaphoreType.DMA((4,)),
        ],
        compiler_params=pltpu.CompilerParams(
            collective_id=0, has_side_effects=True, vmem_limit_bytes=60 * 1024 * 1024
        ),
        cost_estimate=pl.CostEstimate(
            flops=28_000_000_000, bytes_accessed=5_000_000, transcendentals=16_777_216
        ),
    )(
        features,
        zorder_to.reshape(1, PATCH),
        hilbert_from.reshape(1, PATCH),
        qkv_weight,
        proj_weight,
        out_grad,
    )
    return pl.pallas_call(
        finish_kernel,
        out_shape=out_shape,
        in_specs=[anywhere] * 4,
        out_specs=(anywhere,) * 4,
        scratch_shapes=[
            points, points,
            pltpu.VMEM((C, 3 * C), F32),
            pltpu.VMEM((C, C), F32),
            pltpu.SemaphoreType.DMA((2, 4)),
        ],
        compiler_params=pltpu.CompilerParams(vmem_limit_bytes=60 * 1024 * 1024),
        cost_estimate=pl.CostEstimate(flops=0, bytes_accessed=4_000_000, transcendentals=0),
    )(*results)


def solution(mesh):
    in_specs = (
        P(("row", "col"), None),
        P(("row", "col")),
        P(("row", "col")),
        P(),
        P(),
        P(("row", "col"), None),
    )
    out_specs = (P(("row", "col"), None), P(("row", "col"), None), P(), P())
    return jax.shard_map(
        on_device, mesh=mesh, in_specs=in_specs, out_specs=out_specs, check_vma=False
    )
```

```python
import functools

import jax
import jax.numpy as jnp
from jax import lax
from jax.experimental import pallas as pl
from jax.experimental.pallas import tpu as pltpu
from jax.sharding import PartitionSpec as P

HEADS = 16
HEAD_DIM = 16
PATCH = 1024
C = 256
QB = 512
CHUNK = 64
CHUNKS = PATCH // CHUNK
STRIP = 256
EXP_SCALE = 0.25 * 1.4426950408889634

F32 = jnp.float32
BF16 = jnp.bfloat16


def dot(a, b):
    return jnp.dot(a, b, preferred_element_type=F32)


def dot_nt(a, b):
    return lax.dot_general(a, b, (((1,), (1,)), ((), ())), preferred_element_type=F32)


def normalize(x):
    centered = x - jnp.mean(x, axis=1, keepdims=True)
    rstd = lax.rsqrt(jnp.mean(centered * centered, axis=1, keepdims=True) + 1e-05)
    return centered * rstd, rstd


def transposed(a):
    return a.astype(F32).T.astype(BF16)


MESH = pl.DeviceIdType.MESH
N_ROW = 8
N_COL = 16
DEVICES = N_ROW * N_COL
CHIPS = DEVICES // 2
CAP = PATCH // DEVICES
LANES = 128


STRIDE = 1
INVERSE_STRIDE = 1
PARTS = 4
PART_CHIPS = CHIPS // PARTS
PART_ROWS = PATCH // PARTS


def as_column(row):
    return jnp.broadcast_to(row, (LANES, PATCH)).T


def slots(key_row):
    key_col = as_column(key_row)
    ranks = []
    for block in range(PATCH // LANES):
        keys = key_row[:, block * LANES : (block + 1) * LANES]
        below = jnp.where(key_col < keys, 1.0, 0.0)
        ranks.append(jnp.sum(below, axis=0, keepdims=True))
    return jnp.concatenate(ranks, axis=1)


def scatter_rows(slot_row, part):
    row = lax.broadcasted_iota(jnp.int32, (PART_ROWS, PATCH), 0) + part * PART_ROWS
    return jnp.where(slot_row == row.astype(F32), 1.0, 0.0).astype(BF16)


def gather_columns(slot_col, part):
    lane = lax.broadcasted_iota(jnp.int32, (PATCH, LANES), 1) + part * PART_ROWS
    blocks = [
        jnp.where(slot_col == (lane + low).astype(F32), 1.0, 0.0).astype(BF16)
        for low in range(0, PART_ROWS, LANES)
    ]
    return jnp.concatenate(blocks, axis=1)


def chip_and_core(point):
    device = point // PATCH
    row, col = device // N_COL, device % N_COL
    return (row // 2) * N_COL + col, row % 2


def relative_slot(offset, core):
    return ((offset + CHIPS) * INVERSE_STRIDE % CHIPS) * 2 + core


def send_slots(zorder_ref):
    point = zorder_ref[...]
    chip, core = chip_and_core(point)
    slot = relative_slot(chip - position()[1], core)
    return slots((slot * PATCH + point % PATCH).astype(F32))


def recv_slots(hilbert_ref):
    chip, core = chip_and_core(hilbert_ref[...])
    slot = relative_slot(position()[1] - chip, core)
    local = lax.broadcasted_iota(jnp.int32, (1, PATCH), 1)
    return slots((slot * PATCH + local).astype(F32))


def packed(rows):
    rows = rows.reshape(2 * PART_CHIPS, CAP, C)
    pieces = jnp.concatenate([rows[:, :, :LANES], rows[:, :, LANES:]], axis=1).astype(BF16)
    return pieces.reshape(PART_CHIPS, 2, 2 * CAP, LANES)


def unpacked(pieces):
    pieces = pieces.reshape(2 * PART_CHIPS, 2 * CAP, LANES).astype(F32)
    left = pieces[:, :CAP].reshape(PART_ROWS, LANES)
    right = pieces[:, CAP:].reshape(PART_ROWS, LANES)
    return jnp.concatenate([left, right], axis=1).astype(BF16)


def part_chips(part):
    return slice(part * PART_CHIPS, (part + 1) * PART_CHIPS)


def position():
    row, col = lax.axis_index("row"), lax.axis_index("col")
    core = lax.rem(row, 2)
    return core, (row // 2) * N_COL + col, (row + 1 - 2 * core, col)


def chip_device(chip):
    core, _, _ = position()
    return (chip // N_COL) * 2 + core, lax.rem(chip, N_COL)


def for_chips(act):
    _, chip, _ = position()

    def body(step, _):
        other = lax.rem(chip + step * STRIDE, CHIPS)
        act(other, chip_device(other))
        return 0

    lax.fori_loop(1, CHIPS, body, 0)


def greet(barrier):
    _, _, sibling = position()
    pl.semaphore_signal(barrier, inc=1, device_id=sibling, device_id_type=MESH)
    for_chips(
        lambda _, device: pl.semaphore_signal(
            barrier, inc=1, device_id=device, device_id_type=MESH
        )
    )


def pair_copy(out_ref, both_ref, part, sems):
    core, _, sibling = position()
    return pltpu.make_async_remote_copy(
        src_ref=out_ref.at[part_chips(part), 1 - core],
        dst_ref=both_ref.at[part_chips(part), core],
        send_sem=sems.at[0, part],
        recv_sem=sems.at[1, part],
        device_id=sibling,
        device_id_type=MESH,
    )


def start_part(rows, out_ref, both_ref, part, sems):
    core, _, _ = position()
    out_ref[part_chips(part)] = packed(rows)
    pair_copy(out_ref, both_ref, part, sems).start()
    both_ref[part_chips(part), core] = out_ref[part_chips(part), core]


def send_part(out_ref, both_ref, in_ref, part, stride, sems):
    _, chip, _ = position()
    pair_copy(out_ref, both_ref, part, sems).wait()

    def body(step, _):
        pltpu.make_async_remote_copy(
            src_ref=both_ref.at[step],
            dst_ref=in_ref.at[step],
            send_sem=sems.at[2, part],
            recv_sem=sems.at[3, part],
            device_id=chip_device(lax.rem(chip + step * stride, CHIPS)),
            device_id_type=MESH,
        ).start()
        return 0

    lax.fori_loop(max(part * PART_CHIPS, 1), (part + 1) * PART_CHIPS, body, 0)
    if part == 0:
        in_ref[0] = both_ref[0]


def wait_part(in_ref, part, sem):
    wait_bytes(in_ref, PART_CHIPS - (part == 0), sem)


def wait_bytes(ref, count, sem):
    view = ref.at[pl.ds(0, count)]
    pltpu.make_async_copy(view, view, sem).wait()


SIDE = 8
GROUPS = 3
FIRST_HEAD = (0, 8, 13, HEADS)
OWNER_STRIDE = 13
OWNER_INVERSE = 5


def group_heads(g):
    return FIRST_HEAD[g + 1] - FIRST_HEAD[g]


def group_tiles(g):
    return 8 * group_heads(g)


def tiles(section):
    rows = section.shape[0]
    section = section.reshape(rows // 8, 8, C)
    halves = [section[:, None, :, :LANES], section[:, None, :, LANES:]]
    return jnp.concatenate(halves, axis=1).reshape(rows // 4, 8, LANES)


def untiled(pieces):
    pieces = pieces.reshape(-1, 2, 8, LANES)
    return jnp.concatenate([pieces[:, 0], pieces[:, 1]], axis=2).reshape(-1, C)


def block_kernel(
    feat_hbm, zorder_hbm, hilbert_hbm, wqkv_hbm, wp_hbm, og_hbm,
    out_hbm, feat_grad_hbm, qkvg_hbm, projg_hbm,
    out_ref, feat_grad_ref, qkvg_ref, projg_ref,
    feat_ref, zorder_ref, hilbert_ref, wqkv_ref, wp_ref, og_ref, oga_ref, x_ref, normed_ref,
    wqkv_t_ref, xhat_ref, rstd_ref, k_ref, v_ref, qt_ref, kt_ref, vt_ref, dot_ref,
    p_ref, ds_ref, e_ref, at_ref, dqt_ref, dkt_ref, dvt_ref,
    there_out, there_both, there_in, back_out, back_both, back_in,
    part_ref, half_ref, sum_ref, chunk_in_ref, result_ref, total_ref, low_out_ref, low_in_ref,
    load_sems, there_sems, back_sems, group_sems, level_sems, store_sems,
):
    half_width = C // 2
    core, chip, sibling = position()
    barrier = pltpu.get_barrier_semaphore()
    sources = (zorder_hbm, feat_hbm, hilbert_hbm, og_hbm, wp_hbm, wqkv_hbm)
    targets = (zorder_ref, feat_ref, hilbert_ref, og_ref, wp_ref, wqkv_ref)
    loads = [
        pltpu.make_async_copy(source, target, load_sems.at[i])
        for i, (source, target) in enumerate(zip(sources, targets))
    ]
    stores = [
        pltpu.make_async_copy(source, target, store_sems.at[i])
        for i, (source, target) in enumerate((
            (out_ref, out_hbm),
            (feat_grad_ref, feat_grad_hbm),
            (qkvg_ref, qkvg_hbm),
            (projg_ref, projg_hbm),
        ))
    ]
    for load in loads:
        load.start()
    greet(barrier)
    loads[0].wait()
    there_slots = send_slots(zorder_ref)
    loads[1].wait()
    for part in range(PARTS):
        rows = dot(scatter_rows(there_slots, part), feat_ref[...])
        if part == 0:
            pl.semaphore_wait(barrier, CHIPS)
        start_part(rows, there_out, there_both, part, there_sems)
        if part:
            send_part(there_out, there_both, there_in, part - 1, STRIDE, there_sems)
    send_part(there_out, there_both, there_in, PARTS - 1, STRIDE, there_sems)

    for load in loads[2:]:
        load.wait()
    back_slots = recv_slots(hilbert_ref)
    for part in range(PARTS):
        rows = slice(part * PART_ROWS, (part + 1) * PART_ROWS)
        oga_ref[rows] = dot(scatter_rows(back_slots, part), og_ref[...]).astype(BF16)
    do_t = dot_nt(wp_ref[...], oga_ref[...]).astype(BF16).astype(F32)
    dot_ref[...] = (do_t * 0.25).astype(BF16).reshape(HEADS, HEAD_DIM, PATCH)
    wqkv_t_ref[...] = transposed(wqkv_ref[...])
    p_ref[1] = jnp.zeros((PATCH, QB), BF16)
    ds_ref[1] = jnp.zeros((PATCH, QB), BF16)
    dkt_ref[0] = jnp.zeros((HEAD_DIM, PATCH), F32)
    dvt_ref[0] = jnp.zeros((HEAD_DIM, PATCH), F32)

    for part in range(PARTS):
        wait_part(there_in, part, there_sems.at[3, part])
        rows = slice(part * PART_ROWS, (part + 1) * PART_ROWS)
        x = unpacked(there_in[part_chips(part)])
        x_ref[rows] = x
        xhat, rstd = normalize(x.astype(F32))
        xhat_ref[rows] = xhat
        rstd_ref[rows] = rstd
        normed = xhat.astype(BF16)
        normed_ref[rows] = normed
        kv = dot(normed, wqkv_ref[:, C:]).astype(BF16)
        for ref, low in ((k_ref, 0), (v_ref, C)):
            ref[0, rows] = kv[:, low : low + half_width]
            ref[1, rows] = kv[:, low + half_width : low + C]
        qkv_t = dot(wqkv_t_ref[...], transposed(normed)).astype(BF16)
        for ref, low in ((qt_ref, 0), (kt_ref, C), (vt_ref, 2 * C)):
            ref[:, :, rows] = qkv_t[low : low + C].reshape(HEADS, HEAD_DIM, PART_ROWS)

    def group_part(g):
        heads = slice(FIRST_HEAD[g], FIRST_HEAD[g + 1])
        count = group_heads(g) * HEAD_DIM

        def rows(ref):
            return ref[heads].reshape(count, PATCH).astype(BF16)

        cot = jnp.concatenate([rows(ref) for ref in (dqt_ref, dkt_ref, dvt_ref)], axis=0)
        sums = dot(cot, normed_ref[...])
        sums = [sums[i * count : (i + 1) * count] for i in range(3)]
        half = group_tiles(g) // 2
        for section, value in enumerate(sums + [dot(rows(at_ref), oga_ref[...])]):
            low = section % 2 * half
            part_ref[g, section // 2, low : low + half] = tiles(value)
        group_half(g).start()

    def group_half(g):
        count = pl.ds(0, group_tiles(g))
        return pltpu.make_async_remote_copy(
            src_ref=part_ref.at[g, 1 - core, count],
            dst_ref=half_ref.at[g, count],
            send_sem=group_sems.at[g, 0],
            recv_sem=group_sems.at[g, 1],
            device_id=sibling,
            device_id_type=MESH,
        )

    my_tile = lax.rem(chip * OWNER_INVERSE, CHIPS)

    def by_owner(g, act):
        pl.when(my_tile < group_tiles(g))(lambda: act(True))
        pl.when(my_tile >= group_tiles(g))(lambda: act(False))

    def group_scatter(g):
        group_half(g).wait()
        count = group_tiles(g)
        sum_ref[g, :count] = part_ref[g, core, :count] + half_ref[g, :count]

        def body(tile, _):
            owner = lax.rem(tile * OWNER_STRIDE, CHIPS)

            @pl.when(owner != chip)
            def _():
                pltpu.make_async_remote_copy(
                    src_ref=sum_ref.at[g, tile],
                    dst_ref=chunk_in_ref.at[g, chip],
                    send_sem=group_sems.at[g, 2],
                    recv_sem=group_sems.at[g, 3],
                    device_id=chip_device(owner),
                    device_id_type=MESH,
                ).start()

            return 0

        lax.fori_loop(0, count, body, 0)

        @pl.when(my_tile < count)
        def _():
            chunk_in_ref[g, chip] = sum_ref[g, my_tile]

    def group_gather(g):
        @pl.when(my_tile < group_tiles(g))
        def _():
            wait_bytes(chunk_in_ref.at[g], CHIPS - 1, group_sems.at[g, 3])
            result_ref[g] = jnp.sum(chunk_in_ref[g], axis=0)
            for_chips(
                lambda other, device: pltpu.make_async_remote_copy(
                    src_ref=result_ref.at[g],
                    dst_ref=total_ref.at[g, core, my_tile],
                    send_sem=group_sems.at[g, 4],
                    recv_sem=group_sems.at[g, 5],
                    device_id=device,
                    device_id_type=MESH,
                ).start()
            )
            total_ref[g, core, my_tile] = result_ref[g]

    def group_final(g):
        count = pl.ds(0, group_tiles(g))
        return pltpu.make_async_remote_copy(
            src_ref=total_ref.at[g, core, count],
            dst_ref=total_ref.at[g, core, count],
            send_sem=group_sems.at[g, 6],
            recv_sem=group_sems.at[g, 7],
            device_id=sibling,
            device_id_type=MESH,
        )

    def group_finish(g):
        def arrived(owner):
            wait_bytes(total_ref.at[g, core], group_tiles(g) - owner, group_sems.at[g, 5])

        by_owner(g, arrived)
        group_final(g).start()

    high, low = chip // SIDE, lax.rem(chip, SIDE)

    def level_copy(src, dst, to, sem):
        return pltpu.make_async_remote_copy(
            src_ref=src,
            dst_ref=dst,
            send_sem=level_sems.at[0, sem],
            recv_sem=level_sems.at[1, sem],
            device_id=chip_device(to),
            device_id_type=MESH,
        )

    def others(mine, act):
        def body(step, _):
            act(lax.rem(mine + step, SIDE))
            return 0

        lax.fori_loop(1, SIDE, body, 0)

    def level_wait(direction, sem, rows):
        view = sum_ref.at[0, pl.ds(0, (SIDE - 1) * rows)]
        pltpu.make_async_copy(view, view, level_sems.at[direction, sem]).wait()

    def run(index):
        return pl.ds(index * SIDE, SIDE)

    def scatter_high():
        group_half(0).wait()
        sum_ref[0] = part_ref[0, core] + half_ref[0]
        others(high, lambda to: level_copy(
            sum_ref.at[0, run(to)], chunk_in_ref.at[0, run(high)], to * SIDE + low, 0
        ).start())
        chunk_in_ref[0, run(high)] = sum_ref[0, run(high)]

    def scatter_low():
        level_wait(1, 0, SIDE)
        summed = chunk_in_ref[0].reshape(SIDE, SIDE, 8, LANES)
        low_out_ref[...] = jnp.sum(summed, axis=0)
        others(low, lambda to: level_copy(
            low_out_ref.at[to], low_in_ref.at[low], high * SIDE + to, 1
        ).start())
        low_in_ref[low] = low_out_ref[low]

    def gather_low():
        level_wait(1, 1, 1)
        result_ref[0] = jnp.sum(low_in_ref[...], axis=0)
        others(low, lambda to: level_copy(
            result_ref.at[0], total_ref.at[0, core, chip], high * SIDE + to, 2
        ).start())
        total_ref[0, core, chip] = result_ref[0]

    def gather_high():
        level_wait(1, 2, 1)
        others(high, lambda to: level_copy(
            total_ref.at[0, core, run(high)], total_ref.at[0, core, run(high)], to * SIDE + low, 3
        ).start())

    def gather_done():
        level_wait(1, 3, SIDE)
        group_final(0).start()

    def group_close(g):
        group_final(g).wait()
        if g == 0:
            for sem, rows in enumerate((SIDE, 1, 1, SIDE)):
                level_wait(0, sem, rows)
            return

        def sent(owner):
            wait_bytes(sum_ref.at[g], group_tiles(g) - owner, group_sems.at[g, 2])
            if owner:
                wait_bytes(sum_ref.at[g], CHIPS - 1, group_sems.at[g, 4])

        by_owner(g, sent)

    def assemble(section):
        rows = []
        for g in range(GROUPS):
            half = group_tiles(g) // 2
            low = section % 2 * half
            rows.append(untiled(total_ref[g, section // 2, low : low + half]))
        return jnp.concatenate(rows, axis=0)

    def query_side(h, block):
        ql = slice(block * QB, (block + 1) * QB)
        dqt_ref[h, :, ql] = dot(kt_ref[h], ds_ref[block]).astype(BF16)

    def value_side(h, block):
        ql = slice(block * QB, (block + 1) * QB)
        dv = dot_nt(dot_ref[h, :, ql], p_ref[block]) * 4.0
        dvt_ref[h] = dvt_ref[h] + dv if block else dv

    def key_side(h, block):
        ql = slice(block * QB, (block + 1) * QB)
        dk = dot_nt(qt_ref[h, :, ql], ds_ref[block])
        dkt_ref[h] = dkt_ref[h] + dk if block else dk

    def block_step(h, block, km, vm, before):
        half = h // 8
        ql = slice(block * QB, (block + 1) * QB)
        qt = qt_ref[pl.ds(half * 8, 8), :, ql].reshape(half_width, QB)
        dot_t = dot_ref[pl.ds(half * 8, 8), :, ql].reshape(half_width, QB)
        tops, sums = [], []
        for j in range(PATCH // STRIP):
            s = dot(km[j * STRIP : (j + 1) * STRIP], qt)
            if j == 0:
                query_side(before, 1 - block)
            for c in range(STRIP // CHUNK):
                part = s[c * CHUNK : (c + 1) * CHUNK].reshape(CHUNK // 8, 8, QB)
                top = jnp.max(part, axis=0)
                e = jnp.exp2((part - top) * EXP_SCALE)
                e_ref[block, j * (STRIP // CHUNK) + c] = e
                tops.append(top)
                sums.append(jnp.sum(e, axis=0))
        value_side(before, 1 - block)
        peak = functools.reduce(jnp.maximum, tops)
        peak = jnp.max(peak, axis=0, keepdims=True)
        weights = [jnp.exp2((top - peak) * EXP_SCALE) for top in tops]
        total = functools.reduce(jnp.add, [a * w for a, w in zip(sums, weights)])
        inverse = 1.0 / jnp.sum(total, axis=0, keepdims=True)
        for c in range(CHUNKS):
            p = e_ref[block, c] * (weights[c] * inverse)
            p_ref[block, c * CHUNK : (c + 1) * CHUNK] = p.reshape(CHUNK, QB).astype(BF16)
        ot = dot(vt_ref[h], p_ref[block])
        key_side(before, 1 - block)
        at_ref[h, :, ql] = ot.astype(BF16)
        delta = jnp.sum(ot * dot_ref[h, :, ql].astype(F32), axis=0, keepdims=True)
        for j in range(PATCH // STRIP):
            dp = dot(vm[j * STRIP : (j + 1) * STRIP], dot_t)
            for c in range(STRIP // CHUNK):
                rows = slice(j * STRIP + c * CHUNK, j * STRIP + (c + 1) * CHUNK)
                p = p_ref[block, rows].astype(F32)
                ds = p * (dp[c * CHUNK : (c + 1) * CHUNK] - delta)
                ds_ref[block, rows] = ds.astype(BF16)

    def after_scatter():
        gather_done()
        group_scatter(1)

    def head_step(h, _):
        half = h // 8
        lane = lax.broadcasted_iota(jnp.int32, (1, half_width), 1) // HEAD_DIM
        mask = (lane == h % 8).astype(F32).astype(BF16)
        km = k_ref[half] * mask
        vm = v_ref[half] * mask
        block_step(h, 0, km, vm, jnp.maximum(h - 1, 0))
        block_step(h, 1, km, vm, h)

        steps = {
            FIRST_HEAD[1]: lambda: group_part(0),
            FIRST_HEAD[1] + 1: scatter_high,
            FIRST_HEAD[1] + 2: scatter_low,
            FIRST_HEAD[1] + 3: gather_low,
            FIRST_HEAD[1] + 4: gather_high,
            FIRST_HEAD[2]: lambda: group_part(1),
            FIRST_HEAD[2] + 1: after_scatter,
            FIRST_HEAD[2] + 2: lambda: group_gather(1),
        }
        for head, act in steps.items():
            pl.when(h == head)(act)

        return 0

    lax.fori_loop(0, HEADS, head_step, 0)
    query_side(HEADS - 1, 1)
    value_side(HEADS - 1, 1)
    key_side(HEADS - 1, 1)

    group_part(2)
    cot_t = [ref[...].reshape(C, PATCH).astype(BF16) for ref in (dqt_ref, dkt_ref, dvt_ref)]
    ng_t = dot(wqkv_ref[...], jnp.concatenate(cot_t, axis=0))
    for part in range(PARTS):
        rows = slice(part * PART_ROWS, (part + 1) * PART_ROWS)
        ng = ng_t[:, rows].T
        xhat = xhat_ref[rows]
        ng_mean = jnp.mean(ng, axis=1, keepdims=True)
        mixed = jnp.mean(ng * xhat, axis=1, keepdims=True)
        grad = oga_ref[rows].astype(F32) + rstd_ref[rows] * (ng - ng_mean - xhat * mixed)
        start_part(grad, back_out, back_both, part, back_sems)
        if part == 1:
            group_scatter(2)
        if part:
            send_part(back_out, back_both, back_in, part - 1, CHIPS - STRIDE, back_sems)
    send_part(back_out, back_both, back_in, PARTS - 1, CHIPS - STRIDE, back_sems)
    group_gather(2)

    at = at_ref[...].reshape(C, PATCH)
    block_out = x_ref[...].astype(F32) + dot(transposed(at), wp_ref[...])
    block_out = block_out.astype(BF16)
    group_finish(1)
    slot_col = as_column(recv_slots(hilbert_ref))
    gather = [gather_columns(slot_col, part) for part in range(PARTS)]
    out_ref[...] = dot(jnp.concatenate(gather, axis=1), block_out).astype(BF16)
    stores[0].start()
    group_close(0)
    group_close(1)
    slot_col = as_column(send_slots(zorder_ref))
    gather = [gather_columns(slot_col, part) for part in range(PARTS)]
    group_finish(2)
    total = jnp.zeros((PATCH, C), F32)
    for part in range(PARTS):
        wait_part(back_in, part, back_sems.at[3, part])
        total += dot(gather[part], unpacked(back_in[part_chips(part)]))
    feat_grad_ref[...] = total.astype(BF16)
    stores[1].start()
    group_close(2)
    for section in range(3):
        qkvg_ref[:, section * C : (section + 1) * C] = assemble(section).T
    projg_ref[...] = assemble(3)
    stores[2].start()
    stores[3].start()
    for part in range(PARTS):
        wait_part(there_in, part, there_sems.at[2, part])
        wait_part(back_in, part, back_sems.at[2, part])
    for store in stores:
        store.wait()


def finish_kernel(*refs):
    sources, targets, rooms, sems = refs[:4], refs[4:8], refs[8:12], refs[12]
    ins = [
        pltpu.make_async_copy(source, room, sems.at[0, i])
        for i, (source, room) in enumerate(zip(sources, rooms))
    ]
    outs = [
        pltpu.make_async_copy(room, target, sems.at[1, i])
        for i, (room, target) in enumerate(zip(rooms, targets))
    ]
    for copy in ins:
        copy.start()
    for copy_in, copy_out in zip(ins, outs):
        copy_in.wait()
        copy_out.start()
    for copy in outs:
        copy.wait()


def on_device(features, zorder_to, hilbert_from, qkv_weight, proj_weight, out_grad):
    anywhere = pl.BlockSpec(memory_space=pl.ANY)
    out_shape = (
        jax.ShapeDtypeStruct((PATCH, C), BF16),
        jax.ShapeDtypeStruct((PATCH, C), BF16),
        jax.ShapeDtypeStruct((C, 3 * C), F32),
        jax.ShapeDtypeStruct((C, C), F32),
    )
    points = pltpu.VMEM((PATCH, C), BF16)
    index = pltpu.VMEM((1, PATCH), jnp.int32)
    halves = pltpu.VMEM((2, PATCH, C // 2), BF16)
    heads_t = pltpu.VMEM((HEADS, HEAD_DIM, PATCH), BF16)
    heads_f = pltpu.VMEM((HEADS, HEAD_DIM, PATCH), F32)
    queries = pltpu.VMEM((2, PATCH, QB), BF16)
    pieces = pltpu.VMEM((CHIPS, 2, 2 * CAP, LANES), BF16)
    both_cores = pltpu.VMEM((GROUPS, 2, CHIPS, 8, LANES), F32)
    one_core = pltpu.VMEM((GROUPS, CHIPS, 8, LANES), F32)
    results = pl.pallas_call(
        block_kernel,
        out_shape=out_shape,
        in_specs=[anywhere] * 6,
        out_specs=(anywhere,) * 4,
        scratch_shapes=[
            points, points,
            pltpu.VMEM((C, 3 * C), F32),
            pltpu.VMEM((C, C), F32),
            points, index, index,
            pltpu.VMEM((C, 3 * C), BF16),
            pltpu.VMEM((C, C), BF16),
            points, points, points, points,
            pltpu.VMEM((3 * C, C), BF16),
            pltpu.VMEM((PATCH, C), F32),
            pltpu.VMEM((PATCH, 1), F32),
            halves, halves, heads_t, heads_t, heads_t, heads_t,
            queries, queries,
            pltpu.VMEM((2, CHUNKS, CHUNK // 8, 8, QB), F32),
            heads_t, heads_t, heads_f, heads_f,
            pieces, pieces, pieces, pieces, pieces, pieces,
            both_cores, one_core, one_core, one_core,
            pltpu.VMEM((GROUPS, 8, LANES), F32),
            both_cores,
            pltpu.VMEM((SIDE, 8, LANES), F32),
            pltpu.VMEM((SIDE, 8, LANES), F32),
            pltpu.SemaphoreType.DMA((6,)),
            pltpu.SemaphoreType.DMA((4, PARTS)),
            pltpu.SemaphoreType.DMA((4, PARTS)),
            pltpu.SemaphoreType.DMA((GROUPS, 8)),
            pltpu.SemaphoreType.DMA((2, 4)),
            pltpu.SemaphoreType.DMA((4,)),
        ],
        compiler_params=pltpu.CompilerParams(
            collective_id=0, has_side_effects=True, vmem_limit_bytes=60 * 1024 * 1024
        ),
        cost_estimate=pl.CostEstimate(
            flops=28_000_000_000, bytes_accessed=5_000_000, transcendentals=16_777_216
        ),
    )(
        features,
        zorder_to.reshape(1, PATCH),
        hilbert_from.reshape(1, PATCH),
        qkv_weight,
        proj_weight,
        out_grad,
    )
    return pl.pallas_call(
        finish_kernel,
        out_shape=out_shape,
        in_specs=[anywhere] * 4,
        out_specs=(anywhere,) * 4,
        scratch_shapes=[
            points, points,
            pltpu.VMEM((C, 3 * C), F32),
            pltpu.VMEM((C, C), F32),
            pltpu.SemaphoreType.DMA((2, 4)),
        ],
        compiler_params=pltpu.CompilerParams(vmem_limit_bytes=60 * 1024 * 1024),
        cost_estimate=pl.CostEstimate(flops=0, bytes_accessed=4_000_000, transcendentals=0),
    )(*results)


def solution(mesh):
    in_specs = (
        P(("row", "col"), None),
        P(("row", "col")),
        P(("row", "col")),
        P(),
        P(),
        P(("row", "col"), None),
    )
    out_specs = (P(("row", "col"), None), P(("row", "col"), None), P(), P())
    return jax.shard_map(
        on_device, mesh=mesh, in_specs=in_specs, out_specs=out_specs, check_vma=False
    )
```

```python
import functools

import jax
import jax.numpy as jnp
from jax import lax
from jax.experimental import pallas as pl
from jax.experimental.pallas import tpu as pltpu
from jax.sharding import PartitionSpec as P

HEADS = 16
HEAD_DIM = 16
PATCH = 1024
C = 256
QB = 512
CHUNK = 64
CHUNKS = PATCH // CHUNK
STRIP = 512
EXP_SCALE = 0.25 * 1.4426950408889634

F32 = jnp.float32
BF16 = jnp.bfloat16


def dot(a, b):
    return jnp.dot(a, b, preferred_element_type=F32)


def dot_nt(a, b):
    return lax.dot_general(a, b, (((1,), (1,)), ((), ())), preferred_element_type=F32)


def normalize(x):
    centered = x - jnp.mean(x, axis=1, keepdims=True)
    rstd = lax.rsqrt(jnp.mean(centered * centered, axis=1, keepdims=True) + 1e-05)
    return centered * rstd, rstd


def transposed(a):
    return a.astype(F32).T.astype(BF16)


MESH = pl.DeviceIdType.MESH
N_ROW = 8
N_COL = 16
DEVICES = N_ROW * N_COL
CHIPS = DEVICES // 2
CAP = PATCH // DEVICES
LANES = 128


STRIDE = 1
INVERSE_STRIDE = 1
PARTS = 4
PART_CHIPS = CHIPS // PARTS
PART_ROWS = PATCH // PARTS


def as_column(row):
    return jnp.broadcast_to(row, (LANES, PATCH)).T


def slots(key_row):
    key_col = as_column(key_row)
    ranks = []
    for block in range(PATCH // LANES):
        keys = key_row[:, block * LANES : (block + 1) * LANES]
        below = jnp.where(key_col < keys, 1.0, 0.0)
        ranks.append(jnp.sum(below, axis=0, keepdims=True))
    return jnp.concatenate(ranks, axis=1)


def scatter_rows(slot_row, part):
    row = lax.broadcasted_iota(jnp.int32, (PART_ROWS, PATCH), 0) + part * PART_ROWS
    return jnp.where(slot_row == row.astype(F32), 1.0, 0.0).astype(BF16)


def gather_columns(slot_col, part):
    lane = lax.broadcasted_iota(jnp.int32, (PATCH, LANES), 1) + part * PART_ROWS
    blocks = [
        jnp.where(slot_col == (lane + low).astype(F32), 1.0, 0.0).astype(BF16)
        for low in range(0, PART_ROWS, LANES)
    ]
    return jnp.concatenate(blocks, axis=1)


def chip_and_core(point):
    device = point // PATCH
    row, col = device // N_COL, device % N_COL
    return (row // 2) * N_COL + col, row % 2


def relative_slot(offset, core):
    return ((offset + CHIPS) * INVERSE_STRIDE % CHIPS) * 2 + core


def send_slots(zorder_ref):
    point = zorder_ref[...]
    chip, core = chip_and_core(point)
    slot = relative_slot(chip - position()[1], core)
    return slots((slot * PATCH + point % PATCH).astype(F32))


def recv_slots(hilbert_ref):
    chip, core = chip_and_core(hilbert_ref[...])
    slot = relative_slot(position()[1] - chip, core)
    local = lax.broadcasted_iota(jnp.int32, (1, PATCH), 1)
    return slots((slot * PATCH + local).astype(F32))


def packed(rows):
    rows = rows.reshape(2 * PART_CHIPS, CAP, C)
    pieces = jnp.concatenate([rows[:, :, :LANES], rows[:, :, LANES:]], axis=1).astype(BF16)
    return pieces.reshape(PART_CHIPS, 2, 2 * CAP, LANES)


def unpacked(pieces):
    pieces = pieces.reshape(2 * PART_CHIPS, 2 * CAP, LANES).astype(F32)
    left = pieces[:, :CAP].reshape(PART_ROWS, LANES)
    right = pieces[:, CAP:].reshape(PART_ROWS, LANES)
    return jnp.concatenate([left, right], axis=1).astype(BF16)


def part_chips(part):
    return slice(part * PART_CHIPS, (part + 1) * PART_CHIPS)


def position():
    row, col = lax.axis_index("row"), lax.axis_index("col")
    core = lax.rem(row, 2)
    return core, (row // 2) * N_COL + col, (row + 1 - 2 * core, col)


def chip_device(chip):
    core, _, _ = position()
    return (chip // N_COL) * 2 + core, lax.rem(chip, N_COL)


def for_chips(act):
    _, chip, _ = position()

    def body(step, _):
        other = lax.rem(chip + step * STRIDE, CHIPS)
        act(other, chip_device(other))
        return 0

    lax.fori_loop(1, CHIPS, body, 0)


def greet(barrier):
    _, _, sibling = position()
    pl.semaphore_signal(barrier, inc=1, device_id=sibling, device_id_type=MESH)
    for_chips(
        lambda _, device: pl.semaphore_signal(
            barrier, inc=1, device_id=device, device_id_type=MESH
        )
    )


def pair_copy(out_ref, both_ref, part, sems):
    core, _, sibling = position()
    return pltpu.make_async_remote_copy(
        src_ref=out_ref.at[part_chips(part), 1 - core],
        dst_ref=both_ref.at[part_chips(part), core],
        send_sem=sems.at[0, part],
        recv_sem=sems.at[1, part],
        device_id=sibling,
        device_id_type=MESH,
    )


def start_part(rows, out_ref, both_ref, part, sems):
    core, _, _ = position()
    out_ref[part_chips(part)] = packed(rows)
    pair_copy(out_ref, both_ref, part, sems).start()
    both_ref[part_chips(part), core] = out_ref[part_chips(part), core]


def send_part(out_ref, both_ref, in_ref, part, stride, sems):
    _, chip, _ = position()
    pair_copy(out_ref, both_ref, part, sems).wait()

    def body(step, _):
        pltpu.make_async_remote_copy(
            src_ref=both_ref.at[step],
            dst_ref=in_ref.at[step],
            send_sem=sems.at[2, part],
            recv_sem=sems.at[3, part],
            device_id=chip_device(lax.rem(chip + step * stride, CHIPS)),
            device_id_type=MESH,
        ).start()
        return 0

    lax.fori_loop(max(part * PART_CHIPS, 1), (part + 1) * PART_CHIPS, body, 0)
    if part == 0:
        in_ref[0] = both_ref[0]


def wait_part(in_ref, part, sem):
    wait_bytes(in_ref, PART_CHIPS - (part == 0), sem)


def wait_bytes(ref, count, sem):
    view = ref.at[pl.ds(0, count)]
    pltpu.make_async_copy(view, view, sem).wait()


SIDE = 8
GROUPS = 3
FIRST_HEAD = (0, 8, 13, HEADS)
OWNER_STRIDE = 13
OWNER_INVERSE = 5


def group_heads(g):
    return FIRST_HEAD[g + 1] - FIRST_HEAD[g]


def group_tiles(g):
    return 8 * group_heads(g)


def tiles(section):
    rows = section.shape[0]
    section = section.reshape(rows // 8, 8, C)
    halves = [section[:, None, :, :LANES], section[:, None, :, LANES:]]
    return jnp.concatenate(halves, axis=1).reshape(rows // 4, 8, LANES)


def untiled(pieces):
    pieces = pieces.reshape(-1, 2, 8, LANES)
    return jnp.concatenate([pieces[:, 0], pieces[:, 1]], axis=2).reshape(-1, C)


def block_kernel(
    feat_hbm, zorder_hbm, hilbert_hbm, wqkv_hbm, wp_hbm, og_hbm,
    out_hbm, feat_grad_hbm, qkvg_hbm, projg_hbm,
    out_ref, feat_grad_ref, qkvg_ref, projg_ref,
    feat_ref, zorder_ref, hilbert_ref, wqkv_ref, wp_ref, og_ref, oga_ref, x_ref, normed_ref,
    wqkv_t_ref, xhat_ref, rstd_ref, k_ref, v_ref, qt_ref, kt_ref, vt_ref, dot_ref,
    p_ref, ds_ref, e_ref, at_ref, dqt_ref, dkt_ref, dvt_ref,
    there_out, there_both, there_in, back_out, back_both, back_in,
    part_ref, half_ref, sum_ref, chunk_in_ref, result_ref, total_ref, low_out_ref, low_in_ref,
    load_sems, there_sems, back_sems, group_sems, level_sems, store_sems,
):
    half_width = C // 2
    core, chip, sibling = position()
    barrier = pltpu.get_barrier_semaphore()
    sources = (zorder_hbm, feat_hbm, hilbert_hbm, og_hbm, wp_hbm, wqkv_hbm)
    targets = (zorder_ref, feat_ref, hilbert_ref, og_ref, wp_ref, wqkv_ref)
    loads = [
        pltpu.make_async_copy(source, target, load_sems.at[i])
        for i, (source, target) in enumerate(zip(sources, targets))
    ]
    stores = [
        pltpu.make_async_copy(source, target, store_sems.at[i])
        for i, (source, target) in enumerate((
            (out_ref, out_hbm),
            (feat_grad_ref, feat_grad_hbm),
            (qkvg_ref, qkvg_hbm),
            (projg_ref, projg_hbm),
        ))
    ]
    for load in loads:
        load.start()
    greet(barrier)
    loads[0].wait()
    there_slots = send_slots(zorder_ref)
    loads[1].wait()
    for part in range(PARTS):
        rows = dot(scatter_rows(there_slots, part), feat_ref[...])
        if part == 0:
            pl.semaphore_wait(barrier, CHIPS)
        start_part(rows, there_out, there_both, part, there_sems)
        if part:
            send_part(there_out, there_both, there_in, part - 1, STRIDE, there_sems)
    send_part(there_out, there_both, there_in, PARTS - 1, STRIDE, there_sems)

    for load in loads[2:]:
        load.wait()
    back_slots = recv_slots(hilbert_ref)
    for part in range(PARTS):
        rows = slice(part * PART_ROWS, (part + 1) * PART_ROWS)
        oga_ref[rows] = dot(scatter_rows(back_slots, part), og_ref[...]).astype(BF16)
    do_t = dot_nt(wp_ref[...], oga_ref[...]).astype(BF16).astype(F32)
    dot_ref[...] = (do_t * 0.25).astype(BF16).reshape(HEADS, HEAD_DIM, PATCH)
    wqkv_t_ref[...] = transposed(wqkv_ref[...])
    p_ref[1] = jnp.zeros((PATCH, QB), BF16)
    ds_ref[1] = jnp.zeros((PATCH, QB), BF16)
    dkt_ref[0] = jnp.zeros((HEAD_DIM, PATCH), F32)
    dvt_ref[0] = jnp.zeros((HEAD_DIM, PATCH), F32)

    for part in range(PARTS):
        wait_part(there_in, part, there_sems.at[3, part])
        rows = slice(part * PART_ROWS, (part + 1) * PART_ROWS)
        x = unpacked(there_in[part_chips(part)])
        x_ref[rows] = x
        xhat, rstd = normalize(x.astype(F32))
        xhat_ref[rows] = xhat
        rstd_ref[rows] = rstd
        normed = xhat.astype(BF16)
        normed_ref[rows] = normed
        kv = dot(normed, wqkv_ref[:, C:]).astype(BF16)
        for ref, low in ((k_ref, 0), (v_ref, C)):
            ref[0, rows] = kv[:, low : low + half_width]
            ref[1, rows] = kv[:, low + half_width : low + C]
        qkv_t = dot(wqkv_t_ref[...], transposed(normed)).astype(BF16)
        for ref, low in ((qt_ref, 0), (kt_ref, C), (vt_ref, 2 * C)):
            ref[:, :, rows] = qkv_t[low : low + C].reshape(HEADS, HEAD_DIM, PART_ROWS)

    def group_part(g):
        heads = slice(FIRST_HEAD[g], FIRST_HEAD[g + 1])
        count = group_heads(g) * HEAD_DIM

        def rows(ref):
            return ref[heads].reshape(count, PATCH).astype(BF16)

        cot = jnp.concatenate([rows(ref) for ref in (dqt_ref, dkt_ref, dvt_ref)], axis=0)
        sums = dot(cot, normed_ref[...])
        sums = [sums[i * count : (i + 1) * count] for i in range(3)]
        half = group_tiles(g) // 2
        for section, value in enumerate(sums + [dot(rows(at_ref), oga_ref[...])]):
            low = section % 2 * half
            part_ref[g, section // 2, low : low + half] = tiles(value)
        group_half(g).start()

    def group_half(g):
        count = pl.ds(0, group_tiles(g))
        return pltpu.make_async_remote_copy(
            src_ref=part_ref.at[g, 1 - core, count],
            dst_ref=half_ref.at[g, count],
            send_sem=group_sems.at[g, 0],
            recv_sem=group_sems.at[g, 1],
            device_id=sibling,
            device_id_type=MESH,
        )

    my_tile = lax.rem(chip * OWNER_INVERSE, CHIPS)

    def by_owner(g, act):
        pl.when(my_tile < group_tiles(g))(lambda: act(True))
        pl.when(my_tile >= group_tiles(g))(lambda: act(False))

    def group_scatter(g):
        group_half(g).wait()
        count = group_tiles(g)
        sum_ref[g, :count] = part_ref[g, core, :count] + half_ref[g, :count]

        def body(tile, _):
            owner = lax.rem(tile * OWNER_STRIDE, CHIPS)

            @pl.when(owner != chip)
            def _():
                pltpu.make_async_remote_copy(
                    src_ref=sum_ref.at[g, tile],
                    dst_ref=chunk_in_ref.at[g, chip],
                    send_sem=group_sems.at[g, 2],
                    recv_sem=group_sems.at[g, 3],
                    device_id=chip_device(owner),
                    device_id_type=MESH,
                ).start()

            return 0

        lax.fori_loop(0, count, body, 0)

        @pl.when(my_tile < count)
        def _():
            chunk_in_ref[g, chip] = sum_ref[g, my_tile]

    def group_gather(g):
        @pl.when(my_tile < group_tiles(g))
        def _():
            wait_bytes(chunk_in_ref.at[g], CHIPS - 1, group_sems.at[g, 3])
            result_ref[g] = jnp.sum(chunk_in_ref[g], axis=0)
            for_chips(
                lambda other, device: pltpu.make_async_remote_copy(
                    src_ref=result_ref.at[g],
                    dst_ref=total_ref.at[g, core, my_tile],
                    send_sem=group_sems.at[g, 4],
                    recv_sem=group_sems.at[g, 5],
                    device_id=device,
                    device_id_type=MESH,
                ).start()
            )
            total_ref[g, core, my_tile] = result_ref[g]

    def group_final(g):
        count = pl.ds(0, group_tiles(g))
        return pltpu.make_async_remote_copy(
            src_ref=total_ref.at[g, core, count],
            dst_ref=total_ref.at[g, core, count],
            send_sem=group_sems.at[g, 6],
            recv_sem=group_sems.at[g, 7],
            device_id=sibling,
            device_id_type=MESH,
        )

    def group_finish(g):
        def arrived(owner):
            wait_bytes(total_ref.at[g, core], group_tiles(g) - owner, group_sems.at[g, 5])

        by_owner(g, arrived)
        group_final(g).start()

    high, low = chip // SIDE, lax.rem(chip, SIDE)

    def level_copy(src, dst, to, sem):
        return pltpu.make_async_remote_copy(
            src_ref=src,
            dst_ref=dst,
            send_sem=level_sems.at[0, sem],
            recv_sem=level_sems.at[1, sem],
            device_id=chip_device(to),
            device_id_type=MESH,
        )

    def others(mine, act):
        def body(step, _):
            act(lax.rem(mine + step, SIDE))
            return 0

        lax.fori_loop(1, SIDE, body, 0)

    def level_wait(direction, sem, rows):
        view = sum_ref.at[0, pl.ds(0, (SIDE - 1) * rows)]
        pltpu.make_async_copy(view, view, level_sems.at[direction, sem]).wait()

    def run(index):
        return pl.ds(index * SIDE, SIDE)

    def scatter_high():
        group_half(0).wait()
        sum_ref[0] = part_ref[0, core] + half_ref[0]
        others(high, lambda to: level_copy(
            sum_ref.at[0, run(to)], chunk_in_ref.at[0, run(high)], to * SIDE + low, 0
        ).start())
        chunk_in_ref[0, run(high)] = sum_ref[0, run(high)]

    def scatter_low():
        level_wait(1, 0, SIDE)
        summed = chunk_in_ref[0].reshape(SIDE, SIDE, 8, LANES)
        low_out_ref[...] = jnp.sum(summed, axis=0)
        others(low, lambda to: level_copy(
            low_out_ref.at[to], low_in_ref.at[low], high * SIDE + to, 1
        ).start())
        low_in_ref[low] = low_out_ref[low]

    def gather_low():
        level_wait(1, 1, 1)
        result_ref[0] = jnp.sum(low_in_ref[...], axis=0)
        others(low, lambda to: level_copy(
            result_ref.at[0], total_ref.at[0, core, chip], high * SIDE + to, 2
        ).start())
        total_ref[0, core, chip] = result_ref[0]

    def gather_high():
        level_wait(1, 2, 1)
        others(high, lambda to: level_copy(
            total_ref.at[0, core, run(high)], total_ref.at[0, core, run(high)], to * SIDE + low, 3
        ).start())

    def gather_done():
        level_wait(1, 3, SIDE)
        group_final(0).start()

    def group_close(g):
        group_final(g).wait()
        if g == 0:
            for sem, rows in enumerate((SIDE, 1, 1, SIDE)):
                level_wait(0, sem, rows)
            return

        def sent(owner):
            wait_bytes(sum_ref.at[g], group_tiles(g) - owner, group_sems.at[g, 2])
            if owner:
                wait_bytes(sum_ref.at[g], CHIPS - 1, group_sems.at[g, 4])

        by_owner(g, sent)

    def assemble(section):
        rows = []
        for g in range(GROUPS):
            half = group_tiles(g) // 2
            low = section % 2 * half
            rows.append(untiled(total_ref[g, section // 2, low : low + half]))
        return jnp.concatenate(rows, axis=0)

    def query_side(h, block):
        ql = slice(block * QB, (block + 1) * QB)
        dqt_ref[h, :, ql] = dot(kt_ref[h], ds_ref[block]).astype(BF16)

    def value_side(h, block):
        ql = slice(block * QB, (block + 1) * QB)
        dv = dot_nt(dot_ref[h, :, ql], p_ref[block]) * 4.0
        dvt_ref[h] = dvt_ref[h] + dv if block else dv

    def key_side(h, block):
        ql = slice(block * QB, (block + 1) * QB)
        dk = dot_nt(qt_ref[h, :, ql], ds_ref[block])
        dkt_ref[h] = dkt_ref[h] + dk if block else dk

    def block_step(h, block, km, vm, before):
        half = h // 8
        ql = slice(block * QB, (block + 1) * QB)
        qt = qt_ref[pl.ds(half * 8, 8), :, ql].reshape(half_width, QB)
        dot_t = dot_ref[pl.ds(half * 8, 8), :, ql].reshape(half_width, QB)
        tops, sums = [], []
        for j in range(PATCH // STRIP):
            s = dot(km[j * STRIP : (j + 1) * STRIP], qt)
            if j == 0:
                query_side(before, 1 - block)
            for c in range(STRIP // CHUNK):
                part = s[c * CHUNK : (c + 1) * CHUNK].reshape(CHUNK // 8, 8, QB)
                top = jnp.max(part, axis=0)
                e = jnp.exp2((part - top) * EXP_SCALE)
                e_ref[block, j * (STRIP // CHUNK) + c] = e
                tops.append(top)
                sums.append(jnp.sum(e, axis=0))
        value_side(before, 1 - block)
        peak = functools.reduce(jnp.maximum, tops)
        peak = jnp.max(peak, axis=0, keepdims=True)
        weights = [jnp.exp2((top - peak) * EXP_SCALE) for top in tops]
        total = functools.reduce(jnp.add, [a * w for a, w in zip(sums, weights)])
        inverse = 1.0 / jnp.sum(total, axis=0, keepdims=True)
        for c in range(CHUNKS):
            p = e_ref[block, c] * (weights[c] * inverse)
            p_ref[block, c * CHUNK : (c + 1) * CHUNK] = p.reshape(CHUNK, QB).astype(BF16)
        ot = dot(vt_ref[h], p_ref[block])
        key_side(before, 1 - block)
        at_ref[h, :, ql] = ot.astype(BF16)
        delta = jnp.sum(ot * dot_ref[h, :, ql].astype(F32), axis=0, keepdims=True)
        for j in range(PATCH // STRIP):
            dp = dot(vm[j * STRIP : (j + 1) * STRIP], dot_t)
            for c in range(STRIP // CHUNK):
                rows = slice(j * STRIP + c * CHUNK, j * STRIP + (c + 1) * CHUNK)
                p = p_ref[block, rows].astype(F32)
                ds = p * (dp[c * CHUNK : (c + 1) * CHUNK] - delta)
                ds_ref[block, rows] = ds.astype(BF16)

    def after_scatter():
        gather_done()
        group_scatter(1)

    def head_step(h, _):
        half = h // 8
        lane = lax.broadcasted_iota(jnp.int32, (1, half_width), 1) // HEAD_DIM
        mask = (lane == h % 8).astype(F32).astype(BF16)
        km = k_ref[half] * mask
        vm = v_ref[half] * mask
        block_step(h, 0, km, vm, jnp.maximum(h - 1, 0))
        block_step(h, 1, km, vm, h)

        steps = {
            FIRST_HEAD[1]: lambda: group_part(0),
            FIRST_HEAD[1] + 1: scatter_high,
            FIRST_HEAD[1] + 2: scatter_low,
            FIRST_HEAD[1] + 3: gather_low,
            FIRST_HEAD[1] + 4: gather_high,
            FIRST_HEAD[2]: lambda: group_part(1),
            FIRST_HEAD[2] + 1: after_scatter,
            FIRST_HEAD[2] + 2: lambda: group_gather(1),
        }
        for head, act in steps.items():
            pl.when(h == head)(act)

        return 0

    lax.fori_loop(0, HEADS, head_step, 0)
    query_side(HEADS - 1, 1)
    value_side(HEADS - 1, 1)
    key_side(HEADS - 1, 1)

    group_part(2)
    cot_t = [ref[...].reshape(C, PATCH).astype(BF16) for ref in (dqt_ref, dkt_ref, dvt_ref)]
    ng_t = dot(wqkv_ref[...], jnp.concatenate(cot_t, axis=0))
    for part in range(PARTS):
        rows = slice(part * PART_ROWS, (part + 1) * PART_ROWS)
        ng = ng_t[:, rows].T
        xhat = xhat_ref[rows]
        ng_mean = jnp.mean(ng, axis=1, keepdims=True)
        mixed = jnp.mean(ng * xhat, axis=1, keepdims=True)
        grad = oga_ref[rows].astype(F32) + rstd_ref[rows] * (ng - ng_mean - xhat * mixed)
        start_part(grad, back_out, back_both, part, back_sems)
        if part == 1:
            group_scatter(2)
        if part:
            send_part(back_out, back_both, back_in, part - 1, CHIPS - STRIDE, back_sems)
    send_part(back_out, back_both, back_in, PARTS - 1, CHIPS - STRIDE, back_sems)
    group_gather(2)

    at = at_ref[...].reshape(C, PATCH)
    block_out = x_ref[...].astype(F32) + dot(transposed(at), wp_ref[...])
    block_out = block_out.astype(BF16)
    group_finish(1)
    slot_col = as_column(recv_slots(hilbert_ref))
    gather = [gather_columns(slot_col, part) for part in range(PARTS)]
    out_ref[...] = dot(jnp.concatenate(gather, axis=1), block_out).astype(BF16)
    stores[0].start()
    group_close(0)
    group_close(1)
    slot_col = as_column(send_slots(zorder_ref))
    gather = [gather_columns(slot_col, part) for part in range(PARTS)]
    group_finish(2)
    total = jnp.zeros((PATCH, C), F32)
    for part in range(PARTS):
        wait_part(back_in, part, back_sems.at[3, part])
        total += dot(gather[part], unpacked(back_in[part_chips(part)]))
    feat_grad_ref[...] = total.astype(BF16)
    stores[1].start()
    group_close(2)
    for section in range(3):
        qkvg_ref[:, section * C : (section + 1) * C] = assemble(section).T
    projg_ref[...] = assemble(3)
    stores[2].start()
    stores[3].start()
    for part in range(PARTS):
        wait_part(there_in, part, there_sems.at[2, part])
        wait_part(back_in, part, back_sems.at[2, part])
    for store in stores:
        store.wait()


def finish_kernel(*refs):
    sources, targets, rooms, sems = refs[:4], refs[4:8], refs[8:12], refs[12]
    ins = [
        pltpu.make_async_copy(source, room, sems.at[0, i])
        for i, (source, room) in enumerate(zip(sources, rooms))
    ]
    outs = [
        pltpu.make_async_copy(room, target, sems.at[1, i])
        for i, (room, target) in enumerate(zip(rooms, targets))
    ]
    for copy in ins:
        copy.start()
    for copy_in, copy_out in zip(ins, outs):
        copy_in.wait()
        copy_out.start()
    for copy in outs:
        copy.wait()


def on_device(features, zorder_to, hilbert_from, qkv_weight, proj_weight, out_grad):
    anywhere = pl.BlockSpec(memory_space=pl.ANY)
    out_shape = (
        jax.ShapeDtypeStruct((PATCH, C), BF16),
        jax.ShapeDtypeStruct((PATCH, C), BF16),
        jax.ShapeDtypeStruct((C, 3 * C), F32),
        jax.ShapeDtypeStruct((C, C), F32),
    )
    points = pltpu.VMEM((PATCH, C), BF16)
    index = pltpu.VMEM((1, PATCH), jnp.int32)
    halves = pltpu.VMEM((2, PATCH, C // 2), BF16)
    heads_t = pltpu.VMEM((HEADS, HEAD_DIM, PATCH), BF16)
    heads_f = pltpu.VMEM((HEADS, HEAD_DIM, PATCH), F32)
    queries = pltpu.VMEM((2, PATCH, QB), BF16)
    pieces = pltpu.VMEM((CHIPS, 2, 2 * CAP, LANES), BF16)
    both_cores = pltpu.VMEM((GROUPS, 2, CHIPS, 8, LANES), F32)
    one_core = pltpu.VMEM((GROUPS, CHIPS, 8, LANES), F32)
    results = pl.pallas_call(
        block_kernel,
        out_shape=out_shape,
        in_specs=[anywhere] * 6,
        out_specs=(anywhere,) * 4,
        scratch_shapes=[
            points, points,
            pltpu.VMEM((C, 3 * C), F32),
            pltpu.VMEM((C, C), F32),
            points, index, index,
            pltpu.VMEM((C, 3 * C), BF16),
            pltpu.VMEM((C, C), BF16),
            points, points, points, points,
            pltpu.VMEM((3 * C, C), BF16),
            pltpu.VMEM((PATCH, C), F32),
            pltpu.VMEM((PATCH, 1), F32),
            halves, halves, heads_t, heads_t, heads_t, heads_t,
            queries, queries,
            pltpu.VMEM((2, CHUNKS, CHUNK // 8, 8, QB), F32),
            heads_t, heads_t, heads_f, heads_f,
            pieces, pieces, pieces, pieces, pieces, pieces,
            both_cores, one_core, one_core, one_core,
            pltpu.VMEM((GROUPS, 8, LANES), F32),
            both_cores,
            pltpu.VMEM((SIDE, 8, LANES), F32),
            pltpu.VMEM((SIDE, 8, LANES), F32),
            pltpu.SemaphoreType.DMA((6,)),
            pltpu.SemaphoreType.DMA((4, PARTS)),
            pltpu.SemaphoreType.DMA((4, PARTS)),
            pltpu.SemaphoreType.DMA((GROUPS, 8)),
            pltpu.SemaphoreType.DMA((2, 4)),
            pltpu.SemaphoreType.DMA((4,)),
        ],
        compiler_params=pltpu.CompilerParams(
            collective_id=0, has_side_effects=True, vmem_limit_bytes=60 * 1024 * 1024
        ),
        cost_estimate=pl.CostEstimate(
            flops=28_000_000_000, bytes_accessed=5_000_000, transcendentals=16_777_216
        ),
    )(
        features,
        zorder_to.reshape(1, PATCH),
        hilbert_from.reshape(1, PATCH),
        qkv_weight,
        proj_weight,
        out_grad,
    )
    return pl.pallas_call(
        finish_kernel,
        out_shape=out_shape,
        in_specs=[anywhere] * 4,
        out_specs=(anywhere,) * 4,
        scratch_shapes=[
            points, points,
            pltpu.VMEM((C, 3 * C), F32),
            pltpu.VMEM((C, C), F32),
            pltpu.SemaphoreType.DMA((2, 4)),
        ],
        compiler_params=pltpu.CompilerParams(vmem_limit_bytes=60 * 1024 * 1024),
        cost_estimate=pl.CostEstimate(flops=0, bytes_accessed=4_000_000, transcendentals=0),
    )(*results)


def solution(mesh):
    in_specs = (
        P(("row", "col"), None),
        P(("row", "col")),
        P(("row", "col")),
        P(),
        P(),
        P(("row", "col"), None),
    )
    out_specs = (P(("row", "col"), None), P(("row", "col"), None), P(), P())
    return jax.shard_map(
        on_device, mesh=mesh, in_specs=in_specs, out_specs=out_specs, check_vma=False
    )
```

```python
import functools

import jax
import jax.numpy as jnp
from jax import lax
from jax.experimental import pallas as pl
from jax.experimental.pallas import tpu as pltpu
from jax.sharding import PartitionSpec as P

HEADS = 16
HEAD_DIM = 16
PATCH = 1024
C = 256
QB = 512
CHUNK = 64
CHUNKS = PATCH // CHUNK
STRIP = 256
EXP_SCALE = 0.25 * 1.4426950408889634

F32 = jnp.float32
BF16 = jnp.bfloat16


def dot(a, b):
    return jnp.dot(a, b, preferred_element_type=F32)


def dot_nt(a, b):
    return lax.dot_general(a, b, (((1,), (1,)), ((), ())), preferred_element_type=F32)


def normalize(x):
    centered = x - jnp.mean(x, axis=1, keepdims=True)
    rstd = lax.rsqrt(jnp.mean(centered * centered, axis=1, keepdims=True) + 1e-05)
    return centered * rstd, rstd


def transposed(a):
    return a.astype(F32).T.astype(BF16)


MESH = pl.DeviceIdType.MESH
N_ROW = 8
N_COL = 16
DEVICES = N_ROW * N_COL
CHIPS = DEVICES // 2
CAP = PATCH // DEVICES
LANES = 128


STRIDE = 1
INVERSE_STRIDE = 1
PARTS = 4
PART_CHIPS = CHIPS // PARTS
PART_ROWS = PATCH // PARTS


def as_column(row):
    return jnp.broadcast_to(row, (LANES, PATCH)).T


def slots(key_row):
    key_col = as_column(key_row)
    ranks = []
    for block in range(PATCH // LANES):
        keys = key_row[:, block * LANES : (block + 1) * LANES]
        below = jnp.where(key_col < keys, 1.0, 0.0)
        ranks.append(jnp.sum(below, axis=0, keepdims=True))
    return jnp.concatenate(ranks, axis=1)


def scatter_rows(slot_row, part):
    row = lax.broadcasted_iota(jnp.int32, (PART_ROWS, PATCH), 0) + part * PART_ROWS
    return jnp.where(slot_row == row.astype(F32), 1.0, 0.0).astype(BF16)


def gather_columns(slot_col, part):
    lane = lax.broadcasted_iota(jnp.int32, (PATCH, LANES), 1) + part * PART_ROWS
    blocks = [
        jnp.where(slot_col == (lane + low).astype(F32), 1.0, 0.0).astype(BF16)
        for low in range(0, PART_ROWS, LANES)
    ]
    return jnp.concatenate(blocks, axis=1)


def chip_and_core(point):
    device = point // PATCH
    row, col = device // N_COL, device % N_COL
    return (row // 2) * N_COL + col, row % 2


def relative_slot(offset, core):
    return ((offset + CHIPS) * INVERSE_STRIDE % CHIPS) * 2 + core


def send_slots(zorder_ref):
    point = zorder_ref[...]
    chip, core = chip_and_core(point)
    slot = relative_slot(chip - position()[1], core)
    return slots((slot * PATCH + point % PATCH).astype(F32))


def recv_slots(hilbert_ref):
    chip, core = chip_and_core(hilbert_ref[...])
    slot = relative_slot(position()[1] - chip, core)
    local = lax.broadcasted_iota(jnp.int32, (1, PATCH), 1)
    return slots((slot * PATCH + local).astype(F32))


def packed(rows):
    rows = rows.reshape(2 * PART_CHIPS, CAP, C)
    pieces = jnp.concatenate([rows[:, :, :LANES], rows[:, :, LANES:]], axis=1).astype(BF16)
    return pieces.reshape(PART_CHIPS, 2, 2 * CAP, LANES)


def unpacked(pieces):
    pieces = pieces.reshape(2 * PART_CHIPS, 2 * CAP, LANES).astype(F32)
    left = pieces[:, :CAP].reshape(PART_ROWS, LANES)
    right = pieces[:, CAP:].reshape(PART_ROWS, LANES)
    return jnp.concatenate([left, right], axis=1).astype(BF16)


def part_chips(part):
    return slice(part * PART_CHIPS, (part + 1) * PART_CHIPS)


def position():
    row, col = lax.axis_index("row"), lax.axis_index("col")
    core = lax.rem(row, 2)
    return core, (row // 2) * N_COL + col, (row + 1 - 2 * core, col)


def chip_device(chip):
    core, _, _ = position()
    return (chip // N_COL) * 2 + core, lax.rem(chip, N_COL)


def for_chips(act):
    _, chip, _ = position()

    def body(step, _):
        other = lax.rem(chip + step * STRIDE, CHIPS)
        act(other, chip_device(other))
        return 0

    lax.fori_loop(1, CHIPS, body, 0)


def greet(barrier):
    _, _, sibling = position()
    pl.semaphore_signal(barrier, inc=1, device_id=sibling, device_id_type=MESH)
    for_chips(
        lambda _, device: pl.semaphore_signal(
            barrier, inc=1, device_id=device, device_id_type=MESH
        )
    )


def pair_copy(out_ref, both_ref, part, sems):
    core, _, sibling = position()
    return pltpu.make_async_remote_copy(
        src_ref=out_ref.at[part_chips(part), 1 - core],
        dst_ref=both_ref.at[part_chips(part), core],
        send_sem=sems.at[0, part],
        recv_sem=sems.at[1, part],
        device_id=sibling,
        device_id_type=MESH,
    )


def start_part(rows, out_ref, both_ref, part, sems):
    core, _, _ = position()
    out_ref[part_chips(part)] = packed(rows)
    pair_copy(out_ref, both_ref, part, sems).start()
    both_ref[part_chips(part), core] = out_ref[part_chips(part), core]


def send_part(out_ref, both_ref, in_ref, part, stride, sems):
    _, chip, _ = position()
    pair_copy(out_ref, both_ref, part, sems).wait()

    def body(step, _):
        pltpu.make_async_remote_copy(
            src_ref=both_ref.at[step],
            dst_ref=in_ref.at[step],
            send_sem=sems.at[2, part],
            recv_sem=sems.at[3, part],
            device_id=chip_device(lax.rem(chip + step * stride, CHIPS)),
            device_id_type=MESH,
        ).start()
        return 0

    lax.fori_loop(max(part * PART_CHIPS, 1), (part + 1) * PART_CHIPS, body, 0)
    if part == 0:
        in_ref[0] = both_ref[0]


def wait_part(in_ref, part, sem):
    wait_bytes(in_ref, PART_CHIPS - (part == 0), sem)


def wait_bytes(ref, count, sem):
    view = ref.at[pl.ds(0, count)]
    pltpu.make_async_copy(view, view, sem).wait()


SIDE = 8
GROUPS = 3
FIRST_HEAD = (0, 8, 14, HEADS)
OWNER_STRIDE = 13
OWNER_INVERSE = 5


def group_heads(g):
    return FIRST_HEAD[g + 1] - FIRST_HEAD[g]


def group_tiles(g):
    return 8 * group_heads(g)


def tiles(section):
    rows = section.shape[0]
    section = section.reshape(rows // 8, 8, C)
    halves = [section[:, None, :, :LANES], section[:, None, :, LANES:]]
    return jnp.concatenate(halves, axis=1).reshape(rows // 4, 8, LANES)


def untiled(pieces):
    pieces = pieces.reshape(-1, 2, 8, LANES)
    return jnp.concatenate([pieces[:, 0], pieces[:, 1]], axis=2).reshape(-1, C)


def block_kernel(
    feat_hbm, zorder_hbm, hilbert_hbm, wqkv_hbm, wp_hbm, og_hbm,
    out_hbm, feat_grad_hbm, qkvg_hbm, projg_hbm,
    out_ref, feat_grad_ref, qkvg_ref, projg_ref,
    feat_ref, zorder_ref, hilbert_ref, wqkv_ref, wp_ref, og_ref, oga_ref, x_ref, normed_ref,
    wqkv_t_ref, xhat_ref, rstd_ref, k_ref, v_ref, qt_ref, kt_ref, vt_ref, dot_ref,
    p_ref, ds_ref, rhs_ref, e_ref, at_ref, dqt_ref, dkt_ref, dvt_ref,
    there_out, there_both, there_in, back_out, back_both, back_in,
    part_ref, half_ref, sum_ref, chunk_in_ref, result_ref, total_ref, low_out_ref, low_in_ref,
    load_sems, there_sems, back_sems, group_sems, level_sems, store_sems,
):
    half_width = C // 2
    core, chip, sibling = position()
    barrier = pltpu.get_barrier_semaphore()
    sources = (zorder_hbm, feat_hbm, hilbert_hbm, og_hbm, wp_hbm, wqkv_hbm)
    targets = (zorder_ref, feat_ref, hilbert_ref, og_ref, wp_ref, wqkv_ref)
    loads = [
        pltpu.make_async_copy(source, target, load_sems.at[i])
        for i, (source, target) in enumerate(zip(sources, targets))
    ]
    stores = [
        pltpu.make_async_copy(source, target, store_sems.at[i])
        for i, (source, target) in enumerate((
            (out_ref, out_hbm),
            (feat_grad_ref, feat_grad_hbm),
            (qkvg_ref, qkvg_hbm),
            (projg_ref, projg_hbm),
        ))
    ]
    for load in loads:
        load.start()
    greet(barrier)
    loads[0].wait()
    there_slots = send_slots(zorder_ref)
    loads[1].wait()
    for part in range(PARTS):
        rows = dot(scatter_rows(there_slots, part), feat_ref[...])
        if part == 0:
            pl.semaphore_wait(barrier, CHIPS)
        start_part(rows, there_out, there_both, part, there_sems)
        if part:
            send_part(there_out, there_both, there_in, part - 1, STRIDE, there_sems)
    send_part(there_out, there_both, there_in, PARTS - 1, STRIDE, there_sems)

    for load in loads[2:]:
        load.wait()
    back_slots = recv_slots(hilbert_ref)
    for part in range(PARTS):
        rows = slice(part * PART_ROWS, (part + 1) * PART_ROWS)
        oga_ref[rows] = dot(scatter_rows(back_slots, part), og_ref[...]).astype(BF16)
    do_t = dot_nt(wp_ref[...], oga_ref[...]).astype(BF16).astype(F32)
    dot_ref[...] = (do_t * 0.25).astype(BF16).reshape(HEADS, HEAD_DIM, PATCH)
    wqkv_t_ref[...] = transposed(wqkv_ref[...])
    p_ref[1] = jnp.zeros((PATCH, QB), BF16)
    ds_ref[1] = jnp.zeros((PATCH, QB), BF16)
    dkt_ref[0] = jnp.zeros((HEAD_DIM, PATCH), F32)
    dvt_ref[0] = jnp.zeros((HEAD_DIM, PATCH), F32)

    for part in range(PARTS):
        wait_part(there_in, part, there_sems.at[3, part])
        rows = slice(part * PART_ROWS, (part + 1) * PART_ROWS)
        x = unpacked(there_in[part_chips(part)])
        x_ref[rows] = x
        xhat, rstd = normalize(x.astype(F32))
        xhat_ref[rows] = xhat
        rstd_ref[rows] = rstd
        normed = xhat.astype(BF16)
        normed_ref[rows] = normed
        kv = dot(normed, wqkv_ref[:, C:]).astype(BF16)
        for ref, low in ((k_ref, 0), (v_ref, C)):
            ref[0, rows] = kv[:, low : low + half_width]
            ref[1, rows] = kv[:, low + half_width : low + C]
        qkv_t = dot(wqkv_t_ref[...], transposed(normed)).astype(BF16)
        for ref, low in ((qt_ref, 0), (kt_ref, C), (vt_ref, 2 * C)):
            ref[:, :, rows] = qkv_t[low : low + C].reshape(HEADS, HEAD_DIM, PART_ROWS)

    def group_part(g):
        heads = slice(FIRST_HEAD[g], FIRST_HEAD[g + 1])
        count = group_heads(g) * HEAD_DIM

        def rows(ref):
            return ref[heads].reshape(count, PATCH).astype(BF16)

        cot = jnp.concatenate([rows(ref) for ref in (dqt_ref, dkt_ref, dvt_ref)], axis=0)
        sums = dot(cot, normed_ref[...])
        sums = [sums[i * count : (i + 1) * count] for i in range(3)]
        half = group_tiles(g) // 2
        for section, value in enumerate(sums + [dot(rows(at_ref), oga_ref[...])]):
            low = section % 2 * half
            part_ref[g, section // 2, low : low + half] = tiles(value)
        group_half(g).start()

    def group_half(g):
        count = pl.ds(0, group_tiles(g))
        return pltpu.make_async_remote_copy(
            src_ref=part_ref.at[g, 1 - core, count],
            dst_ref=half_ref.at[g, count],
            send_sem=group_sems.at[g, 0],
            recv_sem=group_sems.at[g, 1],
            device_id=sibling,
            device_id_type=MESH,
        )

    my_tile = lax.rem(chip * OWNER_INVERSE, CHIPS)

    def by_owner(g, act):
        pl.when(my_tile < group_tiles(g))(lambda: act(True))
        pl.when(my_tile >= group_tiles(g))(lambda: act(False))

    def group_scatter(g):
        group_half(g).wait()
        count = group_tiles(g)
        sum_ref[g, :count] = part_ref[g, core, :count] + half_ref[g, :count]

        def body(tile, _):
            owner = lax.rem(tile * OWNER_STRIDE, CHIPS)

            @pl.when(owner != chip)
            def _():
                pltpu.make_async_remote_copy(
                    src_ref=sum_ref.at[g, tile],
                    dst_ref=chunk_in_ref.at[g, chip],
                    send_sem=group_sems.at[g, 2],
                    recv_sem=group_sems.at[g, 3],
                    device_id=chip_device(owner),
                    device_id_type=MESH,
                ).start()

            return 0

        lax.fori_loop(0, count, body, 0)

        @pl.when(my_tile < count)
        def _():
            chunk_in_ref[g, chip] = sum_ref[g, my_tile]

    def group_gather(g):
        @pl.when(my_tile < group_tiles(g))
        def _():
            wait_bytes(chunk_in_ref.at[g], CHIPS - 1, group_sems.at[g, 3])
            result_ref[g] = jnp.sum(chunk_in_ref[g], axis=0)
            for_chips(
                lambda other, device: pltpu.make_async_remote_copy(
                    src_ref=result_ref.at[g],
                    dst_ref=total_ref.at[g, core, my_tile],
                    send_sem=group_sems.at[g, 4],
                    recv_sem=group_sems.at[g, 5],
                    device_id=device,
                    device_id_type=MESH,
                ).start()
            )
            total_ref[g, core, my_tile] = result_ref[g]

    def group_final(g):
        count = pl.ds(0, group_tiles(g))
        return pltpu.make_async_remote_copy(
            src_ref=total_ref.at[g, core, count],
            dst_ref=total_ref.at[g, core, count],
            send_sem=group_sems.at[g, 6],
            recv_sem=group_sems.at[g, 7],
            device_id=sibling,
            device_id_type=MESH,
        )

    def group_finish(g):
        def arrived(owner):
            wait_bytes(total_ref.at[g, core], group_tiles(g) - owner, group_sems.at[g, 5])

        by_owner(g, arrived)
        group_final(g).start()

    high, low = chip // SIDE, lax.rem(chip, SIDE)

    def level_copy(src, dst, to, sem):
        return pltpu.make_async_remote_copy(
            src_ref=src,
            dst_ref=dst,
            send_sem=level_sems.at[0, sem],
            recv_sem=level_sems.at[1, sem],
            device_id=chip_device(to),
            device_id_type=MESH,
        )

    def others(mine, act):
        def body(step, _):
            act(lax.rem(mine + step, SIDE))
            return 0

        lax.fori_loop(1, SIDE, body, 0)

    def level_wait(direction, sem, rows):
        view = sum_ref.at[0, pl.ds(0, (SIDE - 1) * rows)]
        pltpu.make_async_copy(view, view, level_sems.at[direction, sem]).wait()

    def run(index):
        return pl.ds(index * SIDE, SIDE)

    def scatter_high():
        group_half(0).wait()
        sum_ref[0] = part_ref[0, core] + half_ref[0]
        others(high, lambda to: level_copy(
            sum_ref.at[0, run(to)], chunk_in_ref.at[0, run(high)], to * SIDE + low, 0
        ).start())
        chunk_in_ref[0, run(high)] = sum_ref[0, run(high)]

    def scatter_low():
        level_wait(1, 0, SIDE)
        summed = chunk_in_ref[0].reshape(SIDE, SIDE, 8, LANES)
        low_out_ref[...] = jnp.sum(summed, axis=0)
        others(low, lambda to: level_copy(
            low_out_ref.at[to], low_in_ref.at[low], high * SIDE + to, 1
        ).start())
        low_in_ref[low] = low_out_ref[low]

    def gather_low():
        level_wait(1, 1, 1)
        result_ref[0] = jnp.sum(low_in_ref[...], axis=0)
        others(low, lambda to: level_copy(
            result_ref.at[0], total_ref.at[0, core, chip], high * SIDE + to, 2
        ).start())
        total_ref[0, core, chip] = result_ref[0]

    def gather_high():
        level_wait(1, 2, 1)
        others(high, lambda to: level_copy(
            total_ref.at[0, core, run(high)], total_ref.at[0, core, run(high)], to * SIDE + low, 3
        ).start())

    def gather_done():
        level_wait(1, 3, SIDE)
        group_final(0).start()

    def group_close(g):
        group_final(g).wait()
        if g == 0:
            for sem, rows in enumerate((SIDE, 1, 1, SIDE)):
                level_wait(0, sem, rows)
            return

        def sent(owner):
            wait_bytes(sum_ref.at[g], group_tiles(g) - owner, group_sems.at[g, 2])
            if owner:
                wait_bytes(sum_ref.at[g], CHIPS - 1, group_sems.at[g, 4])

        by_owner(g, sent)

    def assemble(section):
        rows = []
        for g in range(GROUPS):
            half = group_tiles(g) // 2
            low = section % 2 * half
            rows.append(untiled(total_ref[g, section // 2, low : low + half]))
        return jnp.concatenate(rows, axis=0)

    def query_side(h, block):
        ql = slice(block * QB, (block + 1) * QB)
        dqt_ref[h, :, ql] = dot(kt_ref[h], ds_ref[block]).astype(BF16)

    def value_side(h, block):
        ql = slice(block * QB, (block + 1) * QB)
        dv = dot_nt(dot_ref[h, :, ql], p_ref[block]) * 4.0
        dvt_ref[h] = dvt_ref[h] + dv if block else dv

    def key_side(h, block):
        ql = slice(block * QB, (block + 1) * QB)
        dk = dot_nt(qt_ref[h, :, ql], ds_ref[block])
        dkt_ref[h] = dkt_ref[h] + dk if block else dk

    def block_step(h, block, km, vm, before):
        half = h // 8
        ql = slice(block * QB, (block + 1) * QB)
        qt = qt_ref[pl.ds(half * 8, 8), :, ql].reshape(half_width, QB)
        tops, sums = [], []
        for j in range(PATCH // STRIP):
            s = dot(km[j * STRIP : (j + 1) * STRIP], qt)
            if j == 0:
                query_side(before, 1 - block)
            for c in range(STRIP // CHUNK):
                part = s[c * CHUNK : (c + 1) * CHUNK].reshape(CHUNK // 8, 8, QB)
                top = jnp.max(part, axis=0)
                e = jnp.exp2((part - top) * EXP_SCALE)
                e_ref[block, j * (STRIP // CHUNK) + c] = e
                tops.append(top)
                sums.append(jnp.sum(e, axis=0))
        value_side(before, 1 - block)
        peak = functools.reduce(jnp.maximum, tops)
        peak = jnp.max(peak, axis=0, keepdims=True)
        weights = [jnp.exp2((top - peak) * EXP_SCALE) for top in tops]
        total = functools.reduce(jnp.add, [a * w for a, w in zip(sums, weights)])
        inverse = 1.0 / jnp.sum(total, axis=0, keepdims=True)
        for c in range(CHUNKS):
            p = e_ref[block, c] * (weights[c] * inverse)
            p_ref[block, c * CHUNK : (c + 1) * CHUNK] = p.reshape(CHUNK, QB).astype(BF16)
        ot = dot(vt_ref[h], p_ref[block])
        key_side(before, 1 - block)
        at_ref[h, :, ql] = ot.astype(BF16)
        delta = jnp.sum(ot * dot_ref[h, :, ql].astype(F32), axis=0, keepdims=True)
        pieces = []
        for _ in range(3):
            pieces.append(delta.astype(BF16).astype(F32))
            delta = delta - pieces[-1]
        pieces.append(jnp.zeros((HEAD_DIM - 3, QB), F32))
        rhs_ref[block] = dot_ref[pl.ds(half * 8, 8), :, ql]
        rhs_ref[block, lax.rem(h + 1, 8)] = jnp.concatenate(pieces, axis=0).astype(BF16)
        dot_t = rhs_ref[block].reshape(half_width, QB)
        for j in range(PATCH // STRIP):
            dp = dot(vm[j * STRIP : (j + 1) * STRIP], dot_t)
            for c in range(STRIP // CHUNK):
                rows = slice(j * STRIP + c * CHUNK, j * STRIP + (c + 1) * CHUNK)
                p = p_ref[block, rows].astype(F32)
                ds = p * dp[c * CHUNK : (c + 1) * CHUNK]
                ds_ref[block, rows] = ds.astype(BF16)

    def head_step(h, _):
        half = h // 8
        lane = lax.broadcasted_iota(jnp.int32, (1, half_width), 1)
        mask = (lane // HEAD_DIM == h % 8).astype(F32).astype(BF16)
        beyond = lane - (h + 1) % 8 * HEAD_DIM
        minus = -((beyond >= 0) & (beyond < 3)).astype(F32).astype(BF16)
        km = k_ref[half] * mask
        vm = v_ref[half] * mask + minus
        block_step(h, 0, km, vm, jnp.maximum(h - 1, 0))
        block_step(h, 1, km, vm, h)

        steps = {
            FIRST_HEAD[1]: lambda: group_part(0),
            FIRST_HEAD[1] + 1: scatter_high,
            FIRST_HEAD[1] + 2: scatter_low,
            FIRST_HEAD[1] + 3: gather_low,
            FIRST_HEAD[1] + 4: gather_high,
            FIRST_HEAD[1] + 5: gather_done,
            FIRST_HEAD[2]: lambda: group_part(1),
        }
        for head, act in steps.items():
            pl.when(h == head)(act)

        return 0

    lax.fori_loop(0, HEADS, head_step, 0)
    query_side(HEADS - 1, 1)
    value_side(HEADS - 1, 1)
    key_side(HEADS - 1, 1)

    group_part(2)
    group_scatter(1)
    cot_t = [ref[...].reshape(C, PATCH).astype(BF16) for ref in (dqt_ref, dkt_ref, dvt_ref)]
    ng_t = dot(wqkv_ref[...], jnp.concatenate(cot_t, axis=0))
    for part in range(PARTS):
        rows = slice(part * PART_ROWS, (part + 1) * PART_ROWS)
        ng = ng_t[:, rows].T
        xhat = xhat_ref[rows]
        ng_mean = jnp.mean(ng, axis=1, keepdims=True)
        mixed = jnp.mean(ng * xhat, axis=1, keepdims=True)
        grad = oga_ref[rows].astype(F32) + rstd_ref[rows] * (ng - ng_mean - xhat * mixed)
        start_part(grad, back_out, back_both, part, back_sems)
        if part == 1:
            group_scatter(2)
        if part:
            send_part(back_out, back_both, back_in, part - 1, CHIPS - STRIDE, back_sems)
    send_part(back_out, back_both, back_in, PARTS - 1, CHIPS - STRIDE, back_sems)
    group_gather(1)
    group_gather(2)

    at = at_ref[...].reshape(C, PATCH)
    block_out = x_ref[...].astype(F32) + dot(transposed(at), wp_ref[...])
    block_out = block_out.astype(BF16)
    group_finish(1)
    slot_col = as_column(recv_slots(hilbert_ref))
    gather = [gather_columns(slot_col, part) for part in range(PARTS)]
    out_ref[...] = dot(jnp.concatenate(gather, axis=1), block_out).astype(BF16)
    stores[0].start()
    group_close(0)
    group_close(1)
    slot_col = as_column(send_slots(zorder_ref))
    gather = [gather_columns(slot_col, part) for part in range(PARTS)]
    group_finish(2)
    total = jnp.zeros((PATCH, C), F32)
    for part in range(PARTS):
        wait_part(back_in, part, back_sems.at[3, part])
        total += dot(gather[part], unpacked(back_in[part_chips(part)]))
    feat_grad_ref[...] = total.astype(BF16)
    stores[1].start()
    group_close(2)
    for section in range(3):
        qkvg_ref[:, section * C : (section + 1) * C] = assemble(section).T
    projg_ref[...] = assemble(3)
    stores[2].start()
    stores[3].start()
    for part in range(PARTS):
        wait_part(there_in, part, there_sems.at[2, part])
        wait_part(back_in, part, back_sems.at[2, part])
    for store in stores:
        store.wait()


def finish_kernel(*refs):
    sources, targets, rooms, sems = refs[:4], refs[4:8], refs[8:12], refs[12]
    ins = [
        pltpu.make_async_copy(source, room, sems.at[0, i])
        for i, (source, room) in enumerate(zip(sources, rooms))
    ]
    outs = [
        pltpu.make_async_copy(room, target, sems.at[1, i])
        for i, (room, target) in enumerate(zip(rooms, targets))
    ]
    for copy in ins:
        copy.start()
    for copy_in, copy_out in zip(ins, outs):
        copy_in.wait()
        copy_out.start()
    for copy in outs:
        copy.wait()


def on_device(features, zorder_to, hilbert_from, qkv_weight, proj_weight, out_grad):
    anywhere = pl.BlockSpec(memory_space=pl.ANY)
    out_shape = (
        jax.ShapeDtypeStruct((PATCH, C), BF16),
        jax.ShapeDtypeStruct((PATCH, C), BF16),
        jax.ShapeDtypeStruct((C, 3 * C), F32),
        jax.ShapeDtypeStruct((C, C), F32),
    )
    points = pltpu.VMEM((PATCH, C), BF16)
    index = pltpu.VMEM((1, PATCH), jnp.int32)
    halves = pltpu.VMEM((2, PATCH, C // 2), BF16)
    heads_t = pltpu.VMEM((HEADS, HEAD_DIM, PATCH), BF16)
    heads_f = pltpu.VMEM((HEADS, HEAD_DIM, PATCH), F32)
    queries = pltpu.VMEM((2, PATCH, QB), BF16)
    pieces = pltpu.VMEM((CHIPS, 2, 2 * CAP, LANES), BF16)
    both_cores = pltpu.VMEM((GROUPS, 2, CHIPS, 8, LANES), F32)
    one_core = pltpu.VMEM((GROUPS, CHIPS, 8, LANES), F32)
    results = pl.pallas_call(
        block_kernel,
        out_shape=out_shape,
        in_specs=[anywhere] * 6,
        out_specs=(anywhere,) * 4,
        scratch_shapes=[
            points, points,
            pltpu.VMEM((C, 3 * C), F32),
            pltpu.VMEM((C, C), F32),
            points, index, index,
            pltpu.VMEM((C, 3 * C), BF16),
            pltpu.VMEM((C, C), BF16),
            points, points, points, points,
            pltpu.VMEM((3 * C, C), BF16),
            pltpu.VMEM((PATCH, C), F32),
            pltpu.VMEM((PATCH, 1), F32),
            halves, halves, heads_t, heads_t, heads_t, heads_t,
            queries, queries,
            pltpu.VMEM((2, 8, HEAD_DIM, QB), BF16),
            pltpu.VMEM((2, CHUNKS, CHUNK // 8, 8, QB), F32),
            heads_t, heads_t, heads_f, heads_f,
            pieces, pieces, pieces, pieces, pieces, pieces,
            both_cores, one_core, one_core, one_core,
            pltpu.VMEM((GROUPS, 8, LANES), F32),
            both_cores,
            pltpu.VMEM((SIDE, 8, LANES), F32),
            pltpu.VMEM((SIDE, 8, LANES), F32),
            pltpu.SemaphoreType.DMA((6,)),
            pltpu.SemaphoreType.DMA((4, PARTS)),
            pltpu.SemaphoreType.DMA((4, PARTS)),
            pltpu.SemaphoreType.DMA((GROUPS, 8)),
            pltpu.SemaphoreType.DMA((2, 4)),
            pltpu.SemaphoreType.DMA((4,)),
        ],
        compiler_params=pltpu.CompilerParams(
            collective_id=0, has_side_effects=True, vmem_limit_bytes=60 * 1024 * 1024
        ),
        cost_estimate=pl.CostEstimate(
            flops=28_000_000_000, bytes_accessed=5_000_000, transcendentals=16_777_216
        ),
    )(
        features,
        zorder_to.reshape(1, PATCH),
        hilbert_from.reshape(1, PATCH),
        qkv_weight,
        proj_weight,
        out_grad,
    )
    return pl.pallas_call(
        finish_kernel,
        out_shape=out_shape,
        in_specs=[anywhere] * 4,
        out_specs=(anywhere,) * 4,
        scratch_shapes=[
            points, points,
            pltpu.VMEM((C, 3 * C), F32),
            pltpu.VMEM((C, C), F32),
            pltpu.SemaphoreType.DMA((2, 4)),
        ],
        compiler_params=pltpu.CompilerParams(vmem_limit_bytes=60 * 1024 * 1024),
        cost_estimate=pl.CostEstimate(flops=0, bytes_accessed=4_000_000, transcendentals=0),
    )(*results)


def solution(mesh):
    in_specs = (
        P(("row", "col"), None),
        P(("row", "col")),
        P(("row", "col")),
        P(),
        P(),
        P(("row", "col"), None),
    )
    out_specs = (P(("row", "col"), None), P(("row", "col"), None), P(), P())
    return jax.shard_map(
        on_device, mesh=mesh, in_specs=in_specs, out_specs=out_specs, check_vma=False
    )
```

```python
import functools

import jax
import jax.numpy as jnp
from jax import lax
from jax.experimental import pallas as pl
from jax.experimental.pallas import tpu as pltpu
from jax.sharding import PartitionSpec as P

HEADS = 16
HEAD_DIM = 16
PATCH = 1024
C = 256
QB = 512
CHUNK = 64
CHUNKS = PATCH // CHUNK
STRIP = 256
EXP_SCALE = 0.25 * 1.4426950408889634

F32 = jnp.float32
BF16 = jnp.bfloat16


def dot(a, b):
    return jnp.dot(a, b, preferred_element_type=F32)


def dot_nt(a, b):
    return lax.dot_general(a, b, (((1,), (1,)), ((), ())), preferred_element_type=F32)


def normalize(x):
    centered = x - jnp.mean(x, axis=1, keepdims=True)
    rstd = lax.rsqrt(jnp.mean(centered * centered, axis=1, keepdims=True) + 1e-05)
    return centered * rstd, rstd


def transposed(a):
    return a.astype(F32).T.astype(BF16)


MESH = pl.DeviceIdType.MESH
N_ROW = 8
N_COL = 16
DEVICES = N_ROW * N_COL
CHIPS = DEVICES // 2
CAP = PATCH // DEVICES
LANES = 128


STRIDE = 1
INVERSE_STRIDE = 1
PARTS = 4
PART_CHIPS = CHIPS // PARTS
PART_ROWS = PATCH // PARTS


def as_column(row):
    return jnp.broadcast_to(row, (LANES, PATCH)).T


def slots(key_row):
    key_col = as_column(key_row)
    ranks = []
    for block in range(PATCH // LANES):
        keys = key_row[:, block * LANES : (block + 1) * LANES]
        below = jnp.where(key_col < keys, 1.0, 0.0)
        ranks.append(jnp.sum(below, axis=0, keepdims=True))
    return jnp.concatenate(ranks, axis=1)


def scatter_rows(slot_row, part):
    row = lax.broadcasted_iota(jnp.int32, (PART_ROWS, PATCH), 0) + part * PART_ROWS
    return jnp.where(slot_row == row.astype(F32), 1.0, 0.0).astype(BF16)


def gather_columns(slot_col, part):
    lane = lax.broadcasted_iota(jnp.int32, (PATCH, LANES), 1) + part * PART_ROWS
    blocks = [
        jnp.where(slot_col == (lane + low).astype(F32), 1.0, 0.0).astype(BF16)
        for low in range(0, PART_ROWS, LANES)
    ]
    return jnp.concatenate(blocks, axis=1)


def chip_and_core(point):
    device = point // PATCH
    row, col = device // N_COL, device % N_COL
    return (row // 2) * N_COL + col, row % 2


def relative_slot(offset, core):
    return ((offset + CHIPS) * INVERSE_STRIDE % CHIPS) * 2 + core


def send_slots(zorder_ref):
    point = zorder_ref[...]
    chip, core = chip_and_core(point)
    slot = relative_slot(chip - position()[1], core)
    return slots((slot * PATCH + point % PATCH).astype(F32))


def recv_slots(hilbert_ref):
    chip, core = chip_and_core(hilbert_ref[...])
    slot = relative_slot(position()[1] - chip, core)
    local = lax.broadcasted_iota(jnp.int32, (1, PATCH), 1)
    return slots((slot * PATCH + local).astype(F32))


def packed(rows):
    rows = rows.reshape(2 * PART_CHIPS, CAP, C)
    pieces = jnp.concatenate([rows[:, :, :LANES], rows[:, :, LANES:]], axis=1).astype(BF16)
    return pieces.reshape(PART_CHIPS, 2, 2 * CAP, LANES)


def unpacked(pieces):
    pieces = pieces.reshape(2 * PART_CHIPS, 2 * CAP, LANES).astype(F32)
    left = pieces[:, :CAP].reshape(PART_ROWS, LANES)
    right = pieces[:, CAP:].reshape(PART_ROWS, LANES)
    return jnp.concatenate([left, right], axis=1).astype(BF16)


def part_chips(part):
    return slice(part * PART_CHIPS, (part + 1) * PART_CHIPS)


def position():
    row, col = lax.axis_index("row"), lax.axis_index("col")
    core = lax.rem(row, 2)
    return core, (row // 2) * N_COL + col, (row + 1 - 2 * core, col)


def chip_device(chip):
    core, _, _ = position()
    return (chip // N_COL) * 2 + core, lax.rem(chip, N_COL)


def for_chips(act):
    _, chip, _ = position()

    def body(step, _):
        other = lax.rem(chip + step * STRIDE, CHIPS)
        act(other, chip_device(other))
        return 0

    lax.fori_loop(1, CHIPS, body, 0)


def greet(barrier):
    _, _, sibling = position()
    pl.semaphore_signal(barrier, inc=1, device_id=sibling, device_id_type=MESH)
    for_chips(
        lambda _, device: pl.semaphore_signal(
            barrier, inc=1, device_id=device, device_id_type=MESH
        )
    )


def pair_copy(out_ref, both_ref, part, sems):
    core, _, sibling = position()
    return pltpu.make_async_remote_copy(
        src_ref=out_ref.at[part_chips(part), 1 - core],
        dst_ref=both_ref.at[part_chips(part), core],
        send_sem=sems.at[0, part],
        recv_sem=sems.at[1, part],
        device_id=sibling,
        device_id_type=MESH,
    )


def start_part(rows, out_ref, both_ref, part, sems):
    core, _, _ = position()
    out_ref[part_chips(part)] = packed(rows)
    pair_copy(out_ref, both_ref, part, sems).start()
    both_ref[part_chips(part), core] = out_ref[part_chips(part), core]


def send_part(out_ref, both_ref, in_ref, part, stride, sems):
    _, chip, _ = position()
    pair_copy(out_ref, both_ref, part, sems).wait()

    def body(step, _):
        pltpu.make_async_remote_copy(
            src_ref=both_ref.at[step],
            dst_ref=in_ref.at[step],
            send_sem=sems.at[2, part],
            recv_sem=sems.at[3, part],
            device_id=chip_device(lax.rem(chip + step * stride, CHIPS)),
            device_id_type=MESH,
        ).start()
        return 0

    lax.fori_loop(max(part * PART_CHIPS, 1), (part + 1) * PART_CHIPS, body, 0)
    if part == 0:
        in_ref[0] = both_ref[0]


def wait_part(in_ref, part, sem):
    wait_bytes(in_ref, PART_CHIPS - (part == 0), sem)


def wait_bytes(ref, count, sem):
    view = ref.at[pl.ds(0, count)]
    pltpu.make_async_copy(view, view, sem).wait()


SIDE = 8
GROUPS = 3
FIRST_HEAD = (0, 8, 13, HEADS)
OWNER_STRIDE = 13
OWNER_INVERSE = 5


def group_heads(g):
    return FIRST_HEAD[g + 1] - FIRST_HEAD[g]


def group_tiles(g):
    return 8 * group_heads(g)


def tiles(section):
    rows = section.shape[0]
    section = section.reshape(rows // 8, 8, C)
    halves = [section[:, None, :, :LANES], section[:, None, :, LANES:]]
    return jnp.concatenate(halves, axis=1).reshape(rows // 4, 8, LANES)


def untiled(pieces):
    pieces = pieces.reshape(-1, 2, 8, LANES)
    return jnp.concatenate([pieces[:, 0], pieces[:, 1]], axis=2).reshape(-1, C)


def block_kernel(
    feat_hbm, zorder_hbm, hilbert_hbm, wqkv_hbm, wp_hbm, og_hbm,
    out_hbm, feat_grad_hbm, qkvg_hbm, projg_hbm,
    out_ref, feat_grad_ref, qkvg_ref, projg_ref,
    feat_ref, zorder_ref, hilbert_ref, wqkv_ref, wp_ref, og_ref, oga_ref, x_ref, normed_ref,
    wqkv_t_ref, xhat_ref, rstd_ref, k_ref, v_ref, qt_ref, kt_ref, vt_ref, dot_ref,
    p_ref, ds_ref, pt_ref, dst_ref, e_ref, at_ref, dqt_ref, dkt_ref, dvt_ref,
    there_out, there_both, there_in, back_out, back_both, back_in,
    part_ref, half_ref, sum_ref, chunk_in_ref, result_ref, total_ref, low_out_ref, low_in_ref,
    load_sems, there_sems, back_sems, group_sems, level_sems, store_sems,
):
    half_width = C // 2
    core, chip, sibling = position()
    barrier = pltpu.get_barrier_semaphore()
    sources = (zorder_hbm, feat_hbm, hilbert_hbm, og_hbm, wp_hbm, wqkv_hbm)
    targets = (zorder_ref, feat_ref, hilbert_ref, og_ref, wp_ref, wqkv_ref)
    loads = [
        pltpu.make_async_copy(source, target, load_sems.at[i])
        for i, (source, target) in enumerate(zip(sources, targets))
    ]
    stores = [
        pltpu.make_async_copy(source, target, store_sems.at[i])
        for i, (source, target) in enumerate((
            (out_ref, out_hbm),
            (feat_grad_ref, feat_grad_hbm),
            (qkvg_ref, qkvg_hbm),
            (projg_ref, projg_hbm),
        ))
    ]
    for load in loads:
        load.start()
    greet(barrier)
    loads[0].wait()
    there_slots = send_slots(zorder_ref)
    loads[1].wait()
    for part in range(PARTS):
        rows = dot(scatter_rows(there_slots, part), feat_ref[...])
        if part == 0:
            pl.semaphore_wait(barrier, CHIPS)
        start_part(rows, there_out, there_both, part, there_sems)
        if part:
            send_part(there_out, there_both, there_in, part - 1, STRIDE, there_sems)
    send_part(there_out, there_both, there_in, PARTS - 1, STRIDE, there_sems)

    for load in loads[2:]:
        load.wait()
    back_slots = recv_slots(hilbert_ref)
    for part in range(PARTS):
        rows = slice(part * PART_ROWS, (part + 1) * PART_ROWS)
        oga_ref[rows] = dot(scatter_rows(back_slots, part), og_ref[...]).astype(BF16)
    do_t = dot_nt(wp_ref[...], oga_ref[...]).astype(BF16).astype(F32)
    dot_ref[...] = (do_t * 0.25).astype(BF16).reshape(HEADS, HEAD_DIM, PATCH)
    wqkv_t_ref[...] = transposed(wqkv_ref[...])
    p_ref[1] = jnp.zeros((PATCH, QB), BF16)
    ds_ref[1] = jnp.zeros((PATCH, QB), BF16)
    dkt_ref[0] = jnp.zeros((HEAD_DIM, PATCH), F32)
    dvt_ref[0] = jnp.zeros((HEAD_DIM, PATCH), F32)

    for part in range(PARTS):
        wait_part(there_in, part, there_sems.at[3, part])
        rows = slice(part * PART_ROWS, (part + 1) * PART_ROWS)
        x = unpacked(there_in[part_chips(part)])
        x_ref[rows] = x
        xhat, rstd = normalize(x.astype(F32))
        xhat_ref[rows] = xhat
        rstd_ref[rows] = rstd
        normed = xhat.astype(BF16)
        normed_ref[rows] = normed
        kv = dot(normed, wqkv_ref[:, C:]).astype(BF16)
        for ref, low in ((k_ref, 0), (v_ref, C)):
            ref[0, rows] = kv[:, low : low + half_width]
            ref[1, rows] = kv[:, low + half_width : low + C]
        qkv_t = dot(wqkv_t_ref[...], transposed(normed)).astype(BF16)
        for ref, low in ((qt_ref, 0), (kt_ref, C), (vt_ref, 2 * C)):
            ref[:, :, rows] = qkv_t[low : low + C].reshape(HEADS, HEAD_DIM, PART_ROWS)

    def group_part(g):
        heads = slice(FIRST_HEAD[g], FIRST_HEAD[g + 1])
        count = group_heads(g) * HEAD_DIM

        def rows(ref):
            return ref[heads].reshape(count, PATCH).astype(BF16)

        cot = jnp.concatenate([rows(ref) for ref in (dqt_ref, dkt_ref, dvt_ref)], axis=0)
        sums = dot(cot, normed_ref[...])
        sums = [sums[i * count : (i + 1) * count] for i in range(3)]
        half = group_tiles(g) // 2
        for section, value in enumerate(sums + [dot(rows(at_ref), oga_ref[...])]):
            low = section % 2 * half
            part_ref[g, section // 2, low : low + half] = tiles(value)
        group_half(g).start()

    def group_half(g):
        count = pl.ds(0, group_tiles(g))
        return pltpu.make_async_remote_copy(
            src_ref=part_ref.at[g, 1 - core, count],
            dst_ref=half_ref.at[g, count],
            send_sem=group_sems.at[g, 0],
            recv_sem=group_sems.at[g, 1],
            device_id=sibling,
            device_id_type=MESH,
        )

    my_tile = lax.rem(chip * OWNER_INVERSE, CHIPS)

    def by_owner(g, act):
        pl.when(my_tile < group_tiles(g))(lambda: act(True))
        pl.when(my_tile >= group_tiles(g))(lambda: act(False))

    def group_scatter(g):
        group_half(g).wait()
        count = group_tiles(g)
        sum_ref[g, :count] = part_ref[g, core, :count] + half_ref[g, :count]

        def body(tile, _):
            owner = lax.rem(tile * OWNER_STRIDE, CHIPS)

            @pl.when(owner != chip)
            def _():
                pltpu.make_async_remote_copy(
                    src_ref=sum_ref.at[g, tile],
                    dst_ref=chunk_in_ref.at[g, chip],
                    send_sem=group_sems.at[g, 2],
                    recv_sem=group_sems.at[g, 3],
                    device_id=chip_device(owner),
                    device_id_type=MESH,
                ).start()

            return 0

        lax.fori_loop(0, count, body, 0)

        @pl.when(my_tile < count)
        def _():
            chunk_in_ref[g, chip] = sum_ref[g, my_tile]

    def group_gather(g):
        @pl.when(my_tile < group_tiles(g))
        def _():
            wait_bytes(chunk_in_ref.at[g], CHIPS - 1, group_sems.at[g, 3])
            result_ref[g] = jnp.sum(chunk_in_ref[g], axis=0)
            for_chips(
                lambda other, device: pltpu.make_async_remote_copy(
                    src_ref=result_ref.at[g],
                    dst_ref=total_ref.at[g, core, my_tile],
                    send_sem=group_sems.at[g, 4],
                    recv_sem=group_sems.at[g, 5],
                    device_id=device,
                    device_id_type=MESH,
                ).start()
            )
            total_ref[g, core, my_tile] = result_ref[g]

    def group_final(g):
        count = pl.ds(0, group_tiles(g))
        return pltpu.make_async_remote_copy(
            src_ref=total_ref.at[g, core, count],
            dst_ref=total_ref.at[g, core, count],
            send_sem=group_sems.at[g, 6],
            recv_sem=group_sems.at[g, 7],
            device_id=sibling,
            device_id_type=MESH,
        )

    def group_finish(g):
        def arrived(owner):
            wait_bytes(total_ref.at[g, core], group_tiles(g) - owner, group_sems.at[g, 5])

        by_owner(g, arrived)
        group_final(g).start()

    high, low = chip // SIDE, lax.rem(chip, SIDE)

    def level_copy(src, dst, to, sem):
        return pltpu.make_async_remote_copy(
            src_ref=src,
            dst_ref=dst,
            send_sem=level_sems.at[0, sem],
            recv_sem=level_sems.at[1, sem],
            device_id=chip_device(to),
            device_id_type=MESH,
        )

    def others(mine, act):
        def body(step, _):
            act(lax.rem(mine + step, SIDE))
            return 0

        lax.fori_loop(1, SIDE, body, 0)

    def level_wait(direction, sem, rows):
        view = sum_ref.at[0, pl.ds(0, (SIDE - 1) * rows)]
        pltpu.make_async_copy(view, view, level_sems.at[direction, sem]).wait()

    def run(index):
        return pl.ds(index * SIDE, SIDE)

    def scatter_high():
        group_half(0).wait()
        sum_ref[0] = part_ref[0, core] + half_ref[0]
        others(high, lambda to: level_copy(
            sum_ref.at[0, run(to)], chunk_in_ref.at[0, run(high)], to * SIDE + low, 0
        ).start())
        chunk_in_ref[0, run(high)] = sum_ref[0, run(high)]

    def scatter_low():
        level_wait(1, 0, SIDE)
        summed = chunk_in_ref[0].reshape(SIDE, SIDE, 8, LANES)
        low_out_ref[...] = jnp.sum(summed, axis=0)
        others(low, lambda to: level_copy(
            low_out_ref.at[to], low_in_ref.at[low], high * SIDE + to, 1
        ).start())
        low_in_ref[low] = low_out_ref[low]

    def gather_low():
        level_wait(1, 1, 1)
        result_ref[0] = jnp.sum(low_in_ref[...], axis=0)
        others(low, lambda to: level_copy(
            result_ref.at[0], total_ref.at[0, core, chip], high * SIDE + to, 2
        ).start())
        total_ref[0, core, chip] = result_ref[0]

    def gather_high():
        level_wait(1, 2, 1)
        others(high, lambda to: level_copy(
            total_ref.at[0, core, run(high)], total_ref.at[0, core, run(high)], to * SIDE + low, 3
        ).start())

    def gather_done():
        level_wait(1, 3, SIDE)
        group_final(0).start()

    def group_close(g):
        group_final(g).wait()
        if g == 0:
            for sem, rows in enumerate((SIDE, 1, 1, SIDE)):
                level_wait(0, sem, rows)
            return

        def sent(owner):
            wait_bytes(sum_ref.at[g], group_tiles(g) - owner, group_sems.at[g, 2])
            if owner:
                wait_bytes(sum_ref.at[g], CHIPS - 1, group_sems.at[g, 4])

        by_owner(g, sent)

    def assemble(section):
        rows = []
        for g in range(GROUPS):
            half = group_tiles(g) // 2
            low = section % 2 * half
            rows.append(untiled(total_ref[g, section // 2, low : low + half]))
        return jnp.concatenate(rows, axis=0)

    def query_side(h, block):
        ql = slice(block * QB, (block + 1) * QB)
        dqt_ref[h, :, ql] = dot(kt_ref[h], ds_ref[block]).astype(BF16)

    def value_side(h, block):
        ql = slice(block * QB, (block + 1) * QB)
        dv = dot(dot_ref[h, :, ql], pt_ref[...]) * 4.0
        dvt_ref[h] = dvt_ref[h] + dv if block else dv

    def key_side(h, block):
        ql = slice(block * QB, (block + 1) * QB)
        dk = dot(qt_ref[h, :, ql], dst_ref[...])
        dkt_ref[h] = dkt_ref[h] + dk if block else dk

    def block_step(h, block, km, vm, before):
        half = h // 8
        ql = slice(block * QB, (block + 1) * QB)
        qt = qt_ref[pl.ds(half * 8, 8), :, ql].reshape(half_width, QB)
        dot_t = dot_ref[pl.ds(half * 8, 8), :, ql].reshape(half_width, QB)
        pt_ref[...] = p_ref[1 - block].T
        dst_ref[...] = ds_ref[1 - block].T
        tops, sums = [], []
        for j in range(PATCH // STRIP):
            s = dot(km[j * STRIP : (j + 1) * STRIP], qt)
            if j == 0:
                query_side(before, 1 - block)
            for c in range(STRIP // CHUNK):
                part = s[c * CHUNK : (c + 1) * CHUNK].reshape(CHUNK // 8, 8, QB)
                top = jnp.max(part, axis=0)
                e = jnp.exp2((part - top) * EXP_SCALE)
                e_ref[block, j * (STRIP // CHUNK) + c] = e
                tops.append(top)
                sums.append(jnp.sum(e, axis=0))
        value_side(before, 1 - block)
        peak = functools.reduce(jnp.maximum, tops)
        peak = jnp.max(peak, axis=0, keepdims=True)
        weights = [jnp.exp2((top - peak) * EXP_SCALE) for top in tops]
        total = functools.reduce(jnp.add, [a * w for a, w in zip(sums, weights)])
        inverse = 1.0 / jnp.sum(total, axis=0, keepdims=True)
        for c in range(CHUNKS):
            p = e_ref[block, c] * (weights[c] * inverse)
            p_ref[block, c * CHUNK : (c + 1) * CHUNK] = p.reshape(CHUNK, QB).astype(BF16)
        ot = dot(vt_ref[h], p_ref[block])
        key_side(before, 1 - block)
        at_ref[h, :, ql] = ot.astype(BF16)
        delta = jnp.sum(ot * dot_ref[h, :, ql].astype(F32), axis=0, keepdims=True)
        for j in range(PATCH // STRIP):
            dp = dot(vm[j * STRIP : (j + 1) * STRIP], dot_t)
            for c in range(STRIP // CHUNK):
                rows = slice(j * STRIP + c * CHUNK, j * STRIP + (c + 1) * CHUNK)
                p = p_ref[block, rows].astype(F32)
                ds = p * (dp[c * CHUNK : (c + 1) * CHUNK] - delta)
                ds_ref[block, rows] = ds.astype(BF16)

    def after_scatter():
        gather_done()
        group_scatter(1)

    def head_step(h, _):
        half = h // 8
        lane = lax.broadcasted_iota(jnp.int32, (1, half_width), 1) // HEAD_DIM
        mask = (lane == h % 8).astype(F32).astype(BF16)
        km = k_ref[half] * mask
        vm = v_ref[half] * mask
        block_step(h, 0, km, vm, jnp.maximum(h - 1, 0))
        block_step(h, 1, km, vm, h)

        steps = {
            FIRST_HEAD[1]: lambda: group_part(0),
            FIRST_HEAD[1] + 1: scatter_high,
            FIRST_HEAD[1] + 2: scatter_low,
            FIRST_HEAD[1] + 3: gather_low,
            FIRST_HEAD[1] + 4: gather_high,
            FIRST_HEAD[2]: lambda: group_part(1),
            FIRST_HEAD[2] + 1: after_scatter,
            FIRST_HEAD[2] + 2: lambda: group_gather(1),
        }
        for head, act in steps.items():
            pl.when(h == head)(act)

        return 0

    lax.fori_loop(0, HEADS, head_step, 0)
    pt_ref[...] = p_ref[1].T
    dst_ref[...] = ds_ref[1].T
    query_side(HEADS - 1, 1)
    value_side(HEADS - 1, 1)
    key_side(HEADS - 1, 1)

    group_part(2)
    cot_t = [ref[...].reshape(C, PATCH).astype(BF16) for ref in (dqt_ref, dkt_ref, dvt_ref)]
    ng_t = dot(wqkv_ref[...], jnp.concatenate(cot_t, axis=0))
    for part in range(PARTS):
        rows = slice(part * PART_ROWS, (part + 1) * PART_ROWS)
        ng = ng_t[:, rows].T
        xhat = xhat_ref[rows]
        ng_mean = jnp.mean(ng, axis=1, keepdims=True)
        mixed = jnp.mean(ng * xhat, axis=1, keepdims=True)
        grad = oga_ref[rows].astype(F32) + rstd_ref[rows] * (ng - ng_mean - xhat * mixed)
        start_part(grad, back_out, back_both, part, back_sems)
        if part == 1:
            group_scatter(2)
        if part:
            send_part(back_out, back_both, back_in, part - 1, CHIPS - STRIDE, back_sems)
    send_part(back_out, back_both, back_in, PARTS - 1, CHIPS - STRIDE, back_sems)
    group_gather(2)

    at = at_ref[...].reshape(C, PATCH)
    block_out = x_ref[...].astype(F32) + dot(transposed(at), wp_ref[...])
    block_out = block_out.astype(BF16)
    group_finish(1)
    slot_col = as_column(recv_slots(hilbert_ref))
    gather = [gather_columns(slot_col, part) for part in range(PARTS)]
    out_ref[...] = dot(jnp.concatenate(gather, axis=1), block_out).astype(BF16)
    stores[0].start()
    group_close(0)
    group_close(1)
    slot_col = as_column(send_slots(zorder_ref))
    gather = [gather_columns(slot_col, part) for part in range(PARTS)]
    group_finish(2)
    total = jnp.zeros((PATCH, C), F32)
    for part in range(PARTS):
        wait_part(back_in, part, back_sems.at[3, part])
        total += dot(gather[part], unpacked(back_in[part_chips(part)]))
    feat_grad_ref[...] = total.astype(BF16)
    stores[1].start()
    group_close(2)
    for section in range(3):
        qkvg_ref[:, section * C : (section + 1) * C] = assemble(section).T
    projg_ref[...] = assemble(3)
    stores[2].start()
    stores[3].start()
    for part in range(PARTS):
        wait_part(there_in, part, there_sems.at[2, part])
        wait_part(back_in, part, back_sems.at[2, part])
    for store in stores:
        store.wait()


def finish_kernel(*refs):
    sources, targets, rooms, sems = refs[:4], refs[4:8], refs[8:12], refs[12]
    ins = [
        pltpu.make_async_copy(source, room, sems.at[0, i])
        for i, (source, room) in enumerate(zip(sources, rooms))
    ]
    outs = [
        pltpu.make_async_copy(room, target, sems.at[1, i])
        for i, (room, target) in enumerate(zip(rooms, targets))
    ]
    for copy in ins:
        copy.start()
    for copy_in, copy_out in zip(ins, outs):
        copy_in.wait()
        copy_out.start()
    for copy in outs:
        copy.wait()


def on_device(features, zorder_to, hilbert_from, qkv_weight, proj_weight, out_grad):
    anywhere = pl.BlockSpec(memory_space=pl.ANY)
    out_shape = (
        jax.ShapeDtypeStruct((PATCH, C), BF16),
        jax.ShapeDtypeStruct((PATCH, C), BF16),
        jax.ShapeDtypeStruct((C, 3 * C), F32),
        jax.ShapeDtypeStruct((C, C), F32),
    )
    points = pltpu.VMEM((PATCH, C), BF16)
    index = pltpu.VMEM((1, PATCH), jnp.int32)
    halves = pltpu.VMEM((2, PATCH, C // 2), BF16)
    heads_t = pltpu.VMEM((HEADS, HEAD_DIM, PATCH), BF16)
    heads_f = pltpu.VMEM((HEADS, HEAD_DIM, PATCH), F32)
    queries = pltpu.VMEM((2, PATCH, QB), BF16)
    pieces = pltpu.VMEM((CHIPS, 2, 2 * CAP, LANES), BF16)
    both_cores = pltpu.VMEM((GROUPS, 2, CHIPS, 8, LANES), F32)
    one_core = pltpu.VMEM((GROUPS, CHIPS, 8, LANES), F32)
    results = pl.pallas_call(
        block_kernel,
        out_shape=out_shape,
        in_specs=[anywhere] * 6,
        out_specs=(anywhere,) * 4,
        scratch_shapes=[
            points, points,
            pltpu.VMEM((C, 3 * C), F32),
            pltpu.VMEM((C, C), F32),
            points, index, index,
            pltpu.VMEM((C, 3 * C), BF16),
            pltpu.VMEM((C, C), BF16),
            points, points, points, points,
            pltpu.VMEM((3 * C, C), BF16),
            pltpu.VMEM((PATCH, C), F32),
            pltpu.VMEM((PATCH, 1), F32),
            halves, halves, heads_t, heads_t, heads_t, heads_t,
            queries, queries,
            pltpu.VMEM((QB, PATCH), BF16),
            pltpu.VMEM((QB, PATCH), BF16),
            pltpu.VMEM((2, CHUNKS, CHUNK // 8, 8, QB), F32),
            heads_t, heads_t, heads_f, heads_f,
            pieces, pieces, pieces, pieces, pieces, pieces,
            both_cores, one_core, one_core, one_core,
            pltpu.VMEM((GROUPS, 8, LANES), F32),
            both_cores,
            pltpu.VMEM((SIDE, 8, LANES), F32),
            pltpu.VMEM((SIDE, 8, LANES), F32),
            pltpu.SemaphoreType.DMA((6,)),
            pltpu.SemaphoreType.DMA((4, PARTS)),
            pltpu.SemaphoreType.DMA((4, PARTS)),
            pltpu.SemaphoreType.DMA((GROUPS, 8)),
            pltpu.SemaphoreType.DMA((2, 4)),
            pltpu.SemaphoreType.DMA((4,)),
        ],
        compiler_params=pltpu.CompilerParams(
            collective_id=0, has_side_effects=True, vmem_limit_bytes=60 * 1024 * 1024
        ),
        cost_estimate=pl.CostEstimate(
            flops=28_000_000_000, bytes_accessed=5_000_000, transcendentals=16_777_216
        ),
    )(
        features,
        zorder_to.reshape(1, PATCH),
        hilbert_from.reshape(1, PATCH),
        qkv_weight,
        proj_weight,
        out_grad,
    )
    return pl.pallas_call(
        finish_kernel,
        out_shape=out_shape,
        in_specs=[anywhere] * 4,
        out_specs=(anywhere,) * 4,
        scratch_shapes=[
            points, points,
            pltpu.VMEM((C, 3 * C), F32),
            pltpu.VMEM((C, C), F32),
            pltpu.SemaphoreType.DMA((2, 4)),
        ],
        compiler_params=pltpu.CompilerParams(vmem_limit_bytes=60 * 1024 * 1024),
        cost_estimate=pl.CostEstimate(flops=0, bytes_accessed=4_000_000, transcendentals=0),
    )(*results)


def solution(mesh):
    in_specs = (
        P(("row", "col"), None),
        P(("row", "col")),
        P(("row", "col")),
        P(),
        P(),
        P(("row", "col"), None),
    )
    out_specs = (P(("row", "col"), None), P(("row", "col"), None), P(), P())
    return jax.shard_map(
        on_device, mesh=mesh, in_specs=in_specs, out_specs=out_specs, check_vma=False
    )
```

```python
import functools

import jax
import jax.numpy as jnp
from jax import lax
from jax.experimental import pallas as pl
from jax.experimental.pallas import tpu as pltpu
from jax.sharding import PartitionSpec as P

HEADS = 16
HEAD_DIM = 16
PATCH = 1024
C = 256
QB = 1024
CHUNK = 32
CHUNKS = PATCH // CHUNK
STRIP = 256
EXP_SCALE = 0.25 * 1.4426950408889634

F32 = jnp.float32
BF16 = jnp.bfloat16


def dot(a, b):
    return jnp.dot(a, b, preferred_element_type=F32)


def dot_nt(a, b):
    return lax.dot_general(a, b, (((1,), (1,)), ((), ())), preferred_element_type=F32)


def normalize(x):
    centered = x - jnp.mean(x, axis=1, keepdims=True)
    rstd = lax.rsqrt(jnp.mean(centered * centered, axis=1, keepdims=True) + 1e-05)
    return centered * rstd, rstd


def transposed(a):
    return a.astype(F32).T.astype(BF16)


MESH = pl.DeviceIdType.MESH
N_ROW = 8
N_COL = 16
DEVICES = N_ROW * N_COL
CHIPS = DEVICES // 2
CAP = PATCH // DEVICES
LANES = 128


STRIDE = 1
INVERSE_STRIDE = 1
PARTS = 4
PART_CHIPS = CHIPS // PARTS
PART_ROWS = PATCH // PARTS


def as_column(row):
    return jnp.broadcast_to(row, (LANES, PATCH)).T


def slots(key_row):
    key_col = as_column(key_row)
    ranks = []
    for block in range(PATCH // LANES):
        keys = key_row[:, block * LANES : (block + 1) * LANES]
        below = jnp.where(key_col < keys, 1.0, 0.0)
        ranks.append(jnp.sum(below, axis=0, keepdims=True))
    return jnp.concatenate(ranks, axis=1)


def scatter_rows(slot_row, part):
    row = lax.broadcasted_iota(jnp.int32, (PART_ROWS, PATCH), 0) + part * PART_ROWS
    return jnp.where(slot_row == row.astype(F32), 1.0, 0.0).astype(BF16)


def gather_columns(slot_col, part):
    lane = lax.broadcasted_iota(jnp.int32, (PATCH, LANES), 1) + part * PART_ROWS
    blocks = [
        jnp.where(slot_col == (lane + low).astype(F32), 1.0, 0.0).astype(BF16)
        for low in range(0, PART_ROWS, LANES)
    ]
    return jnp.concatenate(blocks, axis=1)


def chip_and_core(point):
    device = point // PATCH
    row, col = device // N_COL, device % N_COL
    return (row // 2) * N_COL + col, row % 2


def relative_slot(offset, core):
    return ((offset + CHIPS) * INVERSE_STRIDE % CHIPS) * 2 + core


def send_slots(zorder_ref):
    point = zorder_ref[...]
    chip, core = chip_and_core(point)
    slot = relative_slot(chip - position()[1], core)
    return slots((slot * PATCH + point % PATCH).astype(F32))


def recv_slots(hilbert_ref):
    chip, core = chip_and_core(hilbert_ref[...])
    slot = relative_slot(position()[1] - chip, core)
    local = lax.broadcasted_iota(jnp.int32, (1, PATCH), 1)
    return slots((slot * PATCH + local).astype(F32))


def packed(rows):
    rows = rows.reshape(2 * PART_CHIPS, CAP, C)
    pieces = jnp.concatenate([rows[:, :, :LANES], rows[:, :, LANES:]], axis=1).astype(BF16)
    return pieces.reshape(PART_CHIPS, 2, 2 * CAP, LANES)


def unpacked(pieces):
    pieces = pieces.reshape(2 * PART_CHIPS, 2 * CAP, LANES).astype(F32)
    left = pieces[:, :CAP].reshape(PART_ROWS, LANES)
    right = pieces[:, CAP:].reshape(PART_ROWS, LANES)
    return jnp.concatenate([left, right], axis=1).astype(BF16)


def part_chips(part):
    return slice(part * PART_CHIPS, (part + 1) * PART_CHIPS)


def position():
    row, col = lax.axis_index("row"), lax.axis_index("col")
    core = lax.rem(row, 2)
    return core, (row // 2) * N_COL + col, (row + 1 - 2 * core, col)


def chip_device(chip):
    core, _, _ = position()
    return (chip // N_COL) * 2 + core, lax.rem(chip, N_COL)


def for_chips(act):
    _, chip, _ = position()

    def body(step, _):
        other = lax.rem(chip + step * STRIDE, CHIPS)
        act(other, chip_device(other))
        return 0

    lax.fori_loop(1, CHIPS, body, 0)


def greet(barrier):
    _, _, sibling = position()
    pl.semaphore_signal(barrier, inc=1, device_id=sibling, device_id_type=MESH)
    for_chips(
        lambda _, device: pl.semaphore_signal(
            barrier, inc=1, device_id=device, device_id_type=MESH
        )
    )


def pair_copy(out_ref, both_ref, part, sems):
    core, _, sibling = position()
    return pltpu.make_async_remote_copy(
        src_ref=out_ref.at[part_chips(part), 1 - core],
        dst_ref=both_ref.at[part_chips(part), core],
        send_sem=sems.at[0, part],
        recv_sem=sems.at[1, part],
        device_id=sibling,
        device_id_type=MESH,
    )


def start_part(rows, out_ref, both_ref, part, sems):
    core, _, _ = position()
    out_ref[part_chips(part)] = packed(rows)
    pair_copy(out_ref, both_ref, part, sems).start()
    both_ref[part_chips(part), core] = out_ref[part_chips(part), core]


def send_part(out_ref, both_ref, in_ref, part, stride, sems):
    _, chip, _ = position()
    pair_copy(out_ref, both_ref, part, sems).wait()

    def body(step, _):
        pltpu.make_async_remote_copy(
            src_ref=both_ref.at[step],
            dst_ref=in_ref.at[step],
            send_sem=sems.at[2, part],
            recv_sem=sems.at[3, part],
            device_id=chip_device(lax.rem(chip + step * stride, CHIPS)),
            device_id_type=MESH,
        ).start()
        return 0

    lax.fori_loop(max(part * PART_CHIPS, 1), (part + 1) * PART_CHIPS, body, 0)
    if part == 0:
        in_ref[0] = both_ref[0]


def wait_part(in_ref, part, sem):
    wait_bytes(in_ref, PART_CHIPS - (part == 0), sem)


def wait_bytes(ref, count, sem):
    view = ref.at[pl.ds(0, count)]
    pltpu.make_async_copy(view, view, sem).wait()


SIDE = 8
GROUPS = 3
FIRST_HEAD = (0, 8, 13, HEADS)
OWNER_STRIDE = 13
OWNER_INVERSE = 5


def group_heads(g):
    return FIRST_HEAD[g + 1] - FIRST_HEAD[g]


def group_tiles(g):
    return 8 * group_heads(g)


def tiles(section):
    rows = section.shape[0]
    section = section.reshape(rows // 8, 8, C)
    halves = [section[:, None, :, :LANES], section[:, None, :, LANES:]]
    return jnp.concatenate(halves, axis=1).reshape(rows // 4, 8, LANES)


def untiled(pieces):
    pieces = pieces.reshape(-1, 2, 8, LANES)
    return jnp.concatenate([pieces[:, 0], pieces[:, 1]], axis=2).reshape(-1, C)


def block_kernel(
    feat_hbm, zorder_hbm, hilbert_hbm, wqkv_hbm, wp_hbm, og_hbm,
    out_hbm, feat_grad_hbm, qkvg_hbm, projg_hbm,
    out_ref, feat_grad_ref, qkvg_ref, projg_ref,
    feat_ref, zorder_ref, hilbert_ref, wqkv_ref, wp_ref, og_ref, oga_ref, x_ref, normed_ref,
    wqkv_t_ref, xhat_ref, rstd_ref, k_ref, v_ref, qt_ref, kt_ref, vt_ref, dot_ref,
    p_ref, ds_ref, e_ref, at_ref, dqt_ref, dkt_ref, dvt_ref,
    there_out, there_both, there_in, back_out, back_both, back_in,
    part_ref, half_ref, sum_ref, chunk_in_ref, result_ref, total_ref, low_out_ref, low_in_ref,
    load_sems, there_sems, back_sems, group_sems, level_sems, store_sems,
):
    half_width = C // 2
    core, chip, sibling = position()
    barrier = pltpu.get_barrier_semaphore()
    sources = (zorder_hbm, feat_hbm, hilbert_hbm, og_hbm, wp_hbm, wqkv_hbm)
    targets = (zorder_ref, feat_ref, hilbert_ref, og_ref, wp_ref, wqkv_ref)
    loads = [
        pltpu.make_async_copy(source, target, load_sems.at[i])
        for i, (source, target) in enumerate(zip(sources, targets))
    ]
    stores = [
        pltpu.make_async_copy(source, target, store_sems.at[i])
        for i, (source, target) in enumerate((
            (out_ref, out_hbm),
            (feat_grad_ref, feat_grad_hbm),
            (qkvg_ref, qkvg_hbm),
            (projg_ref, projg_hbm),
        ))
    ]
    for load in loads:
        load.start()
    greet(barrier)
    loads[0].wait()
    there_slots = send_slots(zorder_ref)
    loads[1].wait()
    for part in range(PARTS):
        rows = dot(scatter_rows(there_slots, part), feat_ref[...])
        if part == 0:
            pl.semaphore_wait(barrier, CHIPS)
        start_part(rows, there_out, there_both, part, there_sems)
        if part:
            send_part(there_out, there_both, there_in, part - 1, STRIDE, there_sems)
    send_part(there_out, there_both, there_in, PARTS - 1, STRIDE, there_sems)

    for load in loads[2:]:
        load.wait()
    back_slots = recv_slots(hilbert_ref)
    for part in range(PARTS):
        rows = slice(part * PART_ROWS, (part + 1) * PART_ROWS)
        oga_ref[rows] = dot(scatter_rows(back_slots, part), og_ref[...]).astype(BF16)
    do_t = dot_nt(wp_ref[...], oga_ref[...]).astype(BF16).astype(F32)
    dot_ref[...] = (do_t * 0.25).astype(BF16).reshape(HEADS, HEAD_DIM, PATCH)
    wqkv_t_ref[...] = transposed(wqkv_ref[...])
    p_ref[1] = jnp.zeros((PATCH, QB), BF16)
    ds_ref[1] = jnp.zeros((PATCH, QB), BF16)

    for part in range(PARTS):
        wait_part(there_in, part, there_sems.at[3, part])
        rows = slice(part * PART_ROWS, (part + 1) * PART_ROWS)
        x = unpacked(there_in[part_chips(part)])
        x_ref[rows] = x
        xhat, rstd = normalize(x.astype(F32))
        xhat_ref[rows] = xhat
        rstd_ref[rows] = rstd
        normed = xhat.astype(BF16)
        normed_ref[rows] = normed
        kv = dot(normed, wqkv_ref[:, C:]).astype(BF16)
        for ref, low in ((k_ref, 0), (v_ref, C)):
            ref[0, rows] = kv[:, low : low + half_width]
            ref[1, rows] = kv[:, low + half_width : low + C]
        qkv_t = dot(wqkv_t_ref[...], transposed(normed)).astype(BF16)
        for ref, low in ((qt_ref, 0), (kt_ref, C), (vt_ref, 2 * C)):
            ref[:, :, rows] = qkv_t[low : low + C].reshape(HEADS, HEAD_DIM, PART_ROWS)

    def group_part(g):
        heads = slice(FIRST_HEAD[g], FIRST_HEAD[g + 1])
        count = group_heads(g) * HEAD_DIM

        def rows(ref):
            return ref[heads].reshape(count, PATCH).astype(BF16)

        cot = jnp.concatenate([rows(ref) for ref in (dqt_ref, dkt_ref, dvt_ref)], axis=0)
        sums = dot(cot, normed_ref[...])
        sums = [sums[i * count : (i + 1) * count] for i in range(3)]
        half = group_tiles(g) // 2
        for section, value in enumerate(sums + [dot(rows(at_ref), oga_ref[...])]):
            low = section % 2 * half
            part_ref[g, section // 2, low : low + half] = tiles(value)
        group_half(g).start()

    def group_half(g):
        count = pl.ds(0, group_tiles(g))
        return pltpu.make_async_remote_copy(
            src_ref=part_ref.at[g, 1 - core, count],
            dst_ref=half_ref.at[g, count],
            send_sem=group_sems.at[g, 0],
            recv_sem=group_sems.at[g, 1],
            device_id=sibling,
            device_id_type=MESH,
        )

    my_tile = lax.rem(chip * OWNER_INVERSE, CHIPS)

    def by_owner(g, act):
        pl.when(my_tile < group_tiles(g))(lambda: act(True))
        pl.when(my_tile >= group_tiles(g))(lambda: act(False))

    def group_scatter(g):
        group_half(g).wait()
        count = group_tiles(g)
        sum_ref[g, :count] = part_ref[g, core, :count] + half_ref[g, :count]

        def body(tile, _):
            owner = lax.rem(tile * OWNER_STRIDE, CHIPS)

            @pl.when(owner != chip)
            def _():
                pltpu.make_async_remote_copy(
                    src_ref=sum_ref.at[g, tile],
                    dst_ref=chunk_in_ref.at[g, chip],
                    send_sem=group_sems.at[g, 2],
                    recv_sem=group_sems.at[g, 3],
                    device_id=chip_device(owner),
                    device_id_type=MESH,
                ).start()

            return 0

        lax.fori_loop(0, count, body, 0)

        @pl.when(my_tile < count)
        def _():
            chunk_in_ref[g, chip] = sum_ref[g, my_tile]

    def group_gather(g):
        @pl.when(my_tile < group_tiles(g))
        def _():
            wait_bytes(chunk_in_ref.at[g], CHIPS - 1, group_sems.at[g, 3])
            result_ref[g] = jnp.sum(chunk_in_ref[g], axis=0)
            for_chips(
                lambda other, device: pltpu.make_async_remote_copy(
                    src_ref=result_ref.at[g],
                    dst_ref=total_ref.at[g, core, my_tile],
                    send_sem=group_sems.at[g, 4],
                    recv_sem=group_sems.at[g, 5],
                    device_id=device,
                    device_id_type=MESH,
                ).start()
            )
            total_ref[g, core, my_tile] = result_ref[g]

    def group_final(g):
        count = pl.ds(0, group_tiles(g))
        return pltpu.make_async_remote_copy(
            src_ref=total_ref.at[g, core, count],
            dst_ref=total_ref.at[g, core, count],
            send_sem=group_sems.at[g, 6],
            recv_sem=group_sems.at[g, 7],
            device_id=sibling,
            device_id_type=MESH,
        )

    def group_finish(g):
        def arrived(owner):
            wait_bytes(total_ref.at[g, core], group_tiles(g) - owner, group_sems.at[g, 5])

        by_owner(g, arrived)
        group_final(g).start()

    high, low = chip // SIDE, lax.rem(chip, SIDE)

    def level_copy(src, dst, to, sem):
        return pltpu.make_async_remote_copy(
            src_ref=src,
            dst_ref=dst,
            send_sem=level_sems.at[0, sem],
            recv_sem=level_sems.at[1, sem],
            device_id=chip_device(to),
            device_id_type=MESH,
        )

    def others(mine, act):
        def body(step, _):
            act(lax.rem(mine + step, SIDE))
            return 0

        lax.fori_loop(1, SIDE, body, 0)

    def level_wait(direction, sem, rows):
        view = sum_ref.at[0, pl.ds(0, (SIDE - 1) * rows)]
        pltpu.make_async_copy(view, view, level_sems.at[direction, sem]).wait()

    def run(index):
        return pl.ds(index * SIDE, SIDE)

    def scatter_high():
        group_half(0).wait()
        sum_ref[0] = part_ref[0, core] + half_ref[0]
        others(high, lambda to: level_copy(
            sum_ref.at[0, run(to)], chunk_in_ref.at[0, run(high)], to * SIDE + low, 0
        ).start())
        chunk_in_ref[0, run(high)] = sum_ref[0, run(high)]

    def scatter_low():
        level_wait(1, 0, SIDE)
        summed = chunk_in_ref[0].reshape(SIDE, SIDE, 8, LANES)
        low_out_ref[...] = jnp.sum(summed, axis=0)
        others(low, lambda to: level_copy(
            low_out_ref.at[to], low_in_ref.at[low], high * SIDE + to, 1
        ).start())
        low_in_ref[low] = low_out_ref[low]

    def gather_low():
        level_wait(1, 1, 1)
        result_ref[0] = jnp.sum(low_in_ref[...], axis=0)
        others(low, lambda to: level_copy(
            result_ref.at[0], total_ref.at[0, core, chip], high * SIDE + to, 2
        ).start())
        total_ref[0, core, chip] = result_ref[0]

    def gather_high():
        level_wait(1, 2, 1)
        others(high, lambda to: level_copy(
            total_ref.at[0, core, run(high)], total_ref.at[0, core, run(high)], to * SIDE + low, 3
        ).start())

    def gather_done():
        level_wait(1, 3, SIDE)
        group_final(0).start()

    def group_close(g):
        group_final(g).wait()
        if g == 0:
            for sem, rows in enumerate((SIDE, 1, 1, SIDE)):
                level_wait(0, sem, rows)
            return

        def sent(owner):
            wait_bytes(sum_ref.at[g], group_tiles(g) - owner, group_sems.at[g, 2])
            if owner:
                wait_bytes(sum_ref.at[g], CHIPS - 1, group_sems.at[g, 4])

        by_owner(g, sent)

    def assemble(section):
        rows = []
        for g in range(GROUPS):
            half = group_tiles(g) // 2
            low = section % 2 * half
            rows.append(untiled(total_ref[g, section // 2, low : low + half]))
        return jnp.concatenate(rows, axis=0)

    def query_side(h, slot):
        dqt_ref[h] = dot(kt_ref[h], ds_ref[slot]).astype(BF16)

    def value_side(h, slot):
        dvt_ref[h] = dot_nt(dot_ref[h], p_ref[slot]) * 4.0

    def key_side(h, slot):
        dkt_ref[h] = dot_nt(qt_ref[h], ds_ref[slot])

    def block_step(h, block, km, vm, before):
        half = h // 8
        ql = slice(0, QB)
        qt = qt_ref[pl.ds(half * 8, 8), :, ql].reshape(half_width, QB)
        dot_t = dot_ref[pl.ds(half * 8, 8), :, ql].reshape(half_width, QB)
        tops, sums = [], []
        for j in range(PATCH // STRIP):
            s = dot(km[j * STRIP : (j + 1) * STRIP], qt)
            if j == 0:
                query_side(before, 1 - block)
            for c in range(STRIP // CHUNK):
                part = s[c * CHUNK : (c + 1) * CHUNK].reshape(CHUNK // 8, 8, QB)
                top = jnp.max(part, axis=0)
                e = jnp.exp2((part - top) * EXP_SCALE)
                e_ref[block, j * (STRIP // CHUNK) + c] = e
                tops.append(top)
                sums.append(jnp.sum(e, axis=0))
        value_side(before, 1 - block)
        peak = functools.reduce(jnp.maximum, tops)
        peak = jnp.max(peak, axis=0, keepdims=True)
        weights = [jnp.exp2((top - peak) * EXP_SCALE) for top in tops]
        total = functools.reduce(jnp.add, [a * w for a, w in zip(sums, weights)])
        inverse = 1.0 / jnp.sum(total, axis=0, keepdims=True)
        for c in range(CHUNKS):
            p = e_ref[block, c] * (weights[c] * inverse)
            p_ref[block, c * CHUNK : (c + 1) * CHUNK] = p.reshape(CHUNK, QB).astype(BF16)
        ot = dot(vt_ref[h], p_ref[block])
        key_side(before, 1 - block)
        at_ref[h, :, ql] = ot.astype(BF16)
        delta = jnp.sum(ot * dot_ref[h, :, ql].astype(F32), axis=0, keepdims=True)
        for j in range(PATCH // STRIP):
            dp = dot(vm[j * STRIP : (j + 1) * STRIP], dot_t)
            for c in range(STRIP // CHUNK):
                rows = slice(j * STRIP + c * CHUNK, j * STRIP + (c + 1) * CHUNK)
                p = p_ref[block, rows].astype(F32)
                ds = p * (dp[c * CHUNK : (c + 1) * CHUNK] - delta)
                ds_ref[block, rows] = ds.astype(BF16)

    def after_scatter():
        gather_done()
        group_scatter(1)

    def head_step(pair, _):
        for slot in range(2):
            h = pair * 2 + slot
            half = h // 8
            lane = lax.broadcasted_iota(jnp.int32, (1, half_width), 1) // HEAD_DIM
            mask = (lane == h % 8).astype(F32).astype(BF16)
            km = k_ref[half] * mask
            vm = v_ref[half] * mask
            block_step(h, slot, km, vm, jnp.maximum(h - 1, 0))
            group_steps(h, slot)
        return 0

    def group_steps(h, slot):
        steps = {
            FIRST_HEAD[1]: lambda: group_part(0),
            FIRST_HEAD[1] + 1: scatter_high,
            FIRST_HEAD[1] + 2: scatter_low,
            FIRST_HEAD[1] + 3: gather_low,
            FIRST_HEAD[1] + 4: gather_high,
            FIRST_HEAD[2]: lambda: group_part(1),
            FIRST_HEAD[2] + 1: after_scatter,
            FIRST_HEAD[2] + 2: lambda: group_gather(1),
        }
        for head, act in steps.items():
            if head % 2 == slot:
                pl.when(h == head)(act)

    lax.fori_loop(0, HEADS // 2, head_step, 0)
    query_side(HEADS - 1, 1)
    value_side(HEADS - 1, 1)
    key_side(HEADS - 1, 1)

    group_part(2)
    cot_t = [ref[...].reshape(C, PATCH).astype(BF16) for ref in (dqt_ref, dkt_ref, dvt_ref)]
    ng_t = dot(wqkv_ref[...], jnp.concatenate(cot_t, axis=0))
    for part in range(PARTS):
        rows = slice(part * PART_ROWS, (part + 1) * PART_ROWS)
        ng = ng_t[:, rows].T
        xhat = xhat_ref[rows]
        ng_mean = jnp.mean(ng, axis=1, keepdims=True)
        mixed = jnp.mean(ng * xhat, axis=1, keepdims=True)
        grad = oga_ref[rows].astype(F32) + rstd_ref[rows] * (ng - ng_mean - xhat * mixed)
        start_part(grad, back_out, back_both, part, back_sems)
        if part == 1:
            group_scatter(2)
        if part:
            send_part(back_out, back_both, back_in, part - 1, CHIPS - STRIDE, back_sems)
    send_part(back_out, back_both, back_in, PARTS - 1, CHIPS - STRIDE, back_sems)
    group_gather(2)

    at = at_ref[...].reshape(C, PATCH)
    block_out = x_ref[...].astype(F32) + dot(transposed(at), wp_ref[...])
    block_out = block_out.astype(BF16)
    group_finish(1)
    slot_col = as_column(recv_slots(hilbert_ref))
    gather = [gather_columns(slot_col, part) for part in range(PARTS)]
    out_ref[...] = dot(jnp.concatenate(gather, axis=1), block_out).astype(BF16)
    stores[0].start()
    group_close(0)
    group_close(1)
    slot_col = as_column(send_slots(zorder_ref))
    gather = [gather_columns(slot_col, part) for part in range(PARTS)]
    group_finish(2)
    total = jnp.zeros((PATCH, C), F32)
    for part in range(PARTS):
        wait_part(back_in, part, back_sems.at[3, part])
        total += dot(gather[part], unpacked(back_in[part_chips(part)]))
    feat_grad_ref[...] = total.astype(BF16)
    stores[1].start()
    group_close(2)
    for section in range(3):
        qkvg_ref[:, section * C : (section + 1) * C] = assemble(section).T
    projg_ref[...] = assemble(3)
    stores[2].start()
    stores[3].start()
    for part in range(PARTS):
        wait_part(there_in, part, there_sems.at[2, part])
        wait_part(back_in, part, back_sems.at[2, part])
    for store in stores:
        store.wait()


def finish_kernel(*refs):
    sources, targets, rooms, sems = refs[:4], refs[4:8], refs[8:12], refs[12]
    ins = [
        pltpu.make_async_copy(source, room, sems.at[0, i])
        for i, (source, room) in enumerate(zip(sources, rooms))
    ]
    outs = [
        pltpu.make_async_copy(room, target, sems.at[1, i])
        for i, (room, target) in enumerate(zip(rooms, targets))
    ]
    for copy in ins:
        copy.start()
    for copy_in, copy_out in zip(ins, outs):
        copy_in.wait()
        copy_out.start()
    for copy in outs:
        copy.wait()


def on_device(features, zorder_to, hilbert_from, qkv_weight, proj_weight, out_grad):
    anywhere = pl.BlockSpec(memory_space=pl.ANY)
    out_shape = (
        jax.ShapeDtypeStruct((PATCH, C), BF16),
        jax.ShapeDtypeStruct((PATCH, C), BF16),
        jax.ShapeDtypeStruct((C, 3 * C), F32),
        jax.ShapeDtypeStruct((C, C), F32),
    )
    points = pltpu.VMEM((PATCH, C), BF16)
    index = pltpu.VMEM((1, PATCH), jnp.int32)
    halves = pltpu.VMEM((2, PATCH, C // 2), BF16)
    heads_t = pltpu.VMEM((HEADS, HEAD_DIM, PATCH), BF16)
    heads_f = pltpu.VMEM((HEADS, HEAD_DIM, PATCH), F32)
    queries = pltpu.VMEM((2, PATCH, QB), BF16)
    pieces = pltpu.VMEM((CHIPS, 2, 2 * CAP, LANES), BF16)
    both_cores = pltpu.VMEM((GROUPS, 2, CHIPS, 8, LANES), F32)
    one_core = pltpu.VMEM((GROUPS, CHIPS, 8, LANES), F32)
    results = pl.pallas_call(
        block_kernel,
        out_shape=out_shape,
        in_specs=[anywhere] * 6,
        out_specs=(anywhere,) * 4,
        scratch_shapes=[
            points, points,
            pltpu.VMEM((C, 3 * C), F32),
            pltpu.VMEM((C, C), F32),
            points, index, index,
            pltpu.VMEM((C, 3 * C), BF16),
            pltpu.VMEM((C, C), BF16),
            points, points, points, points,
            pltpu.VMEM((3 * C, C), BF16),
            pltpu.VMEM((PATCH, C), F32),
            pltpu.VMEM((PATCH, 1), F32),
            halves, halves, heads_t, heads_t, heads_t, heads_t,
            queries, queries,
            pltpu.VMEM((2, CHUNKS, CHUNK // 8, 8, QB), F32),
            heads_t, heads_t, heads_f, heads_f,
            pieces, pieces, pieces, pieces, pieces, pieces,
            both_cores, one_core, one_core, one_core,
            pltpu.VMEM((GROUPS, 8, LANES), F32),
            both_cores,
            pltpu.VMEM((SIDE, 8, LANES), F32),
            pltpu.VMEM((SIDE, 8, LANES), F32),
            pltpu.SemaphoreType.DMA((6,)),
            pltpu.SemaphoreType.DMA((4, PARTS)),
            pltpu.SemaphoreType.DMA((4, PARTS)),
            pltpu.SemaphoreType.DMA((GROUPS, 8)),
            pltpu.SemaphoreType.DMA((2, 4)),
            pltpu.SemaphoreType.DMA((4,)),
        ],
        compiler_params=pltpu.CompilerParams(
            collective_id=0, has_side_effects=True, vmem_limit_bytes=60 * 1024 * 1024
        ),
        cost_estimate=pl.CostEstimate(
            flops=28_000_000_000, bytes_accessed=5_000_000, transcendentals=16_777_216
        ),
    )(
        features,
        zorder_to.reshape(1, PATCH),
        hilbert_from.reshape(1, PATCH),
        qkv_weight,
        proj_weight,
        out_grad,
    )
    return pl.pallas_call(
        finish_kernel,
        out_shape=out_shape,
        in_specs=[anywhere] * 4,
        out_specs=(anywhere,) * 4,
        scratch_shapes=[
            points, points,
            pltpu.VMEM((C, 3 * C), F32),
            pltpu.VMEM((C, C), F32),
            pltpu.SemaphoreType.DMA((2, 4)),
        ],
        compiler_params=pltpu.CompilerParams(vmem_limit_bytes=60 * 1024 * 1024),
        cost_estimate=pl.CostEstimate(flops=0, bytes_accessed=4_000_000, transcendentals=0),
    )(*results)


def solution(mesh):
    in_specs = (
        P(("row", "col"), None),
        P(("row", "col")),
        P(("row", "col")),
        P(),
        P(),
        P(("row", "col"), None),
    )
    out_specs = (P(("row", "col"), None), P(("row", "col"), None), P(), P())
    return jax.shard_map(
        on_device, mesh=mesh, in_specs=in_specs, out_specs=out_specs, check_vma=False
    )
```

```python
import functools

import jax
import jax.numpy as jnp
from jax import lax
from jax.experimental import pallas as pl
from jax.experimental.pallas import tpu as pltpu
from jax.sharding import PartitionSpec as P

HEADS = 16
HEAD_DIM = 16
PATCH = 1024
C = 256
QB = 512
CHUNK = 64
TALL = 128
STRIP = 256
EXP_SCALE = 0.25 * 1.4426950408889634

F32 = jnp.float32
BF16 = jnp.bfloat16


def dot(a, b):
    return jnp.dot(a, b, preferred_element_type=F32)


def dot_nt(a, b):
    return lax.dot_general(a, b, (((1,), (1,)), ((), ())), preferred_element_type=F32)


def normalize(x):
    centered = x - jnp.mean(x, axis=1, keepdims=True)
    rstd = lax.rsqrt(jnp.mean(centered * centered, axis=1, keepdims=True) + 1e-05)
    return centered * rstd, rstd


def transposed(a):
    return a.astype(F32).T.astype(BF16)


MESH = pl.DeviceIdType.MESH
N_ROW = 8
N_COL = 16
DEVICES = N_ROW * N_COL
CHIPS = DEVICES // 2
CAP = PATCH // DEVICES
LANES = 128


STRIDE = 1
INVERSE_STRIDE = 1
PARTS = 4
PART_CHIPS = CHIPS // PARTS
PART_ROWS = PATCH // PARTS


def as_column(row):
    return jnp.broadcast_to(row, (LANES, PATCH)).T


def slots(key_row):
    key_col = as_column(key_row)
    ranks = []
    for block in range(PATCH // LANES):
        keys = key_row[:, block * LANES : (block + 1) * LANES]
        below = jnp.where(key_col < keys, 1.0, 0.0)
        ranks.append(jnp.sum(below, axis=0, keepdims=True))
    return jnp.concatenate(ranks, axis=1)


def scatter_rows(slot_row, part):
    row = lax.broadcasted_iota(jnp.int32, (PART_ROWS, PATCH), 0) + part * PART_ROWS
    return jnp.where(slot_row == row.astype(F32), 1.0, 0.0).astype(BF16)


def gather_columns(slot_col, part):
    lane = lax.broadcasted_iota(jnp.int32, (PATCH, LANES), 1) + part * PART_ROWS
    blocks = [
        jnp.where(slot_col == (lane + low).astype(F32), 1.0, 0.0).astype(BF16)
        for low in range(0, PART_ROWS, LANES)
    ]
    return jnp.concatenate(blocks, axis=1)


def chip_and_core(point):
    device = point // PATCH
    row, col = device // N_COL, device % N_COL
    return (row // 2) * N_COL + col, row % 2


def relative_slot(offset, core):
    return ((offset + CHIPS) * INVERSE_STRIDE % CHIPS) * 2 + core


def send_slots(zorder_ref):
    point = zorder_ref[...]
    chip, core = chip_and_core(point)
    slot = relative_slot(chip - position()[1], core)
    return slots((slot * PATCH + point % PATCH).astype(F32))


def recv_slots(hilbert_ref):
    chip, core = chip_and_core(hilbert_ref[...])
    slot = relative_slot(position()[1] - chip, core)
    local = lax.broadcasted_iota(jnp.int32, (1, PATCH), 1)
    return slots((slot * PATCH + local).astype(F32))


def packed(rows):
    rows = rows.reshape(2 * PART_CHIPS, CAP, C)
    pieces = jnp.concatenate([rows[:, :, :LANES], rows[:, :, LANES:]], axis=1).astype(BF16)
    return pieces.reshape(PART_CHIPS, 2, 2 * CAP, LANES)


def unpacked(pieces):
    pieces = pieces.reshape(2 * PART_CHIPS, 2 * CAP, LANES).astype(F32)
    left = pieces[:, :CAP].reshape(PART_ROWS, LANES)
    right = pieces[:, CAP:].reshape(PART_ROWS, LANES)
    return jnp.concatenate([left, right], axis=1).astype(BF16)


def part_chips(part):
    return slice(part * PART_CHIPS, (part + 1) * PART_CHIPS)


def position():
    row, col = lax.axis_index("row"), lax.axis_index("col")
    core = lax.rem(row, 2)
    return core, (row // 2) * N_COL + col, (row + 1 - 2 * core, col)


def chip_device(chip):
    core, _, _ = position()
    return (chip // N_COL) * 2 + core, lax.rem(chip, N_COL)


def for_chips(act):
    _, chip, _ = position()

    def body(step, _):
        other = lax.rem(chip + step * STRIDE, CHIPS)
        act(other, chip_device(other))
        return 0

    lax.fori_loop(1, CHIPS, body, 0)


def greet(barrier):
    _, _, sibling = position()
    pl.semaphore_signal(barrier, inc=1, device_id=sibling, device_id_type=MESH)
    for_chips(
        lambda _, device: pl.semaphore_signal(
            barrier, inc=1, device_id=device, device_id_type=MESH
        )
    )


def pair_copy(out_ref, both_ref, part, sems):
    core, _, sibling = position()
    return pltpu.make_async_remote_copy(
        src_ref=out_ref.at[part_chips(part), 1 - core],
        dst_ref=both_ref.at[part_chips(part), core],
        send_sem=sems.at[0, part],
        recv_sem=sems.at[1, part],
        device_id=sibling,
        device_id_type=MESH,
    )


def start_part(rows, out_ref, both_ref, part, sems):
    core, _, _ = position()
    out_ref[part_chips(part)] = packed(rows)
    pair_copy(out_ref, both_ref, part, sems).start()
    both_ref[part_chips(part), core] = out_ref[part_chips(part), core]


def send_part(out_ref, both_ref, in_ref, part, stride, sems):
    _, chip, _ = position()
    pair_copy(out_ref, both_ref, part, sems).wait()

    def body(step, _):
        pltpu.make_async_remote_copy(
            src_ref=both_ref.at[step],
            dst_ref=in_ref.at[step],
            send_sem=sems.at[2, part],
            recv_sem=sems.at[3, part],
            device_id=chip_device(lax.rem(chip + step * stride, CHIPS)),
            device_id_type=MESH,
        ).start()
        return 0

    lax.fori_loop(max(part * PART_CHIPS, 1), (part + 1) * PART_CHIPS, body, 0)
    if part == 0:
        in_ref[0] = both_ref[0]


def wait_part(in_ref, part, sem):
    wait_bytes(in_ref, PART_CHIPS - (part == 0), sem)


def wait_bytes(ref, count, sem):
    view = ref.at[pl.ds(0, count)]
    pltpu.make_async_copy(view, view, sem).wait()


SIDE = 8
GROUPS = 3
FIRST_HEAD = (0, 8, 13, HEADS)
OWNER_STRIDE = 13
OWNER_INVERSE = 5


def group_heads(g):
    return FIRST_HEAD[g + 1] - FIRST_HEAD[g]


def group_tiles(g):
    return 8 * group_heads(g)


def tiles(section):
    rows = section.shape[0]
    section = section.reshape(rows // 8, 8, C)
    halves = [section[:, None, :, :LANES], section[:, None, :, LANES:]]
    return jnp.concatenate(halves, axis=1).reshape(rows // 4, 8, LANES)


def untiled(pieces):
    pieces = pieces.reshape(-1, 2, 8, LANES)
    return jnp.concatenate([pieces[:, 0], pieces[:, 1]], axis=2).reshape(-1, C)


def block_kernel(
    feat_hbm, zorder_hbm, hilbert_hbm, wqkv_hbm, wp_hbm, og_hbm,
    out_hbm, feat_grad_hbm, qkvg_hbm, projg_hbm,
    out_ref, feat_grad_ref, qkvg_ref, projg_ref,
    feat_ref, zorder_ref, hilbert_ref, wqkv_ref, wp_ref, og_ref, oga_ref, x_ref, normed_ref,
    wqkv_t_ref, xhat_ref, rstd_ref, k_ref, v_ref, qt_ref, kt_ref, vt_ref, dot_ref,
    p_ref, ds_ref, e_ref, at_ref, dqt_ref, dkt_ref, dvt_ref,
    there_out, there_both, there_in, back_out, back_both, back_in,
    part_ref, half_ref, sum_ref, chunk_in_ref, result_ref, total_ref, low_out_ref, low_in_ref,
    load_sems, there_sems, back_sems, group_sems, level_sems, store_sems,
):
    half_width = C // 2
    core, chip, sibling = position()
    barrier = pltpu.get_barrier_semaphore()
    sources = (zorder_hbm, feat_hbm, hilbert_hbm, og_hbm, wp_hbm, wqkv_hbm)
    targets = (zorder_ref, feat_ref, hilbert_ref, og_ref, wp_ref, wqkv_ref)
    loads = [
        pltpu.make_async_copy(source, target, load_sems.at[i])
        for i, (source, target) in enumerate(zip(sources, targets))
    ]
    stores = [
        pltpu.make_async_copy(source, target, store_sems.at[i])
        for i, (source, target) in enumerate((
            (out_ref, out_hbm),
            (feat_grad_ref, feat_grad_hbm),
            (qkvg_ref, qkvg_hbm),
            (projg_ref, projg_hbm),
        ))
    ]
    for load in loads:
        load.start()
    greet(barrier)
    loads[0].wait()
    there_slots = send_slots(zorder_ref)
    loads[1].wait()
    for part in range(PARTS):
        rows = dot(scatter_rows(there_slots, part), feat_ref[...])
        if part == 0:
            pl.semaphore_wait(barrier, CHIPS)
        start_part(rows, there_out, there_both, part, there_sems)
        if part:
            send_part(there_out, there_both, there_in, part - 1, STRIDE, there_sems)
    send_part(there_out, there_both, there_in, PARTS - 1, STRIDE, there_sems)

    for load in loads[2:]:
        load.wait()
    back_slots = recv_slots(hilbert_ref)
    for part in range(PARTS):
        rows = slice(part * PART_ROWS, (part + 1) * PART_ROWS)
        oga_ref[rows] = dot(scatter_rows(back_slots, part), og_ref[...]).astype(BF16)
    do_t = dot_nt(wp_ref[...], oga_ref[...]).astype(BF16).astype(F32)
    dot_ref[...] = (do_t * 0.25).astype(BF16).reshape(HEADS, HEAD_DIM, PATCH)
    wqkv_t_ref[...] = transposed(wqkv_ref[...])
    p_ref[1] = jnp.zeros((PATCH, QB), BF16)
    ds_ref[1] = jnp.zeros((PATCH, QB), BF16)
    dkt_ref[0] = jnp.zeros((HEAD_DIM, PATCH), F32)
    dvt_ref[0] = jnp.zeros((HEAD_DIM, PATCH), F32)

    for part in range(PARTS):
        wait_part(there_in, part, there_sems.at[3, part])
        rows = slice(part * PART_ROWS, (part + 1) * PART_ROWS)
        x = unpacked(there_in[part_chips(part)])
        x_ref[rows] = x
        xhat, rstd = normalize(x.astype(F32))
        xhat_ref[rows] = xhat
        rstd_ref[rows] = rstd
        normed = xhat.astype(BF16)
        normed_ref[rows] = normed
        kv = dot(normed, wqkv_ref[:, C:]).astype(BF16)
        for ref, low in ((k_ref, 0), (v_ref, C)):
            ref[0, rows] = kv[:, low : low + half_width]
            ref[1, rows] = kv[:, low + half_width : low + C]
        qkv_t = dot(wqkv_t_ref[...], transposed(normed)).astype(BF16)
        for ref, low in ((qt_ref, 0), (kt_ref, C), (vt_ref, 2 * C)):
            ref[:, :, rows] = qkv_t[low : low + C].reshape(HEADS, HEAD_DIM, PART_ROWS)

    def group_part(g):
        heads = slice(FIRST_HEAD[g], FIRST_HEAD[g + 1])
        count = group_heads(g) * HEAD_DIM

        def rows(ref):
            return ref[heads].reshape(count, PATCH).astype(BF16)

        cot = jnp.concatenate([rows(ref) for ref in (dqt_ref, dkt_ref, dvt_ref)], axis=0)
        sums = dot(cot, normed_ref[...])
        sums = [sums[i * count : (i + 1) * count] for i in range(3)]
        half = group_tiles(g) // 2
        for section, value in enumerate(sums + [dot(rows(at_ref), oga_ref[...])]):
            low = section % 2 * half
            part_ref[g, section // 2, low : low + half] = tiles(value)
        group_half(g).start()

    def group_half(g):
        count = pl.ds(0, group_tiles(g))
        return pltpu.make_async_remote_copy(
            src_ref=part_ref.at[g, 1 - core, count],
            dst_ref=half_ref.at[g, count],
            send_sem=group_sems.at[g, 0],
            recv_sem=group_sems.at[g, 1],
            device_id=sibling,
            device_id_type=MESH,
        )

    my_tile = lax.rem(chip * OWNER_INVERSE, CHIPS)

    def by_owner(g, act):
        pl.when(my_tile < group_tiles(g))(lambda: act(True))
        pl.when(my_tile >= group_tiles(g))(lambda: act(False))

    def group_scatter(g):
        group_half(g).wait()
        count = group_tiles(g)
        sum_ref[g, :count] = part_ref[g, core, :count] + half_ref[g, :count]

        def body(tile, _):
            owner = lax.rem(tile * OWNER_STRIDE, CHIPS)

            @pl.when(owner != chip)
            def _():
                pltpu.make_async_remote_copy(
                    src_ref=sum_ref.at[g, tile],
                    dst_ref=chunk_in_ref.at[g, chip],
                    send_sem=group_sems.at[g, 2],
                    recv_sem=group_sems.at[g, 3],
                    device_id=chip_device(owner),
                    device_id_type=MESH,
                ).start()

            return 0

        lax.fori_loop(0, count, body, 0)

        @pl.when(my_tile < count)
        def _():
            chunk_in_ref[g, chip] = sum_ref[g, my_tile]

    def group_gather(g):
        @pl.when(my_tile < group_tiles(g))
        def _():
            wait_bytes(chunk_in_ref.at[g], CHIPS - 1, group_sems.at[g, 3])
            result_ref[g] = jnp.sum(chunk_in_ref[g], axis=0)
            for_chips(
                lambda other, device: pltpu.make_async_remote_copy(
                    src_ref=result_ref.at[g],
                    dst_ref=total_ref.at[g, core, my_tile],
                    send_sem=group_sems.at[g, 4],
                    recv_sem=group_sems.at[g, 5],
                    device_id=device,
                    device_id_type=MESH,
                ).start()
            )
            total_ref[g, core, my_tile] = result_ref[g]

    def group_final(g):
        count = pl.ds(0, group_tiles(g))
        return pltpu.make_async_remote_copy(
            src_ref=total_ref.at[g, core, count],
            dst_ref=total_ref.at[g, core, count],
            send_sem=group_sems.at[g, 6],
            recv_sem=group_sems.at[g, 7],
            device_id=sibling,
            device_id_type=MESH,
        )

    def group_finish(g):
        def arrived(owner):
            wait_bytes(total_ref.at[g, core], group_tiles(g) - owner, group_sems.at[g, 5])

        by_owner(g, arrived)
        group_final(g).start()

    high, low = chip // SIDE, lax.rem(chip, SIDE)

    def level_copy(src, dst, to, sem):
        return pltpu.make_async_remote_copy(
            src_ref=src,
            dst_ref=dst,
            send_sem=level_sems.at[0, sem],
            recv_sem=level_sems.at[1, sem],
            device_id=chip_device(to),
            device_id_type=MESH,
        )

    def others(mine, act):
        def body(step, _):
            act(lax.rem(mine + step, SIDE))
            return 0

        lax.fori_loop(1, SIDE, body, 0)

    def level_wait(direction, sem, rows):
        view = sum_ref.at[0, pl.ds(0, (SIDE - 1) * rows)]
        pltpu.make_async_copy(view, view, level_sems.at[direction, sem]).wait()

    def run(index):
        return pl.ds(index * SIDE, SIDE)

    def scatter_high():
        group_half(0).wait()
        sum_ref[0] = part_ref[0, core] + half_ref[0]
        others(high, lambda to: level_copy(
            sum_ref.at[0, run(to)], chunk_in_ref.at[0, run(high)], to * SIDE + low, 0
        ).start())
        chunk_in_ref[0, run(high)] = sum_ref[0, run(high)]

    def scatter_low():
        level_wait(1, 0, SIDE)
        summed = chunk_in_ref[0].reshape(SIDE, SIDE, 8, LANES)
        low_out_ref[...] = jnp.sum(summed, axis=0)
        others(low, lambda to: level_copy(
            low_out_ref.at[to], low_in_ref.at[low], high * SIDE + to, 1
        ).start())
        low_in_ref[low] = low_out_ref[low]

    def gather_low():
        level_wait(1, 1, 1)
        result_ref[0] = jnp.sum(low_in_ref[...], axis=0)
        others(low, lambda to: level_copy(
            result_ref.at[0], total_ref.at[0, core, chip], high * SIDE + to, 2
        ).start())
        total_ref[0, core, chip] = result_ref[0]

    def gather_high():
        level_wait(1, 2, 1)
        others(high, lambda to: level_copy(
            total_ref.at[0, core, run(high)], total_ref.at[0, core, run(high)], to * SIDE + low, 3
        ).start())

    def gather_done():
        level_wait(1, 3, SIDE)
        group_final(0).start()

    def group_close(g):
        group_final(g).wait()
        if g == 0:
            for sem, rows in enumerate((SIDE, 1, 1, SIDE)):
                level_wait(0, sem, rows)
            return

        def sent(owner):
            wait_bytes(sum_ref.at[g], group_tiles(g) - owner, group_sems.at[g, 2])
            if owner:
                wait_bytes(sum_ref.at[g], CHIPS - 1, group_sems.at[g, 4])

        by_owner(g, sent)

    def assemble(section):
        rows = []
        for g in range(GROUPS):
            half = group_tiles(g) // 2
            low = section % 2 * half
            rows.append(untiled(total_ref[g, section // 2, low : low + half]))
        return jnp.concatenate(rows, axis=0)

    def query_side(h, block):
        ql = slice(block * QB, (block + 1) * QB)
        dqt_ref[h, :, ql] = dot(kt_ref[h], ds_ref[block]).astype(BF16)

    def value_side(h, block):
        ql = slice(block * QB, (block + 1) * QB)
        dv = dot_nt(dot_ref[h, :, ql], p_ref[block]) * 4.0
        dvt_ref[h] = dvt_ref[h] + dv if block else dv

    def key_side(h, block):
        ql = slice(block * QB, (block + 1) * QB)
        dk = dot_nt(qt_ref[h, :, ql], ds_ref[block])
        dkt_ref[h] = dkt_ref[h] + dk if block else dk

    def block_step(h, block, km, vm, before):
        half = h // 8
        ql = slice(block * QB, (block + 1) * QB)
        qt = qt_ref[pl.ds(half * 8, 8), :, ql].reshape(half_width, QB)
        dot_t = dot_ref[pl.ds(half * 8, 8), :, ql].reshape(half_width, QB)
        tops, sums = ([], []), ([], [])
        for j in range(PATCH // STRIP):
            s = dot(km[j * STRIP : (j + 1) * STRIP], qt)
            if j == 0:
                query_side(before, 1 - block)
            for c in range(STRIP // TALL):
                for g in range(2):
                    lanes = slice(g * QB // 2, (g + 1) * QB // 2)
                    part = s[c * TALL : (c + 1) * TALL, lanes].reshape(TALL // 8, 8, QB // 2)
                    top = jnp.max(part, axis=0)
                    e = jnp.exp2((part - top) * EXP_SCALE)
                    e_ref[block, j * (STRIP // TALL) + c, :, :, lanes] = e
                    tops[g].append(top)
                    sums[g].append(jnp.sum(e, axis=0))
        value_side(before, 1 - block)
        weights = []
        for g in range(2):
            peak = functools.reduce(jnp.maximum, tops[g])
            peak = jnp.max(peak, axis=0, keepdims=True)
            scales = [jnp.exp2((top - peak) * EXP_SCALE) for top in tops[g]]
            total = functools.reduce(jnp.add, [a * w for a, w in zip(sums[g], scales)])
            inverse = 1.0 / jnp.sum(total, axis=0, keepdims=True)
            weights.append([scale * inverse for scale in scales])
        for c in range(PATCH // TALL):
            for g in range(2):
                lanes = slice(g * QB // 2, (g + 1) * QB // 2)
                p = e_ref[block, c, :, :, lanes] * weights[g][c]
                rows = slice(c * TALL, (c + 1) * TALL)
                p_ref[block, rows, lanes] = p.reshape(TALL, QB // 2).astype(BF16)
        ot = dot(vt_ref[h], p_ref[block])
        key_side(before, 1 - block)
        at_ref[h, :, ql] = ot.astype(BF16)
        delta = jnp.sum(ot * dot_ref[h, :, ql].astype(F32), axis=0, keepdims=True)
        for j in range(PATCH // STRIP):
            dp = dot(vm[j * STRIP : (j + 1) * STRIP], dot_t)
            for c in range(STRIP // CHUNK):
                rows = slice(j * STRIP + c * CHUNK, j * STRIP + (c + 1) * CHUNK)
                p = p_ref[block, rows].astype(F32)
                ds = p * (dp[c * CHUNK : (c + 1) * CHUNK] - delta)
                ds_ref[block, rows] = ds.astype(BF16)

    def after_scatter():
        gather_done()
        group_scatter(1)

    def head_step(h, _):
        half = h // 8
        lane = lax.broadcasted_iota(jnp.int32, (1, half_width), 1) // HEAD_DIM
        mask = (lane == h % 8).astype(F32).astype(BF16)
        km = k_ref[half] * mask
        vm = v_ref[half] * mask
        block_step(h, 0, km, vm, jnp.maximum(h - 1, 0))
        block_step(h, 1, km, vm, h)

        steps = {
            FIRST_HEAD[1]: lambda: group_part(0),
            FIRST_HEAD[1] + 1: scatter_high,
            FIRST_HEAD[1] + 2: scatter_low,
            FIRST_HEAD[1] + 3: gather_low,
            FIRST_HEAD[1] + 4: gather_high,
            FIRST_HEAD[2]: lambda: group_part(1),
            FIRST_HEAD[2] + 1: after_scatter,
            FIRST_HEAD[2] + 2: lambda: group_gather(1),
        }
        for head, act in steps.items():
            pl.when(h == head)(act)

        return 0

    lax.fori_loop(0, HEADS, head_step, 0)
    query_side(HEADS - 1, 1)
    value_side(HEADS - 1, 1)
    key_side(HEADS - 1, 1)

    group_part(2)
    cot_t = [ref[...].reshape(C, PATCH).astype(BF16) for ref in (dqt_ref, dkt_ref, dvt_ref)]
    ng_t = dot(wqkv_ref[...], jnp.concatenate(cot_t, axis=0))
    for part in range(PARTS):
        rows = slice(part * PART_ROWS, (part + 1) * PART_ROWS)
        ng = ng_t[:, rows].T
        xhat = xhat_ref[rows]
        ng_mean = jnp.mean(ng, axis=1, keepdims=True)
        mixed = jnp.mean(ng * xhat, axis=1, keepdims=True)
        grad = oga_ref[rows].astype(F32) + rstd_ref[rows] * (ng - ng_mean - xhat * mixed)
        start_part(grad, back_out, back_both, part, back_sems)
        if part == 1:
            group_scatter(2)
        if part:
            send_part(back_out, back_both, back_in, part - 1, CHIPS - STRIDE, back_sems)
    send_part(back_out, back_both, back_in, PARTS - 1, CHIPS - STRIDE, back_sems)
    group_gather(2)

    at = at_ref[...].reshape(C, PATCH)
    block_out = x_ref[...].astype(F32) + dot(transposed(at), wp_ref[...])
    block_out = block_out.astype(BF16)
    group_finish(1)
    slot_col = as_column(recv_slots(hilbert_ref))
    gather = [gather_columns(slot_col, part) for part in range(PARTS)]
    out_ref[...] = dot(jnp.concatenate(gather, axis=1), block_out).astype(BF16)
    stores[0].start()
    group_close(0)
    group_close(1)
    slot_col = as_column(send_slots(zorder_ref))
    gather = [gather_columns(slot_col, part) for part in range(PARTS)]
    group_finish(2)
    total = jnp.zeros((PATCH, C), F32)
    for part in range(PARTS):
        wait_part(back_in, part, back_sems.at[3, part])
        total += dot(gather[part], unpacked(back_in[part_chips(part)]))
    feat_grad_ref[...] = total.astype(BF16)
    stores[1].start()
    group_close(2)
    for section in range(3):
        qkvg_ref[:, section * C : (section + 1) * C] = assemble(section).T
    projg_ref[...] = assemble(3)
    stores[2].start()
    stores[3].start()
    for part in range(PARTS):
        wait_part(there_in, part, there_sems.at[2, part])
        wait_part(back_in, part, back_sems.at[2, part])
    for store in stores:
        store.wait()


def finish_kernel(*refs):
    sources, targets, rooms, sems = refs[:4], refs[4:8], refs[8:12], refs[12]
    ins = [
        pltpu.make_async_copy(source, room, sems.at[0, i])
        for i, (source, room) in enumerate(zip(sources, rooms))
    ]
    outs = [
        pltpu.make_async_copy(room, target, sems.at[1, i])
        for i, (room, target) in enumerate(zip(rooms, targets))
    ]
    for copy in ins:
        copy.start()
    for copy_in, copy_out in zip(ins, outs):
        copy_in.wait()
        copy_out.start()
    for copy in outs:
        copy.wait()


def on_device(features, zorder_to, hilbert_from, qkv_weight, proj_weight, out_grad):
    anywhere = pl.BlockSpec(memory_space=pl.ANY)
    out_shape = (
        jax.ShapeDtypeStruct((PATCH, C), BF16),
        jax.ShapeDtypeStruct((PATCH, C), BF16),
        jax.ShapeDtypeStruct((C, 3 * C), F32),
        jax.ShapeDtypeStruct((C, C), F32),
    )
    points = pltpu.VMEM((PATCH, C), BF16)
    index = pltpu.VMEM((1, PATCH), jnp.int32)
    halves = pltpu.VMEM((2, PATCH, C // 2), BF16)
    heads_t = pltpu.VMEM((HEADS, HEAD_DIM, PATCH), BF16)
    heads_f = pltpu.VMEM((HEADS, HEAD_DIM, PATCH), F32)
    queries = pltpu.VMEM((2, PATCH, QB), BF16)
    pieces = pltpu.VMEM((CHIPS, 2, 2 * CAP, LANES), BF16)
    both_cores = pltpu.VMEM((GROUPS, 2, CHIPS, 8, LANES), F32)
    one_core = pltpu.VMEM((GROUPS, CHIPS, 8, LANES), F32)
    results = pl.pallas_call(
        block_kernel,
        out_shape=out_shape,
        in_specs=[anywhere] * 6,
        out_specs=(anywhere,) * 4,
        scratch_shapes=[
            points, points,
            pltpu.VMEM((C, 3 * C), F32),
            pltpu.VMEM((C, C), F32),
            points, index, index,
            pltpu.VMEM((C, 3 * C), BF16),
            pltpu.VMEM((C, C), BF16),
            points, points, points, points,
            pltpu.VMEM((3 * C, C), BF16),
            pltpu.VMEM((PATCH, C), F32),
            pltpu.VMEM((PATCH, 1), F32),
            halves, halves, heads_t, heads_t, heads_t, heads_t,
            queries, queries,
            pltpu.VMEM((2, PATCH // TALL, TALL // 8, 8, QB), F32),
            heads_t, heads_t, heads_f, heads_f,
            pieces, pieces, pieces, pieces, pieces, pieces,
            both_cores, one_core, one_core, one_core,
            pltpu.VMEM((GROUPS, 8, LANES), F32),
            both_cores,
            pltpu.VMEM((SIDE, 8, LANES), F32),
            pltpu.VMEM((SIDE, 8, LANES), F32),
            pltpu.SemaphoreType.DMA((6,)),
            pltpu.SemaphoreType.DMA((4, PARTS)),
            pltpu.SemaphoreType.DMA((4, PARTS)),
            pltpu.SemaphoreType.DMA((GROUPS, 8)),
            pltpu.SemaphoreType.DMA((2, 4)),
            pltpu.SemaphoreType.DMA((4,)),
        ],
        compiler_params=pltpu.CompilerParams(
            collective_id=0, has_side_effects=True, vmem_limit_bytes=60 * 1024 * 1024
        ),
        cost_estimate=pl.CostEstimate(
            flops=28_000_000_000, bytes_accessed=5_000_000, transcendentals=16_777_216
        ),
    )(
        features,
        zorder_to.reshape(1, PATCH),
        hilbert_from.reshape(1, PATCH),
        qkv_weight,
        proj_weight,
        out_grad,
    )
    return pl.pallas_call(
        finish_kernel,
        out_shape=out_shape,
        in_specs=[anywhere] * 4,
        out_specs=(anywhere,) * 4,
        scratch_shapes=[
            points, points,
            pltpu.VMEM((C, 3 * C), F32),
            pltpu.VMEM((C, C), F32),
            pltpu.SemaphoreType.DMA((2, 4)),
        ],
        compiler_params=pltpu.CompilerParams(vmem_limit_bytes=60 * 1024 * 1024),
        cost_estimate=pl.CostEstimate(flops=0, bytes_accessed=4_000_000, transcendentals=0),
    )(*results)


def solution(mesh):
    in_specs = (
        P(("row", "col"), None),
        P(("row", "col")),
        P(("row", "col")),
        P(),
        P(),
        P(("row", "col"), None),
    )
    out_specs = (P(("row", "col"), None), P(("row", "col"), None), P(), P())
    return jax.shard_map(
        on_device, mesh=mesh, in_specs=in_specs, out_specs=out_specs, check_vma=False
    )
```
